512 devices in a mesh: tm: 16 (over x, y), chan: 32 (over z, core).
Axes of the slice: x: 4, y: 4, z: 16, core: 2. Of those that a mesh axis runs over, the one named last changes fastest.
Arguments:
- spectra: bfloat16 [2, 128, 256, 6144], P(None, 'chan', None, 'tm'), may hold values from -6 to 6
- delays: int32 [128], replicated, may hold values from -4096 to 4095
- flags: int32 [128, 128], replicated, may hold values 0 or 1
- taps: float32 [12, 128], replicated, may hold values from -4 to 4
Outputs:
- voltages: bfloat16 [2, 256, 6144, 128], P(None, 'chan', 'tm')
The draws below stay inside these ranges and needn't reach their ends.
All inputs are finite; a program needn't handle non-finite values.
Results may differ from the reference program's by a relative error of at most 0.001.
Values may be sent and summed in bfloat16 or wider, within the bound.
A program may use at most 64 MiB of HBM per device.

```python
import math
import jax
import jax.numpy as jnp
from jax import lax

K = 128
TILES = 128
TAPS = 12
SIGNALS = 256
FRAMES = 6144


def touch_ends(array, key, least, top_value):
    longest = array.shape.index(max(array.shape))
    spots = []
    for shift in (0, 1):
        where = [jax.random.randint(jax.random.fold_in(key, axis), (), 0, length) for axis, length in enumerate(array.shape)]
        where[longest] = (where[longest] + shift) % array.shape[longest]
        spots.append(tuple(where))
    return array.at[spots[0]].set(least).at[spots[1]].set(top_value)


def steps_of(key, dims, cuts, low, top_value):
    factor_of, own = 1.0, jax.random.fold_in(key, 6)
    for dim, shards_of in cuts:
        steps = jnp.exp(jax.random.uniform(jax.random.fold_in(own, dim), (shards_of,), jnp.float32, low / len(cuts), top_value / len(cuts)))
        factor_of = factor_of * jnp.repeat(steps, dims[dim] // shards_of).reshape([-1 if axis == dim else 1 for axis in range(len(dims))])
    return factor_of


def bell_draw(rng, shape, deviation, bound, shards=(), kind=jnp.bfloat16):
    factor_of = steps_of(rng, shape, shards, -0.22, 0.18) if shards else 1.0
    entries = jax.random.normal(rng, shape, jnp.float32) * deviation * factor_of
    return jnp.minimum(jnp.maximum(entries, -bound), bound).astype(kind)


def setup_inputs(seed: int = 0) -> dict:
    streams_of = jax.random.split(jax.random.key(seed), 5)
    return {
        "spectra": bell_draw(streams_of[0], (2, K, SIGNALS, FRAMES), 1.0, 6.0, ((1, 32), (3, 16))),
        "delays": touch_ends(jax.random.randint(streams_of[1], (TILES,), -4096, 4096), jax.random.fold_in(streams_of[1], 1), -4096, 4095).astype(jnp.int32),
        "flags": touch_ends((jax.random.randint(streams_of[2], (K, TILES), 0, 8) < 7).astype(jnp.int32), jax.random.fold_in(streams_of[2], 1), 0, 1),
        "taps": bell_draw(streams_of[3], (TAPS, K), 0.29, 4.0, (), jnp.float32),
    }


def one_tile(spectra, delays, flags, taps, tile_id):
    block = lax.dynamic_slice_in_dim(spectra, tile_id * 2, 2, 2).astype(jnp.float32)
    delay_one = lax.dynamic_slice_in_dim(delays, tile_id, 1, 0)
    flag_one = lax.dynamic_slice_in_dim(flags, tile_id, 1, 1).astype(jnp.float32)
    chan_ids = jnp.arange(K, dtype=jnp.int32)
    turns = chan_ids[:, None] * delay_one[None, :] % K
    phase = 2.0 * math.pi / K * turns.astype(jnp.float32)
    cosine = (jnp.cos(phase) * flag_one)[:, :, None]
    sine = (jnp.sin(phase) * flag_one)[:, :, None]
    real_part = cosine * block[0] + sine * block[1]
    imag_part = cosine * block[1] - sine * block[0]
    spectrum = real_part + 1j * imag_part
    series = jnp.fft.ifft(spectrum, axis=0) * math.sqrt(K)
    series = jnp.transpose(series, (1, 2, 0))
    stacked = jnp.stack([jnp.real(series), jnp.imag(series)]).astype(jnp.float32)
    padded = jnp.pad(stacked, ((0, 0), (0, 0), (TAPS - 1, 0), (0, 0)))
    frames = stacked.shape[2]
    total = jnp.zeros_like(stacked)
    for tap_index in range(TAPS):
        start = TAPS - 1 - tap_index
        total = total + taps[tap_index][None, None, None, :] * padded[:, :, start:start + frames, :]
    return total.astype(jnp.bfloat16)

def reference(spectra, delays, flags, taps):
    blocks = lax.map(lambda tile_id: one_tile(spectra, delays, flags, taps, tile_id), jnp.arange(TILES, dtype=jnp.int32))
    blocks = jnp.transpose(blocks, (1, 0, 2, 3, 4))
    return blocks.reshape(2, SIGNALS, blocks.shape[3], K)
```

```python
import math

import jax
import jax.numpy as jnp
from jax import lax
from jax.experimental import pallas as pl
from jax.experimental.pallas import tpu as pltpu
from jax.sharding import PartitionSpec as P

TAPS = 12
LANES = 128
HALO = 16


def fill_tables(chan, delays_ref, flags_ref, hi_ref, lo_ref):
    tiles, rows, cols = hi_ref.shape
    nfine = rows // 2
    row = lax.broadcasted_iota(jnp.int32, (rows, cols), 0)
    col = lax.broadcasted_iota(jnp.int32, (rows, cols), 1)
    fine = (row >> 3) * 4 + (row & 3)
    sample = col & (nfine - 1)
    quarter = (((row >> 2) & 1) - (col >> 7)) * (nfine // 4)
    frow = lax.broadcasted_iota(jnp.int32, (rows, nfine), 0)
    fcol = lax.broadcasted_iota(jnp.int32, (rows, nfine), 1)
    spread = (fcol == (frow >> 3) * 4 + (frow & 3)).astype(jnp.float32).astype(jnp.bfloat16)
    kept = jnp.dot(
        spread,
        flags_ref[...].astype(jnp.float32).astype(jnp.bfloat16),
        preferred_element_type=jnp.float32,
    )

    def one_tile(t, carry):
        tile = chan * tiles + t
        delay = delays_ref[tile]
        turn = (fine * (sample - delay) + quarter) & (nfine - 1)
        fold = nfine // 4 - jnp.abs(turn - nfine // 2)
        x = fold.astype(jnp.float32) * (2.0 * math.pi / nfine)
        x2 = x * x
        poly = -1.0 / 39916800.0
        for c in (1.0 / 362880.0, -1.0 / 5040.0, 1.0 / 120.0, -1.0 / 6.0, 1.0):
            poly = poly * x2 + c
        lane = lax.broadcasted_iota(jnp.int32, kept.shape, 1)
        keep = jnp.sum(jnp.where(lane == tile, kept, 0.0), axis=1, keepdims=True)
        table = (poly * x) * (keep * (-1.0 / math.sqrt(nfine)))
        hi = table.astype(jnp.bfloat16)
        hi_ref[t] = hi
        lo_ref[t] = (table - hi.astype(jnp.float32)).astype(jnp.bfloat16)
        return carry

    lax.fori_loop(0, tiles, one_tile, 0)


def kernel(
    ntm,
    nchan,
    spectra_ref,
    delays_ref,
    flags_ref,
    taps_ref,
    out_ref,
    raw,
    mix,
    send,
    recv,
    y,
    hi,
    lo,
    result,
    raw_sem,
    send_sem,
    recv_sem,
    halo_sem,
    out_sem,
):
    tm = lax.axis_index("tm")
    chan = lax.axis_index("chan")
    nchunk, _, rows, _ = send.shape
    signals = rows // 8
    tiles = signals // 2

    def peer(j):
        step = j >> 1
        far = nchan // 4 - (step >> 1)
        away = jnp.where((step & 1) == 1, nchan // 2 - far, jnp.where(step == 0, 0, far))
        chip = lax.rem((chan >> 1) + away, nchan // 2)
        return chip * 2 + ((chan & 1) ^ (j & 1))

    load = pltpu.make_async_copy(spectra_ref, raw, raw_sem)
    load.start()

    barrier = pltpu.get_barrier_semaphore()

    def greet(j, carry):
        pl.semaphore_signal(barrier, inc=1, device_id={"chan": peer(j)})
        return carry

    lax.fori_loop(1, nchan, greet, 0)

    @pl.when(tm > 0)
    def _():
        pl.semaphore_signal(barrier, inc=1, device_id={"tm": tm - 1})

    load.wait()

    def arrange(pair, carry):
        part = raw[:, :, pl.ds(pl.multiple_of(pair * 16, 16), 16), :].astype(jnp.float32)
        for q in range(2):
            for c in range(2):
                for k in range(4):
                    for fc in range(nchunk):
                        mix[q, fc, pl.ds(c * 4 + k, signals, stride=8), :] = part[
                            c, k, q * 8 : q * 8 + 8, fc * LANES : (fc + 1) * LANES
                        ]
        for q in range(2):
            for fc in range(nchunk):
                send[fc, pair * 2 + q] = mix[q, fc].astype(jnp.bfloat16)
        return carry

    lax.fori_loop(0, nchan // 2, arrange, 0)

    pl.semaphore_wait(barrier, nchan - 1 + jnp.where(tm < ntm - 1, 1, 0))

    order = (nchunk - 1,) + tuple(range(nchunk - 1))
    for fc in order:

        def push(j, carry):
            to = peer(j)
            pltpu.make_async_remote_copy(
                src_ref=send.at[fc, to],
                dst_ref=recv.at[fc, chan],
                send_sem=send_sem.at[fc],
                recv_sem=recv_sem.at[fc],
                device_id={"chan": to},
            ).start()
            return carry

        lax.fori_loop(1, nchan, push, 0)
        pltpu.make_async_copy(send.at[fc, chan], recv.at[fc, chan], recv_sem.at[fc]).start()

    fill_tables(chan, delays_ref, flags_ref, hi, lo)

    @pl.when(tm == 0)
    def _():
        y[:, :, 0:HALO, :] = jnp.zeros((2, signals, HALO, LANES), jnp.float32)

    def transform(fc):
        base = HALO + fc * LANES

        def one_tile(t, carry):
            part = recv[fc, :, pl.ds(pl.multiple_of(t * 16, 16), 16), :].astype(jnp.float32)
            for p in range(2):
                x = part[:, p * 8 : p * 8 + 8, :].reshape(nchan * 8, LANES).astype(jnp.bfloat16)
                dims = (((0,), (0,)), ((), ()))
                z = lax.dot_general(x, hi[t], dims, preferred_element_type=jnp.float32)
                z += lax.dot_general(x, lo[t], dims, preferred_element_type=jnp.float32)
                y[0, t * 2 + p, base : base + LANES, :] = z[:, :LANES]
                y[1, t * 2 + p, base : base + LANES, :] = z[:, LANES:]
            return carry

        lax.fori_loop(0, tiles, one_tile, 0)

    def fir(first, last):
        def one(i, carry):
            d, s = i // signals, lax.rem(i, signals)
            for lo_row in range(first, last, 64):
                count = min(64, last - lo_row)
                total = None
                for j in range(TAPS):
                    start = HALO + lo_row - j
                    term = taps_ref[j : j + 1, :] * y[d, s, start : start + count, :]
                    total = term if total is None else total + term
                result[d, s, lo_row : lo_row + count, :] = total.astype(jnp.bfloat16)
            return carry

        lax.fori_loop(0, 2 * signals, one, 0)

    def arrived(fc):
        pltpu.make_async_copy(recv.at[fc], recv.at[fc], recv_sem.at[fc]).wait()

    stores = []

    def store(first, last):
        copy = pltpu.make_async_copy(
            result.at[:, :, first:last, :],
            out_ref.at[:, :, first:last, :],
            out_sem.at[len(stores)],
        )
        copy.start()
        stores.append(copy)

    frames = nchunk * LANES
    halo = pltpu.make_async_remote_copy(
        src_ref=y.at[:, :, frames : frames + HALO, :],
        dst_ref=y.at[:, :, 0:HALO, :],
        send_sem=halo_sem.at[0],
        recv_sem=halo_sem.at[1],
        device_id={"tm": lax.rem(tm + 1, ntm)},
    )

    arrived(nchunk - 1)
    transform(nchunk - 1)

    @pl.when(tm < ntm - 1)
    def _():
        halo.start()

    fir((nchunk - 1) * LANES + HALO, frames)
    store((nchunk - 1) * LANES + HALO, frames)

    for fc in range(nchunk - 1):
        arrived(fc)
        transform(fc)
        if fc == 0:

            @pl.when(tm > 0)
            def _():
                halo.wait_recv()

        last = (fc + 1) * LANES + (HALO if fc == nchunk - 2 else 0)
        fir(fc * LANES, last)
        store(fc * LANES, last)

    for fc in range(nchunk):
        sent = send.at[fc, 0 : nchan - 1]
        pltpu.make_async_copy(sent, sent, send_sem.at[fc]).wait()

    @pl.when(tm < ntm - 1)
    def _():
        halo.wait_send()

    for copy in stores:
        copy.wait()


def per_device(ntm, nchan, spectra, delays, flags, taps):
    parts, chans, sigs, frames = spectra.shape
    signals = sigs // nchan
    nfine = chans * nchan
    nchunk = frames // LANES
    rows = parts * chans * signals
    any_spec = pl.BlockSpec(memory_space=pl.ANY)
    vmem_spec = pl.BlockSpec(memory_space=pltpu.VMEM)
    smem_spec = pl.BlockSpec(memory_space=pltpu.SMEM)

    def body(*refs):
        kernel(ntm, nchan, *refs)

    return pl.pallas_call(
        body,
        out_shape=jax.ShapeDtypeStruct((2, signals, frames, nfine), jnp.bfloat16),
        in_specs=[any_spec, smem_spec, vmem_spec, vmem_spec],
        out_specs=any_spec,
        scratch_shapes=[
            pltpu.VMEM(spectra.shape, jnp.bfloat16),
            pltpu.VMEM((2, nchunk, rows, LANES), jnp.float32),
            pltpu.VMEM((nchunk, nchan, rows, LANES), jnp.bfloat16),
            pltpu.VMEM((nchunk, nchan, rows, LANES), jnp.bfloat16),
            pltpu.VMEM((2, signals, HALO + frames, nfine), jnp.float32),
            pltpu.VMEM((signals // 2, 2 * nfine, 2 * nfine), jnp.bfloat16),
            pltpu.VMEM((signals // 2, 2 * nfine, 2 * nfine), jnp.bfloat16),
            pltpu.VMEM((2, signals, frames, nfine), jnp.bfloat16),
            pltpu.SemaphoreType.DMA,
            pltpu.SemaphoreType.DMA((nchunk,)),
            pltpu.SemaphoreType.DMA((nchunk,)),
            pltpu.SemaphoreType.DMA((2,)),
            pltpu.SemaphoreType.DMA((nchunk,)),
        ],
        compiler_params=pltpu.CompilerParams(
            collective_id=0, has_side_effects=True, vmem_limit_bytes=56 * 2**20
        ),
        cost_estimate=pl.CostEstimate(
            flops=8 * 2**27, bytes_accessed=4 * 2**20, transcendentals=0
        ),
        name="resynthesis",
    )(spectra, delays, flags, taps)


def solution(mesh):
    ntm, nchan = mesh.shape["tm"], mesh.shape["chan"]

    def body(spectra, delays, flags, taps):
        return per_device(ntm, nchan, spectra, delays, flags, taps)

    in_specs = (P(None, "chan", None, "tm"), P(), P(), P())
    return jax.shard_map(
        body, mesh=mesh, in_specs=in_specs, out_specs=P(None, "chan", "tm", None), check_vma=False
    )
```

```python
import math

import jax
import jax.numpy as jnp
from jax import lax
from jax.experimental import pallas as pl
from jax.experimental.pallas import tpu as pltpu
from jax.sharding import PartitionSpec as P

TAPS = 12
LANES = 128
HALO = 16


def fill_tables(chan, delays_ref, flags_ref, hi_ref, lo_ref):
    tiles, rows, cols = hi_ref.shape
    nfine = rows // 2
    row = lax.broadcasted_iota(jnp.int32, (rows, cols), 0)
    col = lax.broadcasted_iota(jnp.int32, (rows, cols), 1)
    fine = (row >> 3) * 4 + (row & 3)
    sample = col & (nfine - 1)
    quarter = (((row >> 2) & 1) - (col >> 7)) * (nfine // 4)
    frow = lax.broadcasted_iota(jnp.int32, (rows, nfine), 0)
    fcol = lax.broadcasted_iota(jnp.int32, (rows, nfine), 1)
    spread = (fcol == (frow >> 3) * 4 + (frow & 3)).astype(jnp.float32).astype(jnp.bfloat16)
    kept = jnp.dot(
        spread,
        flags_ref[...].astype(jnp.float32).astype(jnp.bfloat16),
        preferred_element_type=jnp.float32,
    )

    def one_tile(t, carry):
        tile = chan * tiles + t
        delay = delays_ref[tile]
        turn = (fine * (sample - delay) + quarter) & (nfine - 1)
        fold = nfine // 4 - jnp.abs(turn - nfine // 2)
        x = fold.astype(jnp.float32) * (2.0 * math.pi / nfine)
        x2 = x * x
        poly = -1.0 / 39916800.0
        for c in (1.0 / 362880.0, -1.0 / 5040.0, 1.0 / 120.0, -1.0 / 6.0, 1.0):
            poly = poly * x2 + c
        lane = lax.broadcasted_iota(jnp.int32, kept.shape, 1)
        keep = jnp.sum(jnp.where(lane == tile, kept, 0.0), axis=1, keepdims=True)
        table = (poly * x) * (keep * (-1.0 / math.sqrt(nfine)))
        hi = table.astype(jnp.bfloat16)
        hi_ref[t] = hi
        lo_ref[t] = (table - hi.astype(jnp.float32)).astype(jnp.bfloat16)
        return carry

    lax.fori_loop(0, tiles, one_tile, 0)


def stages_of(nchunk, tiles):
    whole = [(nchunk - 1, 0, tiles)] + [(fc, 0, tiles) for fc in range(nchunk - 2)]
    half = tiles // 2
    return whole + [(nchunk - 2, 0, half)] + [(nchunk - 2, t, t + 1) for t in range(half, tiles)]


def kernel(
    ntm,
    nchan,
    spectra_ref,
    delays_ref,
    flags_ref,
    taps_ref,
    out_ref,
    raw,
    mix,
    send,
    recv,
    passing,
    y,
    hi,
    lo,
    result,
    raw_sem,
    send_sem,
    recv_sem,
    relay_send_sem,
    relay_recv_sem,
    halo_sem,
    out_sem,
):
    tm = lax.axis_index("tm")
    chan = lax.axis_index("chan")
    nchunk, _, rows, _ = send.shape
    signals = rows // 8
    tiles = signals // 2
    chips = nchan // 2
    chip, core = chan >> 1, chan & 1
    stages = stages_of(nchunk, tiles)
    order = [fc for i, (fc, _, _) in enumerate(stages) if fc not in [s[0] for s in stages[:i]]]

    def around(away):
        return lax.rem(chip + away, chips)

    loads = {}
    for fc in order:
        loads[fc] = pltpu.make_async_copy(
            spectra_ref.at[:, :, :, fc * LANES : (fc + 1) * LANES], raw.at[fc], raw_sem.at[fc]
        )
        loads[fc].start()

    barrier = pltpu.get_barrier_semaphore()

    def greet(j, carry):
        pl.semaphore_signal(barrier, inc=1, device_id={"chan": lax.rem(chan + j, nchan)})
        return carry

    lax.fori_loop(1, nchan, greet, 0)

    @pl.when(tm > 0)
    def _():
        pl.semaphore_signal(barrier, inc=1, device_id={"tm": tm - 1})

    def arrange(fc, pair):
        at = pl.ds(pl.multiple_of(pair * 16, 16), 16)
        part = raw[fc, :, :, at, :].astype(jnp.float32)
        for q in range(2):
            for c in range(2):
                for k in range(4):
                    mix[q, pl.ds(c * 4 + k, signals, stride=8), :] = part[c, k, q * 8 : q * 8 + 8, :]
        for q in range(2):
            send[fc, pair * 2 + q] = mix[q].astype(jnp.bfloat16)

    def push(stage, to):
        fc, first, last = stages[stage]
        at = pl.ds(first * 16, (last - first) * 16)
        pltpu.make_async_remote_copy(
            src_ref=send.at[fc, to, at],
            dst_ref=recv.at[fc, chan, at],
            send_sem=send_sem.at[stage],
            recv_sem=recv_sem.at[stage],
            device_id={"chan": to},
        ).start()

    def keep(stage):
        fc, first, last = stages[stage]
        at = pl.ds(first * 16, (last - first) * 16)
        pltpu.make_async_copy(
            send.at[fc, chan, at], recv.at[fc, chan, at], recv_sem.at[stage]
        ).start()

    opposite = around(chips // 2)
    onward = around(jnp.where(core == 0, chips // 4, chips - chips // 4))
    origin = around(jnp.where(core == 0, chips - chips // 4, chips // 4)) * 2 + core

    def relay(fc):
        return pltpu.make_async_remote_copy(
            src_ref=send.at[fc, pl.ds(opposite * 2, 2)],
            dst_ref=passing.at[fc],
            send_sem=relay_send_sem.at[fc],
            recv_sem=relay_recv_sem.at[fc],
            device_id={"chan": onward * 2 + core},
        )

    def forward(stage):
        fc, first, last = stages[stage]
        at = pl.ds(first * 16, (last - first) * 16)
        for q in range(2):
            pltpu.make_async_remote_copy(
                src_ref=passing.at[fc, q, at],
                dst_ref=recv.at[fc, origin, at],
                send_sem=send_sem.at[stage],
                recv_sem=recv_sem.at[stage],
                device_id={"chan": onward * 2 + q},
            ).start()

    for fc in order:
        loads[fc].wait()
        arrange(fc, opposite)

    pl.semaphore_wait(barrier, nchan - 1 + jnp.where(tm < ntm - 1, 1, 0))

    for fc in order:
        relay(fc).start()

    def each_chip(work):
        def body(i, carry):
            far = chips // 2 - 1 - (i >> 1)
            work(around(jnp.where((i & 1) == 0, far, chips - far)))
            return carry

        lax.fori_loop(0, chips - 2, body, 0)

    for stage, (fc, first, last) in enumerate(stages):
        fresh = first == 0

        def to_chip(pair):
            if fresh:
                arrange(fc, pair)
            push(stage, pair * 2 + core)
            push(stage, pair * 2 + 1 - core)

        each_chip(to_chip)
        if fresh:
            arrange(fc, chip)
            relay(fc).wait_recv()
        forward(stage)
        push(stage, chip * 2 + 1 - core)
        keep(stage)

    fill_tables(chan, delays_ref, flags_ref, hi, lo)

    @pl.when(tm == 0)
    def _():
        y[:, :, 0:HALO, :] = jnp.zeros((2, signals, HALO, LANES), jnp.float32)

    def transform(stage):
        fc, first, last = stages[stage]
        base = HALO + fc * LANES

        def one_tile(t, carry):
            part = recv[fc, :, pl.ds(pl.multiple_of(t * 16, 16), 16), :].astype(jnp.float32)
            for p in range(2):
                x = part[:, p * 8 : p * 8 + 8, :].reshape(nchan * 8, LANES).astype(jnp.bfloat16)
                dims = (((0,), (0,)), ((), ()))
                z = lax.dot_general(x, hi[t], dims, preferred_element_type=jnp.float32)
                z += lax.dot_general(x, lo[t], dims, preferred_element_type=jnp.float32)
                y[0, t * 2 + p, base : base + LANES, :] = z[:, :LANES]
                y[1, t * 2 + p, base : base + LANES, :] = z[:, LANES:]
            return carry

        lax.fori_loop(first, last, one_tile, 0)

    def fir(stage, begin, end):
        _, first, last = stages[stage]
        sigs = 2 * (last - first)

        def one(i, carry):
            d, s = i // sigs, 2 * first + lax.rem(i, sigs)
            for row in range(begin, end, 64):
                count = min(64, end - row)
                total = None
                for j in range(TAPS):
                    start = HALO + row - j
                    term = taps_ref[j : j + 1, :] * y[d, s, start : start + count, :]
                    total = term if total is None else total + term
                result[d, s, row : row + count, :] = total.astype(jnp.bfloat16)
            return carry

        lax.fori_loop(0, 2 * sigs, one, 0)

    frames = nchunk * LANES
    halo = pltpu.make_async_remote_copy(
        src_ref=y.at[:, :, frames : frames + HALO, :],
        dst_ref=y.at[:, :, 0:HALO, :],
        send_sem=halo_sem.at[0],
        recv_sem=halo_sem.at[1],
        device_id={"tm": lax.rem(tm + 1, ntm)},
    )

    stores = []
    for stage, (fc, first, last) in enumerate(stages):
        arriving = recv.at[fc, :, first * 16 : last * 16]
        pltpu.make_async_copy(arriving, arriving, recv_sem.at[stage]).wait()
        transform(stage)
        if stage == 0:

            @pl.when(tm < ntm - 1)
            def _():
                halo.start()

        if fc == 0:

            @pl.when(tm > 0)
            def _():
                halo.wait_recv()

        begin = fc * LANES + (HALO if stage == 0 else 0)
        end = (fc + 1) * LANES + (HALO if fc == nchunk - 2 else 0)
        fir(stage, begin, end)
        at = (slice(None), slice(2 * first, 2 * last), slice(begin, end))
        stores.append(pltpu.make_async_copy(result.at[at], out_ref.at[at], out_sem.at[stage]))
        stores[-1].start()

    for stage, (fc, first, last) in enumerate(stages):
        sent = send.at[fc, 0 : nchan - 1, first * 16 : last * 16]
        pltpu.make_async_copy(sent, sent, send_sem.at[stage]).wait()
    for fc in order:
        relay(fc).wait_send()

    @pl.when(tm < ntm - 1)
    def _():
        halo.wait_send()

    for copy in stores:
        copy.wait()


def per_device(ntm, nchan, spectra, delays, flags, taps):
    parts, chans, sigs, frames = spectra.shape
    signals = sigs // nchan
    nfine = chans * nchan
    nchunk = frames // LANES
    rows = parts * chans * signals
    nstage = len(stages_of(nchunk, signals // 2))
    any_spec = pl.BlockSpec(memory_space=pl.ANY)
    vmem_spec = pl.BlockSpec(memory_space=pltpu.VMEM)
    smem_spec = pl.BlockSpec(memory_space=pltpu.SMEM)

    def body(*refs):
        kernel(ntm, nchan, *refs)

    return pl.pallas_call(
        body,
        out_shape=jax.ShapeDtypeStruct((2, signals, frames, nfine), jnp.bfloat16),
        in_specs=[any_spec, smem_spec, vmem_spec, vmem_spec],
        out_specs=any_spec,
        scratch_shapes=[
            pltpu.VMEM((nchunk, parts, chans, sigs, LANES), jnp.bfloat16),
            pltpu.VMEM((2, rows, LANES), jnp.float32),
            pltpu.VMEM((nchunk, nchan, rows, LANES), jnp.bfloat16),
            pltpu.VMEM((nchunk, nchan, rows, LANES), jnp.bfloat16),
            pltpu.VMEM((nchunk, 2, rows, LANES), jnp.bfloat16),
            pltpu.VMEM((2, signals, HALO + frames, nfine), jnp.float32),
            pltpu.VMEM((signals // 2, 2 * nfine, 2 * nfine), jnp.bfloat16),
            pltpu.VMEM((signals // 2, 2 * nfine, 2 * nfine), jnp.bfloat16),
            pltpu.VMEM((2, signals, frames, nfine), jnp.bfloat16),
            pltpu.SemaphoreType.DMA((nchunk,)),
            pltpu.SemaphoreType.DMA((nstage,)),
            pltpu.SemaphoreType.DMA((nstage,)),
            pltpu.SemaphoreType.DMA((nchunk,)),
            pltpu.SemaphoreType.DMA((nchunk,)),
            pltpu.SemaphoreType.DMA((2,)),
            pltpu.SemaphoreType.DMA((nstage,)),
        ],
        compiler_params=pltpu.CompilerParams(
            collective_id=0, has_side_effects=True, vmem_limit_bytes=56 * 2**20
        ),
        cost_estimate=pl.CostEstimate(
            flops=8 * 2**27, bytes_accessed=4 * 2**20, transcendentals=0
        ),
        name="resynthesis",
    )(spectra, delays, flags, taps)


def solution(mesh):
    ntm, nchan = mesh.shape["tm"], mesh.shape["chan"]

    def body(spectra, delays, flags, taps):
        return per_device(ntm, nchan, spectra, delays, flags, taps)

    in_specs = (P(None, "chan", None, "tm"), P(), P(), P())
    return jax.shard_map(
        body, mesh=mesh, in_specs=in_specs, out_specs=P(None, "chan", "tm", None), check_vma=False
    )
```

```python
import math

import jax
import jax.numpy as jnp
from jax import lax
from jax.experimental import pallas as pl
from jax.experimental.pallas import tpu as pltpu
from jax.sharding import PartitionSpec as P

TAPS = 12
LANES = 128
HALO = 16


def fill_tables(chan, delays_ref, flags_ref, hi_ref, lo_ref):
    tiles, rows, cols = hi_ref.shape
    nfine = rows // 2
    row = lax.broadcasted_iota(jnp.int32, (rows, cols), 0)
    col = lax.broadcasted_iota(jnp.int32, (rows, cols), 1)
    fine = (row >> 3) * 4 + (row & 3)
    sample = col & (nfine - 1)
    quarter = (((row >> 2) & 1) - (col >> 7)) * (nfine // 4)
    frow = lax.broadcasted_iota(jnp.int32, (rows, nfine), 0)
    fcol = lax.broadcasted_iota(jnp.int32, (rows, nfine), 1)
    spread = (fcol == (frow >> 3) * 4 + (frow & 3)).astype(jnp.float32).astype(jnp.bfloat16)
    kept = jnp.dot(
        spread,
        flags_ref[...].astype(jnp.float32).astype(jnp.bfloat16),
        preferred_element_type=jnp.float32,
    )

    def one_tile(t, carry):
        tile = chan * tiles + t
        delay = delays_ref[tile]
        turn = (fine * (sample - delay) + quarter) & (nfine - 1)
        fold = nfine // 4 - jnp.abs(turn - nfine // 2)
        x = fold.astype(jnp.float32) * (2.0 * math.pi / nfine)
        x2 = x * x
        poly = -1.0 / 39916800.0
        for c in (1.0 / 362880.0, -1.0 / 5040.0, 1.0 / 120.0, -1.0 / 6.0, 1.0):
            poly = poly * x2 + c
        lane = lax.broadcasted_iota(jnp.int32, kept.shape, 1)
        keep = jnp.sum(jnp.where(lane == tile, kept, 0.0), axis=1, keepdims=True)
        table = (poly * x) * (keep * (-1.0 / math.sqrt(nfine)))
        hi = table.astype(jnp.bfloat16)
        hi_ref[t] = hi
        lo_ref[t] = (table - hi.astype(jnp.float32)).astype(jnp.bfloat16)
        return carry

    lax.fori_loop(0, tiles, one_tile, 0)


def stages_of(nchunk, tiles):
    whole = [(nchunk - 1, 0, tiles)] + [(fc, 0, tiles) for fc in range(nchunk - 2)]
    half = tiles // 2
    return whole + [(nchunk - 2, 0, half)] + [(nchunk - 2, t, t + 1) for t in range(half, tiles)]


def kernel(
    ntm,
    nchan,
    spectra_ref,
    delays_ref,
    flags_ref,
    taps_ref,
    out_ref,
    raw,
    mix,
    send,
    recv,
    passing,
    y,
    hi,
    lo,
    result,
    raw_sem,
    send_sem,
    recv_sem,
    relay_send_sem,
    relay_recv_sem,
    halo_sem,
    out_sem,
):
    tm = lax.axis_index("tm")
    chan = lax.axis_index("chan")
    nchunk, _, rows, _ = send.shape
    signals = rows // 8
    tiles = signals // 2
    chips = nchan // 2
    chip, core = chan >> 1, chan & 1
    stages = stages_of(nchunk, tiles)
    order = [fc for i, (fc, _, _) in enumerate(stages) if fc not in [s[0] for s in stages[:i]]]

    def around(away):
        return lax.rem(chip + away, chips)

    loads = {}
    for fc in order:
        loads[fc] = pltpu.make_async_copy(
            spectra_ref.at[:, :, :, fc * LANES : (fc + 1) * LANES], raw.at[fc], raw_sem.at[fc]
        )
        loads[fc].start()

    barrier = pltpu.get_barrier_semaphore()

    def greet(j, carry):
        pl.semaphore_signal(barrier, inc=1, device_id={"chan": lax.rem(chan + j, nchan)})
        return carry

    lax.fori_loop(1, nchan, greet, 0)

    @pl.when(tm > 0)
    def _():
        pl.semaphore_signal(barrier, inc=1, device_id={"tm": tm - 1})

    def arrange(fc, pair):
        at = pl.ds(pl.multiple_of(pair * 16, 16), 16)
        part = raw[fc, :, :, at, :].astype(jnp.float32)
        for q in range(2):
            for c in range(2):
                for k in range(4):
                    mix[q, pl.ds(c * 4 + k, signals, stride=8), :] = part[c, k, q * 8 : q * 8 + 8, :]
        for q in range(2):
            send[fc, pair * 2 + q] = mix[q].astype(jnp.bfloat16)

    def push(stage, to):
        fc, first, last = stages[stage]
        at = pl.ds(first * 16, (last - first) * 16)
        pltpu.make_async_remote_copy(
            src_ref=send.at[fc, to, at],
            dst_ref=recv.at[fc, chan, at],
            send_sem=send_sem.at[stage],
            recv_sem=recv_sem.at[stage],
            device_id={"chan": to},
        ).start()

    def keep(stage):
        fc, first, last = stages[stage]
        at = pl.ds(first * 16, (last - first) * 16)
        pltpu.make_async_copy(
            send.at[fc, chan, at], recv.at[fc, chan, at], recv_sem.at[stage]
        ).start()

    opposite = around(chips // 2)
    onward = around(jnp.where(core == 0, chips // 4, chips - chips // 4))
    origin = around(jnp.where(core == 0, chips - chips // 4, chips // 4)) * 2 + core

    def relay(fc):
        return pltpu.make_async_remote_copy(
            src_ref=send.at[fc, pl.ds(opposite * 2, 2)],
            dst_ref=passing.at[fc],
            send_sem=relay_send_sem.at[fc],
            recv_sem=relay_recv_sem.at[fc],
            device_id={"chan": onward * 2 + core},
        )

    def forward(stage):
        fc, first, last = stages[stage]
        at = pl.ds(first * 16, (last - first) * 16)
        for q in range(2):
            pltpu.make_async_remote_copy(
                src_ref=passing.at[fc, q, at],
                dst_ref=recv.at[fc, origin, at],
                send_sem=send_sem.at[stage],
                recv_sem=recv_sem.at[stage],
                device_id={"chan": onward * 2 + q},
            ).start()

    for fc in order:
        loads[fc].wait()
        arrange(fc, opposite)

    pl.semaphore_wait(barrier, nchan - 1 + jnp.where(tm < ntm - 1, 1, 0))

    for fc in order:
        relay(fc).start()

    def each_chip(work):
        def body(i, carry):
            far = chips // 2 - 1 - (i >> 1)
            work(around(jnp.where((i & 1) == 0, far, chips - far)))
            return carry

        lax.fori_loop(0, chips - 2, body, 0)

    def issue(stage):
        fc, first, last = stages[stage]
        fresh = first == 0

        def to_chip(pair):
            if fresh:
                arrange(fc, pair)
            push(stage, pair * 2 + core)
            push(stage, pair * 2 + 1 - core)

        each_chip(to_chip)
        if fresh:
            arrange(fc, chip)
            relay(fc).wait_recv()
        forward(stage)
        push(stage, chip * 2 + 1 - core)
        keep(stage)

    def left(stage):
        fc, first, last = stages[stage]
        sent = send.at[fc, 0 : nchan - 1, first * 16 : last * 16]
        pltpu.make_async_copy(sent, sent, send_sem.at[stage]).wait()

    issue(0)
    issue(1)
    fill_tables(chan, delays_ref, flags_ref, hi, lo)

    @pl.when(tm == 0)
    def _():
        y[:, :, 0:HALO, :] = jnp.zeros((2, signals, HALO, LANES), jnp.float32)

    def transform(stage):
        fc, first, last = stages[stage]
        base = HALO + fc * LANES

        def one_tile(t, carry):
            part = recv[fc, :, pl.ds(pl.multiple_of(t * 16, 16), 16), :].astype(jnp.float32)
            pols = [part[:, p * 8 : p * 8 + 8, :].reshape(nchan * 8, LANES) for p in range(2)]
            x = jnp.concatenate(pols, axis=1).astype(jnp.bfloat16)
            dims = (((0,), (0,)), ((), ()))
            z = lax.dot_general(x, hi[t], dims, preferred_element_type=jnp.float32)
            z += lax.dot_general(x, lo[t], dims, preferred_element_type=jnp.float32)
            for p in range(2):
                of = slice(p * LANES, (p + 1) * LANES)
                y[0, t * 2 + p, base : base + LANES, :] = z[of, :LANES]
                y[1, t * 2 + p, base : base + LANES, :] = z[of, LANES:]
            return carry

        lax.fori_loop(first, last, one_tile, 0)

    def fir(stage, begin, end):
        _, first, last = stages[stage]
        sigs = 2 * (last - first)

        def one(i, carry):
            d, s = i // sigs, 2 * first + lax.rem(i, sigs)
            for row in range(begin, end, 64):
                count = min(64, end - row)
                total = None
                for j in range(TAPS):
                    start = HALO + row - j
                    term = taps_ref[j : j + 1, :] * y[d, s, start : start + count, :]
                    total = term if total is None else total + term
                result[d, s, row : row + count, :] = total.astype(jnp.bfloat16)
            return carry

        lax.fori_loop(0, 2 * sigs, one, 0)

    frames = nchunk * LANES
    halo = pltpu.make_async_remote_copy(
        src_ref=y.at[:, :, frames : frames + HALO, :],
        dst_ref=y.at[:, :, 0:HALO, :],
        send_sem=halo_sem.at[0],
        recv_sem=halo_sem.at[1],
        device_id={"tm": lax.rem(tm + 1, ntm)},
    )

    stores = []
    for stage, (fc, first, last) in enumerate(stages):
        if stage + 2 < len(stages):
            left(stage)
            issue(stage + 2)
        arriving = recv.at[fc, :, first * 16 : last * 16]
        pltpu.make_async_copy(arriving, arriving, recv_sem.at[stage]).wait()
        transform(stage)
        if stage == 0:

            @pl.when(tm < ntm - 1)
            def _():
                halo.start()

        if fc == 0:

            @pl.when(tm > 0)
            def _():
                halo.wait_recv()

        begin = fc * LANES + (HALO if stage == 0 else 0)
        end = (fc + 1) * LANES + (HALO if fc == nchunk - 2 else 0)
        fir(stage, begin, end)
        at = (slice(None), slice(2 * first, 2 * last), slice(begin, end))
        stores.append(pltpu.make_async_copy(result.at[at], out_ref.at[at], out_sem.at[stage]))
        stores[-1].start()

    for stage in range(len(stages) - 2, len(stages)):
        left(stage)
    for fc in order:
        relay(fc).wait_send()

    @pl.when(tm < ntm - 1)
    def _():
        halo.wait_send()

    for copy in stores:
        copy.wait()


def per_device(ntm, nchan, spectra, delays, flags, taps):
    parts, chans, sigs, frames = spectra.shape
    signals = sigs // nchan
    nfine = chans * nchan
    nchunk = frames // LANES
    rows = parts * chans * signals
    nstage = len(stages_of(nchunk, signals // 2))
    any_spec = pl.BlockSpec(memory_space=pl.ANY)
    vmem_spec = pl.BlockSpec(memory_space=pltpu.VMEM)
    smem_spec = pl.BlockSpec(memory_space=pltpu.SMEM)

    def body(*refs):
        kernel(ntm, nchan, *refs)

    return pl.pallas_call(
        body,
        out_shape=jax.ShapeDtypeStruct((2, signals, frames, nfine), jnp.bfloat16),
        in_specs=[any_spec, smem_spec, vmem_spec, vmem_spec],
        out_specs=any_spec,
        scratch_shapes=[
            pltpu.VMEM((nchunk, parts, chans, sigs, LANES), jnp.bfloat16),
            pltpu.VMEM((2, rows, LANES), jnp.float32),
            pltpu.VMEM((nchunk, nchan, rows, LANES), jnp.bfloat16),
            pltpu.VMEM((nchunk, nchan, rows, LANES), jnp.bfloat16),
            pltpu.VMEM((nchunk, 2, rows, LANES), jnp.bfloat16),
            pltpu.VMEM((2, signals, HALO + frames, nfine), jnp.float32),
            pltpu.VMEM((signals // 2, 2 * nfine, 2 * nfine), jnp.bfloat16),
            pltpu.VMEM((signals // 2, 2 * nfine, 2 * nfine), jnp.bfloat16),
            pltpu.VMEM((2, signals, frames, nfine), jnp.bfloat16),
            pltpu.SemaphoreType.DMA((nchunk,)),
            pltpu.SemaphoreType.DMA((nstage,)),
            pltpu.SemaphoreType.DMA((nstage,)),
            pltpu.SemaphoreType.DMA((nchunk,)),
            pltpu.SemaphoreType.DMA((nchunk,)),
            pltpu.SemaphoreType.DMA((2,)),
            pltpu.SemaphoreType.DMA((nstage,)),
        ],
        compiler_params=pltpu.CompilerParams(
            collective_id=0, has_side_effects=True, vmem_limit_bytes=56 * 2**20
        ),
        cost_estimate=pl.CostEstimate(
            flops=8 * 2**27, bytes_accessed=4 * 2**20, transcendentals=0
        ),
        name="resynthesis",
    )(spectra, delays, flags, taps)


def solution(mesh):
    ntm, nchan = mesh.shape["tm"], mesh.shape["chan"]

    def body(spectra, delays, flags, taps):
        return per_device(ntm, nchan, spectra, delays, flags, taps)

    in_specs = (P(None, "chan", None, "tm"), P(), P(), P())
    return jax.shard_map(
        body, mesh=mesh, in_specs=in_specs, out_specs=P(None, "chan", "tm", None), check_vma=False
    )
```

```python
import math

import jax
import jax.numpy as jnp
from jax import lax
from jax.experimental import pallas as pl
from jax.experimental.pallas import tpu as pltpu
from jax.sharding import PartitionSpec as P

TAPS = 12
LANES = 128
HALO = 16


def fill_tables(chan, delays_ref, flags_ref, hi_ref, lo_ref):
    tiles, rows, cols = hi_ref.shape
    nfine = rows // 2
    row = lax.broadcasted_iota(jnp.int32, (rows, cols), 0)
    col = lax.broadcasted_iota(jnp.int32, (rows, cols), 1)
    fine = (row >> 3) * 4 + (row & 3)
    sample = col & (nfine - 1)
    quarter = (((row >> 2) & 1) - (col >> 7)) * (nfine // 4)
    frow = lax.broadcasted_iota(jnp.int32, (rows, nfine), 0)
    fcol = lax.broadcasted_iota(jnp.int32, (rows, nfine), 1)
    spread = (fcol == (frow >> 3) * 4 + (frow & 3)).astype(jnp.float32).astype(jnp.bfloat16)
    kept = jnp.dot(
        spread,
        flags_ref[...].astype(jnp.float32).astype(jnp.bfloat16),
        preferred_element_type=jnp.float32,
    )

    def one_tile(t, carry):
        tile = chan * tiles + t
        delay = delays_ref[tile]
        turn = (fine * (sample - delay) + quarter) & (nfine - 1)
        fold = nfine // 4 - jnp.abs(turn - nfine // 2)
        x = fold.astype(jnp.float32) * (2.0 * math.pi / nfine)
        x2 = x * x
        poly = -1.0 / 39916800.0
        for c in (1.0 / 362880.0, -1.0 / 5040.0, 1.0 / 120.0, -1.0 / 6.0, 1.0):
            poly = poly * x2 + c
        lane = lax.broadcasted_iota(jnp.int32, kept.shape, 1)
        keep = jnp.sum(jnp.where(lane == tile, kept, 0.0), axis=1, keepdims=True)
        table = (poly * x) * (keep * (-1.0 / math.sqrt(nfine)))
        hi = table.astype(jnp.bfloat16)
        hi_ref[t] = hi
        lo_ref[t] = (table - hi.astype(jnp.float32)).astype(jnp.bfloat16)
        return carry

    lax.fori_loop(0, tiles, one_tile, 0)


def stages_of(nchunk, tiles):
    whole = [(nchunk - 1, 0, tiles)] + [(fc, 0, tiles) for fc in range(nchunk - 2)]
    half = tiles // 2
    return whole + [(nchunk - 2, 0, half)] + [(nchunk - 2, t, t + 1) for t in range(half, tiles)]


def kernel(
    ntm,
    nchan,
    spectra_ref,
    delays_hbm,
    flags_hbm,
    taps_hbm,
    out_ref,
    delays_ref,
    flags_ref,
    taps_ref,
    raw,
    mix,
    send,
    recv,
    passing,
    y,
    hi,
    lo,
    result,
    raw_sem,
    small_sem,
    send_sem,
    recv_sem,
    relay_send_sem,
    relay_recv_sem,
    halo_sem,
    out_sem,
):
    tm = lax.axis_index("tm")
    chan = lax.axis_index("chan")
    nchunk, _, rows, _ = send.shape
    signals = rows // 8
    tiles = signals // 2
    chips = nchan // 2
    chip, core = chan >> 1, chan & 1
    stages = stages_of(nchunk, tiles)
    order = [fc for i, (fc, _, _) in enumerate(stages) if fc not in [s[0] for s in stages[:i]]]

    def around(away):
        return lax.rem(chip + away, chips)

    barrier = pltpu.get_barrier_semaphore()

    def greet(j, carry):
        pl.semaphore_signal(barrier, inc=1, device_id={"chan": lax.rem(chan + j, nchan)})
        return carry

    lax.fori_loop(1, nchan, greet, 0)

    @pl.when(tm > 0)
    def _():
        pl.semaphore_signal(barrier, inc=1, device_id={"tm": tm - 1})

    loads = {}
    for fc in order:
        loads[fc] = pltpu.make_async_copy(
            spectra_ref.at[:, :, :, fc * LANES : (fc + 1) * LANES], raw.at[fc], raw_sem.at[fc]
        )
        loads[fc].start()

    small = [
        pltpu.make_async_copy(whole, mine, small_sem.at[i])
        for i, (whole, mine) in enumerate(
            ((delays_hbm, delays_ref), (flags_hbm, flags_ref), (taps_hbm, taps_ref))
        )
    ]
    for copy in small:
        copy.start()

    def arrange(fc, pair):
        at = pl.ds(pl.multiple_of(pair * 16, 16), 16)
        part = raw[fc, :, :, at, :].astype(jnp.float32)
        for q in range(2):
            for c in range(2):
                for k in range(4):
                    mix[q, pl.ds(c * 4 + k, signals, stride=8), :] = part[c, k, q * 8 : q * 8 + 8, :]
        for q in range(2):
            send[fc, pair * 2 + q] = mix[q].astype(jnp.bfloat16)

    def push(stage, to):
        fc, first, last = stages[stage]
        at = pl.ds(first * 16, (last - first) * 16)
        pltpu.make_async_remote_copy(
            src_ref=send.at[fc, to, at],
            dst_ref=recv.at[fc, chan, at],
            send_sem=send_sem.at[stage],
            recv_sem=recv_sem.at[stage],
            device_id={"chan": to},
        ).start()

    def keep(stage):
        fc, first, last = stages[stage]
        at = pl.ds(first * 16, (last - first) * 16)
        pltpu.make_async_copy(
            send.at[fc, chan, at], recv.at[fc, chan, at], recv_sem.at[stage]
        ).start()

    opposite = around(chips // 2)
    onward = around(jnp.where(core == 0, chips // 4, chips - chips // 4))
    origin = around(jnp.where(core == 0, chips - chips // 4, chips // 4)) * 2 + core

    def relay(fc):
        return pltpu.make_async_remote_copy(
            src_ref=send.at[fc, pl.ds(opposite * 2, 2)],
            dst_ref=passing.at[fc],
            send_sem=relay_send_sem.at[fc],
            recv_sem=relay_recv_sem.at[fc],
            device_id={"chan": onward * 2 + core},
        )

    def forward(stage):
        fc, first, last = stages[stage]
        at = pl.ds(first * 16, (last - first) * 16)
        for q in range(2):
            pltpu.make_async_remote_copy(
                src_ref=passing.at[fc, q, at],
                dst_ref=recv.at[fc, origin, at],
                send_sem=send_sem.at[stage],
                recv_sem=recv_sem.at[stage],
                device_id={"chan": onward * 2 + q},
            ).start()

    def each_chip(work):
        def body(i, carry):
            far = chips // 2 - 1 - (i >> 1)
            work(around(jnp.where((i & 1) == 0, far, chips - far)))
            return carry

        lax.fori_loop(0, chips - 2, body, 0)

    def issue(stage):
        fc, first, last = stages[stage]
        fresh = first == 0

        def to_chip(pair):
            if fresh:
                arrange(fc, pair)
            push(stage, pair * 2 + core)
            push(stage, pair * 2 + 1 - core)

        if fresh:
            loads[fc].wait()
            arrange(fc, opposite)
            if stage == 0:
                pl.semaphore_wait(barrier, nchan - 1 + jnp.where(tm < ntm - 1, 1, 0))
            relay(fc).start()
        each_chip(to_chip)
        if fresh:
            arrange(fc, chip)
            relay(fc).wait_recv()
        forward(stage)
        push(stage, chip * 2 + 1 - core)
        keep(stage)

    def left(stage):
        fc, first, last = stages[stage]
        sent = send.at[fc, 0 : nchan - 1, first * 16 : last * 16]
        pltpu.make_async_copy(sent, sent, send_sem.at[stage]).wait()

    issue(0)
    issue(1)
    for copy in small:
        copy.wait()
    fill_tables(chan, delays_ref, flags_ref, hi, lo)

    @pl.when(tm == 0)
    def _():
        y[:, :, 0:HALO, :] = jnp.zeros((2, signals, HALO, LANES), jnp.float32)

    def transform(stage):
        fc, first, last = stages[stage]
        base = HALO + fc * LANES

        def one_tile(t, carry):
            part = recv[fc, :, pl.ds(pl.multiple_of(t * 16, 16), 16), :].astype(jnp.float32)
            pols = [part[:, p * 8 : p * 8 + 8, :].reshape(nchan * 8, LANES) for p in range(2)]
            x = jnp.concatenate(pols, axis=1).astype(jnp.bfloat16)
            dims = (((0,), (0,)), ((), ()))
            z = lax.dot_general(x, hi[t], dims, preferred_element_type=jnp.float32)
            z += lax.dot_general(x, lo[t], dims, preferred_element_type=jnp.float32)
            for p in range(2):
                of = slice(p * LANES, (p + 1) * LANES)
                y[0, t * 2 + p, base : base + LANES, :] = z[of, :LANES]
                y[1, t * 2 + p, base : base + LANES, :] = z[of, LANES:]
            return carry

        lax.fori_loop(first, last, one_tile, 0)

    def fir(stage, begin, end):
        _, first, last = stages[stage]
        sigs = 2 * (last - first)

        def one(i, carry):
            d, s = i // sigs, 2 * first + lax.rem(i, sigs)
            for row in range(begin, end, 64):
                count = min(64, end - row)
                total = None
                for j in range(TAPS):
                    start = HALO + row - j
                    term = taps_ref[j : j + 1, :] * y[d, s, start : start + count, :]
                    total = term if total is None else total + term
                result[d, s, row : row + count, :] = total.astype(jnp.bfloat16)
            return carry

        lax.fori_loop(0, 2 * sigs, one, 0)

    frames = nchunk * LANES
    halo = pltpu.make_async_remote_copy(
        src_ref=y.at[:, :, frames : frames + HALO, :],
        dst_ref=y.at[:, :, 0:HALO, :],
        send_sem=halo_sem.at[0],
        recv_sem=halo_sem.at[1],
        device_id={"tm": lax.rem(tm + 1, ntm)},
    )

    stores = []
    for stage, (fc, first, last) in enumerate(stages):
        if stage + 2 < len(stages):
            left(stage)
            issue(stage + 2)
        arriving = recv.at[fc, :, first * 16 : last * 16]
        pltpu.make_async_copy(arriving, arriving, recv_sem.at[stage]).wait()
        transform(stage)
        if stage == 0:

            @pl.when(tm < ntm - 1)
            def _():
                halo.start()

        if fc == 0:

            @pl.when(tm > 0)
            def _():
                halo.wait_recv()

        begin = fc * LANES + (HALO if stage == 0 else 0)
        end = (fc + 1) * LANES + (HALO if fc == nchunk - 2 else 0)
        fir(stage, begin, end)
        at = (slice(None), slice(2 * first, 2 * last), slice(begin, end))
        stores.append(pltpu.make_async_copy(result.at[at], out_ref.at[at], out_sem.at[stage]))
        stores[-1].start()

    for stage in range(len(stages) - 2, len(stages)):
        left(stage)
    for fc in order:
        relay(fc).wait_send()

    @pl.when(tm < ntm - 1)
    def _():
        halo.wait_send()

    for copy in stores:
        copy.wait()


def hand_over(from_ref, to_ref, sem):
    copies = [
        pltpu.make_async_copy(from_ref.at[d, s], to_ref.at[d, s], sem.at[d, s])
        for d in range(from_ref.shape[0])
        for s in range(from_ref.shape[1])
    ]
    for copy in copies:
        copy.start()
    for copy in copies:
        copy.wait()


def per_device(ntm, nchan, spectra, delays, flags, taps):
    parts, chans, sigs, frames = spectra.shape
    signals = sigs // nchan
    nfine = chans * nchan
    nchunk = frames // LANES
    rows = parts * chans * signals
    nstage = len(stages_of(nchunk, signals // 2))
    any_spec = pl.BlockSpec(memory_space=pl.ANY)

    def body(*refs):
        kernel(ntm, nchan, *refs)

    voltages = pl.pallas_call(
        body,
        out_shape=jax.ShapeDtypeStruct((2, signals, frames, nfine), jnp.bfloat16),
        in_specs=[any_spec] * 4,
        out_specs=any_spec,
        scratch_shapes=[
            pltpu.SMEM(delays.shape, jnp.int32),
            pltpu.VMEM(flags.shape, jnp.int32),
            pltpu.VMEM(taps.shape, jnp.float32),
            pltpu.VMEM((nchunk, parts, chans, sigs, LANES), jnp.bfloat16),
            pltpu.VMEM((2, rows, LANES), jnp.float32),
            pltpu.VMEM((nchunk, nchan, rows, LANES), jnp.bfloat16),
            pltpu.VMEM((nchunk, nchan, rows, LANES), jnp.bfloat16),
            pltpu.VMEM((nchunk, 2, rows, LANES), jnp.bfloat16),
            pltpu.VMEM((2, signals, HALO + frames, nfine), jnp.float32),
            pltpu.VMEM((signals // 2, 2 * nfine, 2 * nfine), jnp.bfloat16),
            pltpu.VMEM((signals // 2, 2 * nfine, 2 * nfine), jnp.bfloat16),
            pltpu.VMEM((2, signals, frames, nfine), jnp.bfloat16),
            pltpu.SemaphoreType.DMA((nchunk,)),
            pltpu.SemaphoreType.DMA((3,)),
            pltpu.SemaphoreType.DMA((nstage,)),
            pltpu.SemaphoreType.DMA((nstage,)),
            pltpu.SemaphoreType.DMA((nchunk,)),
            pltpu.SemaphoreType.DMA((nchunk,)),
            pltpu.SemaphoreType.DMA((2,)),
            pltpu.SemaphoreType.DMA((nstage,)),
        ],
        compiler_params=pltpu.CompilerParams(
            collective_id=0, has_side_effects=True, vmem_limit_bytes=56 * 2**20
        ),
        cost_estimate=pl.CostEstimate(
            flops=8 * 2**27, bytes_accessed=4 * 2**20, transcendentals=0
        ),
        name="resynthesis",
    )(spectra, delays, flags, taps)
    return pl.pallas_call(
        hand_over,
        out_shape=jax.ShapeDtypeStruct(voltages.shape, voltages.dtype),
        in_specs=[any_spec],
        out_specs=any_spec,
        scratch_shapes=[pltpu.SemaphoreType.DMA((2, signals))],
        cost_estimate=pl.CostEstimate(flops=0, bytes_accessed=3 * 2**20, transcendentals=0),
        name="hand_over",
    )(voltages)


def solution(mesh):
    ntm, nchan = mesh.shape["tm"], mesh.shape["chan"]

    def body(spectra, delays, flags, taps):
        return per_device(ntm, nchan, spectra, delays, flags, taps)

    in_specs = (P(None, "chan", None, "tm"), P(), P(), P())
    return jax.shard_map(
        body, mesh=mesh, in_specs=in_specs, out_specs=P(None, "chan", "tm", None), check_vma=False
    )
```

```python
import math

import jax
import jax.numpy as jnp
from jax import lax
from jax.experimental import pallas as pl
from jax.experimental.pallas import tpu as pltpu
from jax.sharding import PartitionSpec as P

TAPS = 12
LANES = 128
HALO = 16


def fill_tables(chan, delays_ref, flags_ref, hi_ref, lo_ref):
    tiles, rows, cols = hi_ref.shape
    nfine = rows // 2
    row = lax.broadcasted_iota(jnp.int32, (rows, cols), 0)
    col = lax.broadcasted_iota(jnp.int32, (rows, cols), 1)
    fine = (row >> 3) * 4 + (row & 3)
    sample = col & (nfine - 1)
    quarter = (((row >> 2) & 1) - (col >> 7)) * (nfine // 4)
    frow = lax.broadcasted_iota(jnp.int32, (rows, nfine), 0)
    fcol = lax.broadcasted_iota(jnp.int32, (rows, nfine), 1)
    spread = (fcol == (frow >> 3) * 4 + (frow & 3)).astype(jnp.float32).astype(jnp.bfloat16)
    kept = jnp.dot(
        spread,
        flags_ref[...].astype(jnp.float32).astype(jnp.bfloat16),
        preferred_element_type=jnp.float32,
    )

    def one_tile(t, carry):
        tile = chan * tiles + t
        delay = delays_ref[tile]
        turn = (fine * (sample - delay) + quarter) & (nfine - 1)
        fold = nfine // 4 - jnp.abs(turn - nfine // 2)
        x = fold.astype(jnp.float32) * (2.0 * math.pi / nfine)
        x2 = x * x
        poly = -1.0 / 39916800.0
        for c in (1.0 / 362880.0, -1.0 / 5040.0, 1.0 / 120.0, -1.0 / 6.0, 1.0):
            poly = poly * x2 + c
        lane = lax.broadcasted_iota(jnp.int32, kept.shape, 1)
        keep = jnp.sum(jnp.where(lane == tile, kept, 0.0), axis=1, keepdims=True)
        table = (poly * x) * (keep * (-1.0 / math.sqrt(nfine)))
        hi = table.astype(jnp.bfloat16)
        hi_ref[t] = hi
        lo_ref[t] = (table - hi.astype(jnp.float32)).astype(jnp.bfloat16)
        return carry

    lax.fori_loop(0, tiles, one_tile, 0)


def stages_of(nchunk, tiles):
    whole = [(nchunk - 1, 0, tiles)] + [(fc, 0, tiles) for fc in range(nchunk - 2)]
    half = tiles // 2
    return whole + [(nchunk - 2, 0, half)] + [(nchunk - 2, t, t + 1) for t in range(half, tiles)]


def kernel(
    ntm,
    nchan,
    spectra_ref,
    delays_hbm,
    flags_hbm,
    taps_hbm,
    out_ref,
    delays_ref,
    flags_ref,
    taps_ref,
    raw,
    mix,
    send,
    recv,
    passing,
    y,
    hi,
    lo,
    result,
    raw_sem,
    small_sem,
    send_sem,
    recv_sem,
    relay_send_sem,
    relay_recv_sem,
    halo_sem,
    out_sem,
):
    tm = lax.axis_index("tm")
    chan = lax.axis_index("chan")
    nchunk, _, rows, _ = send.shape
    signals = rows // 8
    tiles = signals // 2
    chips = nchan // 2
    chip, core = chan >> 1, chan & 1
    stages = stages_of(nchunk, tiles)
    order = [fc for i, (fc, _, _) in enumerate(stages) if fc not in [s[0] for s in stages[:i]]]

    def around(away):
        return lax.rem(chip + away, chips)

    barrier = pltpu.get_barrier_semaphore()

    def greet(j, carry):
        pl.semaphore_signal(barrier, inc=1, device_id={"chan": lax.rem(chan + j, nchan)})
        return carry

    lax.fori_loop(1, nchan, greet, 0)

    @pl.when(tm > 0)
    def _():
        pl.semaphore_signal(barrier, inc=1, device_id={"tm": tm - 1})

    loads = {}
    for fc in order:
        loads[fc] = pltpu.make_async_copy(
            spectra_ref.at[:, :, :, fc * LANES : (fc + 1) * LANES], raw.at[fc], raw_sem.at[fc]
        )
        loads[fc].start()

    small = [
        pltpu.make_async_copy(whole, mine, small_sem.at[i])
        for i, (whole, mine) in enumerate(
            ((delays_hbm, delays_ref), (flags_hbm, flags_ref), (taps_hbm, taps_ref))
        )
    ]
    for copy in small:
        copy.start()

    def arrange(fc, pair):
        at = pl.ds(pl.multiple_of(pair * 16, 16), 16)
        part = raw[fc, :, :, at, :].astype(jnp.float32)
        for q in range(2):
            for c in range(2):
                for k in range(4):
                    mix[q, pl.ds(c * 4 + k, signals, stride=8), :] = part[c, k, q * 8 : q * 8 + 8, :]
        for q in range(2):
            send[fc, pair * 2 + q] = mix[q].astype(jnp.bfloat16)

    def push(stage, to):
        fc, first, last = stages[stage]
        at = pl.ds(first * 16, (last - first) * 16)
        pltpu.make_async_remote_copy(
            src_ref=send.at[fc, to, at],
            dst_ref=recv.at[fc, chan, at],
            send_sem=send_sem.at[stage],
            recv_sem=recv_sem.at[stage],
            device_id={"chan": to},
        ).start()

    def keep(stage):
        fc, first, last = stages[stage]
        at = pl.ds(first * 16, (last - first) * 16)
        pltpu.make_async_copy(
            send.at[fc, chan, at], recv.at[fc, chan, at], recv_sem.at[stage]
        ).start()

    opposite = around(chips // 2)
    onward = around(jnp.where(core == 0, chips // 4, chips - chips // 4))
    origin = around(jnp.where(core == 0, chips - chips // 4, chips // 4)) * 2 + core

    def relay(fc):
        return pltpu.make_async_remote_copy(
            src_ref=send.at[fc, pl.ds(opposite * 2, 2)],
            dst_ref=passing.at[fc],
            send_sem=relay_send_sem.at[fc],
            recv_sem=relay_recv_sem.at[fc],
            device_id={"chan": onward * 2 + core},
        )

    def forward(stage):
        fc, first, last = stages[stage]
        at = pl.ds(first * 16, (last - first) * 16)
        for q in range(2):
            pltpu.make_async_remote_copy(
                src_ref=passing.at[fc, q, at],
                dst_ref=recv.at[fc, origin, at],
                send_sem=send_sem.at[stage],
                recv_sem=recv_sem.at[stage],
                device_id={"chan": onward * 2 + q},
            ).start()

    def each_chip(work):
        def body(i, carry):
            far = chips // 2 - 1 - (i >> 1)
            work(around(jnp.where((i & 1) == 0, far, chips - far)))
            return carry

        lax.fori_loop(0, chips - 2, body, 0)

    def issue(stage):
        fc, first, last = stages[stage]
        fresh = first == 0

        def to_chip(pair):
            if fresh:
                arrange(fc, pair)
            push(stage, pair * 2 + core)
            push(stage, pair * 2 + 1 - core)

        if fresh:
            loads[fc].wait()
            arrange(fc, opposite)
            if stage == 0:
                pl.semaphore_wait(barrier, nchan - 1 + jnp.where(tm < ntm - 1, 1, 0))
            relay(fc).start()
        each_chip(to_chip)
        if fresh:
            arrange(fc, chip)
            relay(fc).wait_recv()
        forward(stage)
        push(stage, chip * 2 + 1 - core)
        keep(stage)

    def left(stage):
        fc, first, last = stages[stage]
        sent = send.at[fc, 0 : nchan - 1, first * 16 : last * 16]
        pltpu.make_async_copy(sent, sent, send_sem.at[stage]).wait()

    issue(0)
    issue(1)
    for copy in small:
        copy.wait()
    fill_tables(chan, delays_ref, flags_ref, hi, lo)

    @pl.when(tm == 0)
    def _():
        y[:, :, 0:HALO, :] = jnp.zeros((2, signals, HALO, LANES), jnp.float32)

    def transform(stage):
        fc, first, last = stages[stage]
        base = HALO + fc * LANES

        def one_tile(t, carry):
            part = recv[fc, :, pl.ds(pl.multiple_of(t * 16, 16), 16), :].astype(jnp.float32)
            pols = [part[:, p * 8 : p * 8 + 8, :].reshape(nchan * 8, LANES) for p in range(2)]
            x = jnp.concatenate(pols, axis=1).astype(jnp.bfloat16)
            dims = (((0,), (0,)), ((), ()))
            z = lax.dot_general(x, hi[t], dims, preferred_element_type=jnp.float32)
            z += lax.dot_general(x, lo[t], dims, preferred_element_type=jnp.float32)
            for p in range(2):
                of = slice(p * LANES, (p + 1) * LANES)
                y[0, t * 2 + p, base : base + LANES, :] = z[of, :LANES]
                y[1, t * 2 + p, base : base + LANES, :] = z[of, LANES:]
            return carry

        lax.fori_loop(first, last, one_tile, 0)

    def fir(stage, begin, end):
        _, first, last = stages[stage]
        sigs = 2 * (last - first)

        def one(i, carry):
            d, s = i // sigs, 2 * first + lax.rem(i, sigs)
            for row in range(begin, end, 64):
                count = min(64, end - row)
                total = None
                for j in range(TAPS):
                    start = HALO + row - j
                    term = taps_ref[j : j + 1, :] * y[d, s, start : start + count, :]
                    total = term if total is None else total + term
                result[d, s, row : row + count, :] = total.astype(jnp.bfloat16)
            return carry

        lax.fori_loop(0, 2 * sigs, one, 0)

    frames = nchunk * LANES
    halo = pltpu.make_async_remote_copy(
        src_ref=y.at[:, :, frames : frames + HALO, :],
        dst_ref=y.at[:, :, 0:HALO, :],
        send_sem=halo_sem.at[0],
        recv_sem=halo_sem.at[1],
        device_id={"tm": lax.rem(tm + 1, ntm)},
    )

    stores = []
    for stage, (fc, first, last) in enumerate(stages):
        if stage + 2 < len(stages):
            left(stage)
            issue(stage + 2)
        arriving = recv.at[fc, :, first * 16 : last * 16]
        pltpu.make_async_copy(arriving, arriving, recv_sem.at[stage]).wait()
        transform(stage)
        if stage == 0:

            @pl.when(tm < ntm - 1)
            def _():
                halo.start()

        if fc == 0:

            @pl.when(tm > 0)
            def _():
                halo.wait_recv()

        begin = fc * LANES + (HALO if stage == 0 else 0)
        end = (fc + 1) * LANES + (HALO if fc == nchunk - 2 else 0)
        fir(stage, begin, end)
        at = (slice(None), slice(2 * first, 2 * last), slice(begin, end))
        stores.append(pltpu.make_async_copy(result.at[at], out_ref.at[at], out_sem.at[stage]))
        stores[-1].start()

    for stage in range(len(stages) - 2, len(stages)):
        left(stage)
    for fc in order:
        relay(fc).wait_send()

    @pl.when(tm < ntm - 1)
    def _():
        halo.wait_send()

    for copy in stores:
        copy.wait()


def per_device(ntm, nchan, spectra, delays, flags, taps):
    parts, chans, sigs, frames = spectra.shape
    signals = sigs // nchan
    nfine = chans * nchan
    nchunk = frames // LANES
    rows = parts * chans * signals
    nstage = len(stages_of(nchunk, signals // 2))
    any_spec = pl.BlockSpec(memory_space=pl.ANY)

    def body(*refs):
        kernel(ntm, nchan, *refs)

    voltages = pl.pallas_call(
        body,
        out_shape=pltpu.VMEM((2, signals, frames, nfine), jnp.bfloat16),
        in_specs=[any_spec] * 4,
        out_specs=any_spec,
        scratch_shapes=[
            pltpu.SMEM(delays.shape, jnp.int32),
            pltpu.VMEM(flags.shape, jnp.int32),
            pltpu.VMEM(taps.shape, jnp.float32),
            pltpu.VMEM((nchunk, parts, chans, sigs, LANES), jnp.bfloat16),
            pltpu.VMEM((2, rows, LANES), jnp.float32),
            pltpu.VMEM((nchunk, nchan, rows, LANES), jnp.bfloat16),
            pltpu.VMEM((nchunk, nchan, rows, LANES), jnp.bfloat16),
            pltpu.VMEM((nchunk, 2, rows, LANES), jnp.bfloat16),
            pltpu.VMEM((2, signals, HALO + frames, nfine), jnp.float32),
            pltpu.VMEM((signals // 2, 2 * nfine, 2 * nfine), jnp.bfloat16),
            pltpu.VMEM((signals // 2, 2 * nfine, 2 * nfine), jnp.bfloat16),
            pltpu.VMEM((2, signals, frames, nfine), jnp.bfloat16),
            pltpu.SemaphoreType.DMA((nchunk,)),
            pltpu.SemaphoreType.DMA((3,)),
            pltpu.SemaphoreType.DMA((nstage,)),
            pltpu.SemaphoreType.DMA((nstage,)),
            pltpu.SemaphoreType.DMA((nchunk,)),
            pltpu.SemaphoreType.DMA((nchunk,)),
            pltpu.SemaphoreType.DMA((2,)),
            pltpu.SemaphoreType.DMA((nstage,)),
        ],
        compiler_params=pltpu.CompilerParams(
            collective_id=0, has_side_effects=True, vmem_limit_bytes=20 * 2**20
        ),
        cost_estimate=pl.CostEstimate(
            flops=8 * 2**27, bytes_accessed=4 * 2**20, transcendentals=0
        ),
        name="resynthesis",
    )(*(pltpu.with_memory_space_constraint(x, pltpu.HBM) for x in (spectra, delays, flags, taps)))
    return voltages


def solution(mesh):
    ntm, nchan = mesh.shape["tm"], mesh.shape["chan"]

    def body(spectra, delays, flags, taps):
        return per_device(ntm, nchan, spectra, delays, flags, taps)

    in_specs = (P(None, "chan", None, "tm"), P(), P(), P())
    return jax.shard_map(
        body, mesh=mesh, in_specs=in_specs, out_specs=P(None, "chan", "tm", None), check_vma=False
    )
```

```python
import math

import jax
import jax.numpy as jnp
from jax import lax
from jax.experimental import pallas as pl
from jax.experimental.pallas import tpu as pltpu
from jax.sharding import PartitionSpec as P

TAPS = 12
LANES = 128
HALO = 16


def fill_tables(chan, delays_ref, flags_ref, hi_ref, lo_ref):
    tiles, rows, cols = hi_ref.shape
    nfine = rows // 2
    row = lax.broadcasted_iota(jnp.int32, (rows, cols), 0)
    col = lax.broadcasted_iota(jnp.int32, (rows, cols), 1)
    fine = (row >> 3) * 4 + (row & 3)
    sample = col & (nfine - 1)
    quarter = (((row >> 2) & 1) - (col >> 7)) * (nfine // 4)
    frow = lax.broadcasted_iota(jnp.int32, (rows, nfine), 0)
    fcol = lax.broadcasted_iota(jnp.int32, (rows, nfine), 1)
    spread = (fcol == (frow >> 3) * 4 + (frow & 3)).astype(jnp.float32).astype(jnp.bfloat16)
    kept = jnp.dot(
        spread,
        flags_ref[...].astype(jnp.float32).astype(jnp.bfloat16),
        preferred_element_type=jnp.float32,
    )

    def one_tile(t, carry):
        tile = chan * tiles + t
        delay = delays_ref[tile]
        turn = (fine * (sample - delay) + quarter) & (nfine - 1)
        fold = nfine // 4 - jnp.abs(turn - nfine // 2)
        x = fold.astype(jnp.float32) * (2.0 * math.pi / nfine)
        x2 = x * x
        poly = -1.0 / 39916800.0
        for c in (1.0 / 362880.0, -1.0 / 5040.0, 1.0 / 120.0, -1.0 / 6.0, 1.0):
            poly = poly * x2 + c
        lane = lax.broadcasted_iota(jnp.int32, kept.shape, 1)
        keep = jnp.sum(jnp.where(lane == tile, kept, 0.0), axis=1, keepdims=True)
        table = (poly * x) * (keep * (-1.0 / math.sqrt(nfine)))
        hi = table.astype(jnp.bfloat16)
        hi_ref[t] = hi
        lo_ref[t] = (table - hi.astype(jnp.float32)).astype(jnp.bfloat16)
        return carry

    lax.fori_loop(0, tiles, one_tile, 0)


def stages_of(nchunk, tiles):
    whole = [(nchunk - 1, 0, tiles)] + [(fc, 0, tiles) for fc in range(nchunk - 2)]
    half = tiles // 2
    return whole + [(nchunk - 2, 0, half)] + [(nchunk - 2, t, t + 1) for t in range(half, tiles)]


def kernel(
    ntm,
    nchan,
    spectra_ref,
    delays_hbm,
    flags_hbm,
    taps_hbm,
    out_ref,
    delays_ref,
    flags_ref,
    taps_ref,
    raw,
    mix,
    send,
    recv,
    passing,
    y,
    hi,
    lo,
    result,
    raw_sem,
    small_sem,
    send_sem,
    recv_sem,
    relay_send_sem,
    relay_recv_sem,
    halo_sem,
    out_sem,
):
    tm = lax.axis_index("tm")
    chan = lax.axis_index("chan")
    nchunk, _, rows, _ = send.shape
    signals = rows // 8
    tiles = signals // 2
    chips = nchan // 2
    chip, core = chan >> 1, chan & 1
    stages = stages_of(nchunk, tiles)
    order = [fc for i, (fc, _, _) in enumerate(stages) if fc not in [s[0] for s in stages[:i]]]

    def around(away):
        return lax.rem(chip + away, chips)

    barrier = pltpu.get_barrier_semaphore()

    def greet(j, carry):
        pl.semaphore_signal(barrier, inc=1, device_id={"chan": lax.rem(chan + j, nchan)})
        return carry

    lax.fori_loop(1, nchan, greet, 0)

    @pl.when(tm > 0)
    def _():
        pl.semaphore_signal(barrier, inc=1, device_id={"tm": tm - 1})

    loads = {}
    for fc in order:
        loads[fc] = pltpu.make_async_copy(
            spectra_ref.at[:, :, :, fc * LANES : (fc + 1) * LANES], raw.at[fc], raw_sem.at[fc]
        )
        loads[fc].start()

    small = [
        pltpu.make_async_copy(whole, mine, small_sem.at[i])
        for i, (whole, mine) in enumerate(
            ((delays_hbm, delays_ref), (flags_hbm, flags_ref), (taps_hbm, taps_ref))
        )
    ]
    for copy in small:
        copy.start()

    def arrange(fc, pair):
        at = pl.ds(pl.multiple_of(pair * 16, 16), 16)
        part = raw[fc, :, :, at, :].astype(jnp.float32)
        for q in range(2):
            for c in range(2):
                for k in range(4):
                    mix[q, pl.ds(c * 4 + k, signals, stride=8), :] = part[c, k, q * 8 : q * 8 + 8, :]
        for q in range(2):
            send[fc, pair * 2 + q] = mix[q].astype(jnp.bfloat16)

    def push(stage, to):
        fc, first, last = stages[stage]
        at = pl.ds(first * 16, (last - first) * 16)
        pltpu.make_async_remote_copy(
            src_ref=send.at[fc, to, at],
            dst_ref=recv.at[fc, chan, at],
            send_sem=send_sem.at[stage],
            recv_sem=recv_sem.at[stage],
            device_id={"chan": to},
        ).start()

    def keep(stage):
        fc, first, last = stages[stage]
        at = pl.ds(first * 16, (last - first) * 16)
        pltpu.make_async_copy(
            send.at[fc, chan, at], recv.at[fc, chan, at], recv_sem.at[stage]
        ).start()

    opposite = around(chips // 2)
    onward = around(jnp.where(core == 0, chips // 4, chips - chips // 4))
    origin = around(jnp.where(core == 0, chips - chips // 4, chips // 4)) * 2 + core

    def relay(fc):
        return pltpu.make_async_remote_copy(
            src_ref=send.at[fc, pl.ds(opposite * 2, 2)],
            dst_ref=passing.at[fc],
            send_sem=relay_send_sem.at[fc],
            recv_sem=relay_recv_sem.at[fc],
            device_id={"chan": onward * 2 + core},
        )

    def forward(stage):
        fc, first, last = stages[stage]
        at = pl.ds(first * 16, (last - first) * 16)
        for q in range(2):
            pltpu.make_async_remote_copy(
                src_ref=passing.at[fc, q, at],
                dst_ref=recv.at[fc, origin, at],
                send_sem=send_sem.at[stage],
                recv_sem=recv_sem.at[stage],
                device_id={"chan": onward * 2 + q},
            ).start()

    def each_chip(work):
        def body(i, carry):
            pick = i >> 1
            far = jnp.where((pick & 1) == 0, chips // 2 - 1 - (pick >> 1), (pick + 1) >> 1)
            work(around(jnp.where((i & 1) == 0, far, chips - far)))
            return carry

        lax.fori_loop(0, chips - 2, body, 0)

    def issue(stage):
        fc, first, last = stages[stage]
        fresh = first == 0

        def to_chip(pair):
            if fresh:
                arrange(fc, pair)
            push(stage, pair * 2 + core)
            push(stage, pair * 2 + 1 - core)

        if fresh:
            loads[fc].wait()
            arrange(fc, opposite)
            if stage == 0:
                pl.semaphore_wait(barrier, nchan - 1 + jnp.where(tm < ntm - 1, 1, 0))
            relay(fc).start()
        each_chip(to_chip)
        if fresh:
            arrange(fc, chip)
            relay(fc).wait_recv()
        forward(stage)
        push(stage, chip * 2 + 1 - core)
        keep(stage)

    def left(stage):
        fc, first, last = stages[stage]
        sent = send.at[fc, 0 : nchan - 1, first * 16 : last * 16]
        pltpu.make_async_copy(sent, sent, send_sem.at[stage]).wait()

    issue(0)
    issue(1)
    for copy in small:
        copy.wait()
    fill_tables(chan, delays_ref, flags_ref, hi, lo)

    @pl.when(tm == 0)
    def _():
        y[:, :, 0:HALO, :] = jnp.zeros((2, signals, HALO, LANES), jnp.float32)

    def transform(stage):
        fc, first, last = stages[stage]
        base = HALO + fc * LANES

        def one_tile(t, carry):
            part = recv[fc, :, pl.ds(pl.multiple_of(t * 16, 16), 16), :].astype(jnp.float32)
            pols = [part[:, p * 8 : p * 8 + 8, :].reshape(nchan * 8, LANES) for p in range(2)]
            x = jnp.concatenate(pols, axis=1).astype(jnp.bfloat16)
            dims = (((0,), (0,)), ((), ()))
            z = lax.dot_general(x, hi[t], dims, preferred_element_type=jnp.float32)
            z += lax.dot_general(x, lo[t], dims, preferred_element_type=jnp.float32)
            for p in range(2):
                of = slice(p * LANES, (p + 1) * LANES)
                y[0, t * 2 + p, base : base + LANES, :] = z[of, :LANES]
                y[1, t * 2 + p, base : base + LANES, :] = z[of, LANES:]
            return carry

        lax.fori_loop(first, last, one_tile, 0)

    def fir(stage, begin, end):
        _, first, last = stages[stage]
        sigs = 2 * (last - first)

        def one(i, carry):
            d, s = i // sigs, 2 * first + lax.rem(i, sigs)
            for row in range(begin, end, 64):
                count = min(64, end - row)
                total = None
                for j in range(TAPS):
                    start = HALO + row - j
                    term = taps_ref[j : j + 1, :] * y[d, s, start : start + count, :]
                    total = term if total is None else total + term
                result[d, s, row : row + count, :] = total.astype(jnp.bfloat16)
            return carry

        lax.fori_loop(0, 2 * sigs, one, 0)

    frames = nchunk * LANES
    halo = pltpu.make_async_remote_copy(
        src_ref=y.at[:, :, frames : frames + HALO, :],
        dst_ref=y.at[:, :, 0:HALO, :],
        send_sem=halo_sem.at[0],
        recv_sem=halo_sem.at[1],
        device_id={"tm": lax.rem(tm + 1, ntm)},
    )

    stores = []
    for stage, (fc, first, last) in enumerate(stages):
        if stage + 2 < len(stages):
            left(stage)
            issue(stage + 2)
        arriving = recv.at[fc, :, first * 16 : last * 16]
        pltpu.make_async_copy(arriving, arriving, recv_sem.at[stage]).wait()
        transform(stage)
        if stage == 0:

            @pl.when(tm < ntm - 1)
            def _():
                halo.start()

        if fc == 0:

            @pl.when(tm > 0)
            def _():
                halo.wait_recv()

        begin = fc * LANES + (HALO if stage == 0 else 0)
        end = (fc + 1) * LANES + (HALO if fc == nchunk - 2 else 0)
        fir(stage, begin, end)
        at = (slice(None), slice(2 * first, 2 * last), slice(begin, end))
        stores.append(pltpu.make_async_copy(result.at[at], out_ref.at[at], out_sem.at[stage]))
        stores[-1].start()

    for stage in range(len(stages) - 2, len(stages)):
        left(stage)
    for fc in order:
        relay(fc).wait_send()

    @pl.when(tm < ntm - 1)
    def _():
        halo.wait_send()

    for copy in stores:
        copy.wait()


def per_device(ntm, nchan, spectra, delays, flags, taps):
    parts, chans, sigs, frames = spectra.shape
    signals = sigs // nchan
    nfine = chans * nchan
    nchunk = frames // LANES
    rows = parts * chans * signals
    nstage = len(stages_of(nchunk, signals // 2))
    any_spec = pl.BlockSpec(memory_space=pl.ANY)

    def body(*refs):
        kernel(ntm, nchan, *refs)

    voltages = pl.pallas_call(
        body,
        out_shape=pltpu.VMEM((2, signals, frames, nfine), jnp.bfloat16),
        in_specs=[any_spec] * 4,
        out_specs=any_spec,
        scratch_shapes=[
            pltpu.SMEM(delays.shape, jnp.int32),
            pltpu.VMEM(flags.shape, jnp.int32),
            pltpu.VMEM(taps.shape, jnp.float32),
            pltpu.VMEM((nchunk, parts, chans, sigs, LANES), jnp.bfloat16),
            pltpu.VMEM((2, rows, LANES), jnp.float32),
            pltpu.VMEM((nchunk, nchan, rows, LANES), jnp.bfloat16),
            pltpu.VMEM((nchunk, nchan, rows, LANES), jnp.bfloat16),
            pltpu.VMEM((nchunk, 2, rows, LANES), jnp.bfloat16),
            pltpu.VMEM((2, signals, HALO + frames, nfine), jnp.float32),
            pltpu.VMEM((signals // 2, 2 * nfine, 2 * nfine), jnp.bfloat16),
            pltpu.VMEM((signals // 2, 2 * nfine, 2 * nfine), jnp.bfloat16),
            pltpu.VMEM((2, signals, frames, nfine), jnp.bfloat16),
            pltpu.SemaphoreType.DMA((nchunk,)),
            pltpu.SemaphoreType.DMA((3,)),
            pltpu.SemaphoreType.DMA((nstage,)),
            pltpu.SemaphoreType.DMA((nstage,)),
            pltpu.SemaphoreType.DMA((nchunk,)),
            pltpu.SemaphoreType.DMA((nchunk,)),
            pltpu.SemaphoreType.DMA((2,)),
            pltpu.SemaphoreType.DMA((nstage,)),
        ],
        compiler_params=pltpu.CompilerParams(
            collective_id=0, has_side_effects=True, vmem_limit_bytes=20 * 2**20
        ),
        cost_estimate=pl.CostEstimate(
            flops=8 * 2**27, bytes_accessed=4 * 2**20, transcendentals=0
        ),
        name="resynthesis",
    )(*(pltpu.with_memory_space_constraint(x, pltpu.HBM) for x in (spectra, delays, flags, taps)))
    return voltages


def solution(mesh):
    ntm, nchan = mesh.shape["tm"], mesh.shape["chan"]

    def body(spectra, delays, flags, taps):
        return per_device(ntm, nchan, spectra, delays, flags, taps)

    in_specs = (P(None, "chan", None, "tm"), P(), P(), P())
    return jax.shard_map(
        body, mesh=mesh, in_specs=in_specs, out_specs=P(None, "chan", "tm", None), check_vma=False
    )
```

```python
import math

import jax
import jax.numpy as jnp
from jax import lax
from jax.experimental import pallas as pl
from jax.experimental.pallas import tpu as pltpu
from jax.sharding import PartitionSpec as P

TAPS = 12
LANES = 128
HALO = 16


def fill_tables(chan, delays_ref, flags_ref, hi_ref, lo_ref):
    tiles, rows, cols = hi_ref.shape
    nfine = rows // 2
    row = lax.broadcasted_iota(jnp.int32, (rows, cols), 0)
    col = lax.broadcasted_iota(jnp.int32, (rows, cols), 1)
    fine = (row >> 3) * 4 + (row & 3)
    sample = col & (nfine - 1)
    quarter = (((row >> 2) & 1) - (col >> 7)) * (nfine // 4)
    frow = lax.broadcasted_iota(jnp.int32, (rows, nfine), 0)
    fcol = lax.broadcasted_iota(jnp.int32, (rows, nfine), 1)
    spread = (fcol == (frow >> 3) * 4 + (frow & 3)).astype(jnp.float32).astype(jnp.bfloat16)
    kept = jnp.dot(
        spread,
        flags_ref[...].astype(jnp.float32).astype(jnp.bfloat16),
        preferred_element_type=jnp.float32,
    )

    def one_tile(t, carry):
        tile = chan * tiles + t
        delay = delays_ref[tile]
        turn = (fine * (sample - delay) + quarter) & (nfine - 1)
        fold = nfine // 4 - jnp.abs(turn - nfine // 2)
        x = fold.astype(jnp.float32) * (2.0 * math.pi / nfine)
        x2 = x * x
        poly = -1.0 / 39916800.0
        for c in (1.0 / 362880.0, -1.0 / 5040.0, 1.0 / 120.0, -1.0 / 6.0, 1.0):
            poly = poly * x2 + c
        lane = lax.broadcasted_iota(jnp.int32, kept.shape, 1)
        keep = jnp.sum(jnp.where(lane == tile, kept, 0.0), axis=1, keepdims=True)
        table = (poly * x) * (keep * (-1.0 / math.sqrt(nfine)))
        hi = table.astype(jnp.bfloat16)
        hi_ref[t] = hi
        lo_ref[t] = (table - hi.astype(jnp.float32)).astype(jnp.bfloat16)
        return carry

    lax.fori_loop(0, tiles, one_tile, 0)


def stages_of(nchunk, tiles):
    whole = [(nchunk - 1, 0, tiles)] + [(fc, 0, tiles) for fc in range(nchunk - 2)]
    half = tiles // 2
    return whole + [(nchunk - 2, 0, half)] + [(nchunk - 2, t, t + 1) for t in range(half, tiles)]


def kernel(
    ntm,
    nchan,
    spectra_ref,
    delays_hbm,
    flags_hbm,
    taps_hbm,
    out_ref,
    delays_ref,
    flags_ref,
    taps_ref,
    raw,
    mix,
    send,
    recv,
    y,
    hi,
    lo,
    result,
    raw_sem,
    small_sem,
    send_sem,
    recv_sem,
    halo_sem,
    out_sem,
):
    tm = lax.axis_index("tm")
    chan = lax.axis_index("chan")
    nchunk, _, rows, _ = send.shape
    signals = rows // 8
    tiles = signals // 2
    chips = nchan // 2
    chip, core = chan >> 1, chan & 1
    stages = stages_of(nchunk, tiles)
    order = [fc for i, (fc, _, _) in enumerate(stages) if fc not in [s[0] for s in stages[:i]]]

    def around(away):
        return lax.rem(chip + away, chips)

    barrier = pltpu.get_barrier_semaphore()

    def greet(j, carry):
        pl.semaphore_signal(barrier, inc=1, device_id={"chan": lax.rem(chan + j, nchan)})
        return carry

    lax.fori_loop(1, nchan, greet, 0)

    @pl.when(tm > 0)
    def _():
        pl.semaphore_signal(barrier, inc=1, device_id={"tm": tm - 1})

    loads = {}
    for fc in order:
        loads[fc] = pltpu.make_async_copy(
            spectra_ref.at[:, :, :, fc * LANES : (fc + 1) * LANES], raw.at[fc], raw_sem.at[fc]
        )
        loads[fc].start()

    small = [
        pltpu.make_async_copy(whole, mine, small_sem.at[i])
        for i, (whole, mine) in enumerate(
            ((delays_hbm, delays_ref), (flags_hbm, flags_ref), (taps_hbm, taps_ref))
        )
    ]
    for copy in small:
        copy.start()

    def arrange(fc, pair):
        at = pl.ds(pl.multiple_of(pair * 16, 16), 16)
        part = raw[fc, :, :, at, :].astype(jnp.float32)
        for q in range(2):
            for c in range(2):
                for k in range(4):
                    mix[q, pl.ds(c * 4 + k, signals, stride=8), :] = part[c, k, q * 8 : q * 8 + 8, :]
        for q in range(2):
            send[fc, pair * 2 + q] = mix[q].astype(jnp.bfloat16)

    def push(stage, to):
        fc, first, last = stages[stage]
        at = pl.ds(first * 16, (last - first) * 16)
        pltpu.make_async_remote_copy(
            src_ref=send.at[fc, to, at],
            dst_ref=recv.at[fc, chan, at],
            send_sem=send_sem.at[stage],
            recv_sem=recv_sem.at[stage],
            device_id={"chan": to},
        ).start()

    def keep(stage):
        fc, first, last = stages[stage]
        at = pl.ds(first * 16, (last - first) * 16)
        pltpu.make_async_copy(
            send.at[fc, chan, at], recv.at[fc, chan, at], recv_sem.at[stage]
        ).start()

    def each_chip(work):
        def body(i, carry):
            far = chips // 2 - ((i + 1) >> 1)
            work(around(jnp.where((i & 1) == 0, far, chips - far)))
            return carry

        lax.fori_loop(0, chips - 1, body, 0)

    def issue(stage):
        fc, first, last = stages[stage]
        fresh = first == 0

        def to_chip(pair):
            if fresh:
                arrange(fc, pair)
            push(stage, pair * 2 + core)
            push(stage, pair * 2 + 1 - core)

        if fresh:
            loads[fc].wait()
        if stage == 0:
            pl.semaphore_wait(barrier, nchan - 1 + jnp.where(tm < ntm - 1, 1, 0))
        each_chip(to_chip)
        if fresh:
            arrange(fc, chip)
        push(stage, chip * 2 + 1 - core)
        keep(stage)

    def left(stage):
        fc, first, last = stages[stage]
        sent = send.at[fc, 0 : nchan - 1, first * 16 : last * 16]
        pltpu.make_async_copy(sent, sent, send_sem.at[stage]).wait()

    issue(0)
    issue(1)
    for copy in small:
        copy.wait()
    fill_tables(chan, delays_ref, flags_ref, hi, lo)

    @pl.when(tm == 0)
    def _():
        y[:, :, 0:HALO, :] = jnp.zeros((2, signals, HALO, LANES), jnp.float32)

    def transform(stage):
        fc, first, last = stages[stage]
        base = HALO + fc * LANES

        def one_tile(t, carry):
            part = recv[fc, :, pl.ds(pl.multiple_of(t * 16, 16), 16), :].astype(jnp.float32)
            pols = [part[:, p * 8 : p * 8 + 8, :].reshape(nchan * 8, LANES) for p in range(2)]
            x = jnp.concatenate(pols, axis=1).astype(jnp.bfloat16)
            dims = (((0,), (0,)), ((), ()))
            z = lax.dot_general(x, hi[t], dims, preferred_element_type=jnp.float32)
            z += lax.dot_general(x, lo[t], dims, preferred_element_type=jnp.float32)
            for p in range(2):
                of = slice(p * LANES, (p + 1) * LANES)
                y[0, t * 2 + p, base : base + LANES, :] = z[of, :LANES]
                y[1, t * 2 + p, base : base + LANES, :] = z[of, LANES:]
            return carry

        lax.fori_loop(first, last, one_tile, 0)

    def fir(stage, begin, end):
        _, first, last = stages[stage]
        sigs = 2 * (last - first)

        def one(i, carry):
            d, s = i // sigs, 2 * first + lax.rem(i, sigs)
            for row in range(begin, end, 64):
                count = min(64, end - row)
                total = None
                for j in range(TAPS):
                    start = HALO + row - j
                    term = taps_ref[j : j + 1, :] * y[d, s, start : start + count, :]
                    total = term if total is None else total + term
                result[d, s, row : row + count, :] = total.astype(jnp.bfloat16)
            return carry

        lax.fori_loop(0, 2 * sigs, one, 0)

    frames = nchunk * LANES
    halo = pltpu.make_async_remote_copy(
        src_ref=y.at[:, :, frames : frames + HALO, :],
        dst_ref=y.at[:, :, 0:HALO, :],
        send_sem=halo_sem.at[0],
        recv_sem=halo_sem.at[1],
        device_id={"tm": lax.rem(tm + 1, ntm)},
    )

    stores = []
    for stage, (fc, first, last) in enumerate(stages):
        if stage + 2 < len(stages):
            left(stage)
            issue(stage + 2)
        arriving = recv.at[fc, :, first * 16 : last * 16]
        pltpu.make_async_copy(arriving, arriving, recv_sem.at[stage]).wait()
        transform(stage)
        if stage == 0:

            @pl.when(tm < ntm - 1)
            def _():
                halo.start()

        if fc == 0:

            @pl.when(tm > 0)
            def _():
                halo.wait_recv()

        begin = fc * LANES + (HALO if stage == 0 else 0)
        end = (fc + 1) * LANES + (HALO if fc == nchunk - 2 else 0)
        fir(stage, begin, end)
        at = (slice(None), slice(2 * first, 2 * last), slice(begin, end))
        stores.append(pltpu.make_async_copy(result.at[at], out_ref.at[at], out_sem.at[stage]))
        stores[-1].start()

    for stage in range(len(stages) - 2, len(stages)):
        left(stage)

    @pl.when(tm < ntm - 1)
    def _():
        halo.wait_send()

    for copy in stores:
        copy.wait()


def per_device(ntm, nchan, spectra, delays, flags, taps):
    parts, chans, sigs, frames = spectra.shape
    signals = sigs // nchan
    nfine = chans * nchan
    nchunk = frames // LANES
    rows = parts * chans * signals
    nstage = len(stages_of(nchunk, signals // 2))
    any_spec = pl.BlockSpec(memory_space=pl.ANY)

    def body(*refs):
        kernel(ntm, nchan, *refs)

    voltages = pl.pallas_call(
        body,
        out_shape=pltpu.VMEM((2, signals, frames, nfine), jnp.bfloat16),
        in_specs=[any_spec] * 4,
        out_specs=any_spec,
        scratch_shapes=[
            pltpu.SMEM(delays.shape, jnp.int32),
            pltpu.VMEM(flags.shape, jnp.int32),
            pltpu.VMEM(taps.shape, jnp.float32),
            pltpu.VMEM((nchunk, parts, chans, sigs, LANES), jnp.bfloat16),
            pltpu.VMEM((2, rows, LANES), jnp.float32),
            pltpu.VMEM((nchunk, nchan, rows, LANES), jnp.bfloat16),
            pltpu.VMEM((nchunk, nchan, rows, LANES), jnp.bfloat16),
            pltpu.VMEM((2, signals, HALO + frames, nfine), jnp.float32),
            pltpu.VMEM((signals // 2, 2 * nfine, 2 * nfine), jnp.bfloat16),
            pltpu.VMEM((signals // 2, 2 * nfine, 2 * nfine), jnp.bfloat16),
            pltpu.VMEM((2, signals, frames, nfine), jnp.bfloat16),
            pltpu.SemaphoreType.DMA((nchunk,)),
            pltpu.SemaphoreType.DMA((3,)),
            pltpu.SemaphoreType.DMA((nstage,)),
            pltpu.SemaphoreType.DMA((nstage,)),
            pltpu.SemaphoreType.DMA((2,)),
            pltpu.SemaphoreType.DMA((nstage,)),
        ],
        compiler_params=pltpu.CompilerParams(
            collective_id=0, has_side_effects=True, vmem_limit_bytes=20 * 2**20
        ),
        cost_estimate=pl.CostEstimate(
            flops=8 * 2**27, bytes_accessed=4 * 2**20, transcendentals=0
        ),
        name="resynthesis",
    )(*(pltpu.with_memory_space_constraint(x, pltpu.HBM) for x in (spectra, delays, flags, taps)))
    return voltages


def solution(mesh):
    ntm, nchan = mesh.shape["tm"], mesh.shape["chan"]

    def body(spectra, delays, flags, taps):
        return per_device(ntm, nchan, spectra, delays, flags, taps)

    in_specs = (P(None, "chan", None, "tm"), P(), P(), P())
    return jax.shard_map(
        body, mesh=mesh, in_specs=in_specs, out_specs=P(None, "chan", "tm", None), check_vma=False
    )
```

```python
import math

import jax
import jax.numpy as jnp
from jax import lax
from jax.experimental import pallas as pl
from jax.experimental.pallas import tpu as pltpu
from jax.sharding import PartitionSpec as P

TAPS = 12
LANES = 128
HALO = 16


def fill_tables(chan, delays_ref, flags_ref, hi_ref, lo_ref):
    tiles, rows, cols = hi_ref.shape
    nfine = rows // 2
    row = lax.broadcasted_iota(jnp.int32, (rows, cols), 0)
    col = lax.broadcasted_iota(jnp.int32, (rows, cols), 1)
    fine = (row >> 3) * 4 + (row & 3)
    sample = col & (nfine - 1)
    quarter = (((row >> 2) & 1) - (col >> 7)) * (nfine // 4)
    frow = lax.broadcasted_iota(jnp.int32, (rows, nfine), 0)
    fcol = lax.broadcasted_iota(jnp.int32, (rows, nfine), 1)
    spread = (fcol == (frow >> 3) * 4 + (frow & 3)).astype(jnp.float32).astype(jnp.bfloat16)
    kept = jnp.dot(
        spread,
        flags_ref[...].astype(jnp.float32).astype(jnp.bfloat16),
        preferred_element_type=jnp.float32,
    )

    def one_tile(t, carry):
        tile = chan * tiles + t
        delay = delays_ref[tile]
        turn = (fine * (sample - delay) + quarter) & (nfine - 1)
        fold = nfine // 4 - jnp.abs(turn - nfine // 2)
        x = fold.astype(jnp.float32) * (2.0 * math.pi / nfine)
        x2 = x * x
        poly = -1.0 / 39916800.0
        for c in (1.0 / 362880.0, -1.0 / 5040.0, 1.0 / 120.0, -1.0 / 6.0, 1.0):
            poly = poly * x2 + c
        lane = lax.broadcasted_iota(jnp.int32, kept.shape, 1)
        keep = jnp.sum(jnp.where(lane == tile, kept, 0.0), axis=1, keepdims=True)
        table = (poly * x) * (keep * (-1.0 / math.sqrt(nfine)))
        hi = table.astype(jnp.bfloat16)
        hi_ref[t] = hi
        lo_ref[t] = (table - hi.astype(jnp.float32)).astype(jnp.bfloat16)
        return carry

    lax.fori_loop(0, tiles, one_tile, 0)


def stages_of(nchunk, tiles):
    whole = [(nchunk - 1, 0, tiles)] + [(fc, 0, tiles) for fc in range(nchunk - 2)]
    half = tiles // 2
    return whole + [(nchunk - 2, 0, half)] + [(nchunk - 2, t, t + 1) for t in range(half, tiles)]


def kernel(
    ntm,
    nchan,
    spectra_ref,
    delays_hbm,
    flags_hbm,
    taps_hbm,
    out_ref,
    delays_ref,
    flags_ref,
    taps_ref,
    raw,
    mix,
    send,
    recv,
    y,
    hi,
    lo,
    result,
    raw_sem,
    small_sem,
    send_sem,
    recv_sem,
    halo_sem,
    out_sem,
    from_below,
    from_above,
):
    tm = lax.axis_index("tm")
    chan = lax.axis_index("chan")
    nchunk, _, rows, _ = send.shape
    signals = rows // 8
    tiles = signals // 2
    chips = nchan // 2
    chip, core = chan >> 1, chan & 1
    stages = stages_of(nchunk, tiles)
    order = [fc for i, (fc, _, _) in enumerate(stages) if fc not in [s[0] for s in stages[:i]]]

    def around(away):
        return lax.rem(chip + away, chips)

    loads = {
        fc: pltpu.make_async_copy(
            spectra_ref.at[:, :, :, fc * LANES : (fc + 1) * LANES], raw.at[fc], raw_sem.at[fc]
        )
        for fc in order
    }
    loads[order[0]].start()
    barrier = pltpu.get_barrier_semaphore()

    for near in (
        chip * 2 + 1 - core,
        around(1) * 2,
        around(1) * 2 + 1,
        around(chips - 1) * 2,
        around(chips - 1) * 2 + 1,
    ):
        pl.semaphore_signal(barrier, inc=1, device_id={"chan": near})

    @pl.when(tm > 0)
    def _():
        pl.semaphore_signal(barrier, inc=1, device_id={"tm": tm - 1})

    for fc in order[1:]:
        loads[fc].start()

    small = [
        pltpu.make_async_copy(whole, mine, small_sem.at[i])
        for i, (whole, mine) in enumerate(
            ((delays_hbm, delays_ref), (flags_hbm, flags_ref), (taps_hbm, taps_ref))
        )
    ]
    for copy in small:
        copy.start()

    def arrange(fc, pair):
        at = pl.ds(pl.multiple_of(pair * 16, 16), 16)
        part = raw[fc, :, :, at, :].astype(jnp.float32)
        for q in range(2):
            for c in range(2):
                for k in range(4):
                    mix[q, pl.ds(c * 4 + k, signals, stride=8), :] = part[c, k, q * 8 : q * 8 + 8, :]
        for q in range(2):
            send[fc, pair * 2 + q] = mix[q].astype(jnp.bfloat16)

    def push(stage, to):
        fc, first, last = stages[stage]
        at = pl.ds(first * 16, (last - first) * 16)
        pltpu.make_async_remote_copy(
            src_ref=send.at[fc, to, at],
            dst_ref=recv.at[fc, chan, at],
            send_sem=send_sem.at[stage],
            recv_sem=recv_sem.at[stage],
            device_id={"chan": to},
        ).start()

    def keep(stage):
        fc, first, last = stages[stage]
        at = pl.ds(first * 16, (last - first) * 16)
        pltpu.make_async_copy(
            send.at[fc, chan, at], recv.at[fc, chan, at], recv_sem.at[stage]
        ).start()

    def each_chip(work):
        def body(i, carry):
            far = chips // 2 - ((i + 1) >> 1)
            work(around(jnp.where((i & 1) == 0, far, chips - far)))
            return carry

        lax.fori_loop(0, chips - 1, body, 0)

    def as_known(work):
        up, down = around(1) * 2 + core, around(chips - 1) * 2 + core
        last = chips // 2

        def tell_up(d):
            pl.semaphore_signal(from_below.at[d], inc=1, device_id={"chan": up})

        def tell_down(d):
            pl.semaphore_signal(from_above.at[d], inc=1, device_id={"chan": down})

        pl.semaphore_wait(barrier, 5 + jnp.where(tm < ntm - 1, 1, 0))
        tell_up(2)
        tell_down(2)
        work(around(1))
        work(around(chips - 1))

        def body(d, carry):
            pl.semaphore_wait(from_below.at[d], 1)
            tell_up(d + 1)
            pl.semaphore_wait(from_above.at[d], 1)

            @pl.when(d < last - 1)
            def _():
                tell_down(d + 1)

            work(around(d))
            work(around(chips - d))
            return carry

        lax.fori_loop(2, last, body, 0)
        pl.semaphore_wait(from_below.at[last], 1)
        work(around(last))

    def issue(stage):
        fc, first, last = stages[stage]
        fresh = first == 0

        def to_chip(pair):
            if fresh:
                arrange(fc, pair)
            push(stage, pair * 2 + core)
            push(stage, pair * 2 + 1 - core)

        if fresh:
            loads[fc].wait()
        if stage == 0:
            as_known(to_chip)
        else:
            each_chip(to_chip)
        if fresh:
            arrange(fc, chip)
        push(stage, chip * 2 + 1 - core)
        keep(stage)

    def left(stage):
        fc, first, last = stages[stage]
        sent = send.at[fc, 0 : nchan - 1, first * 16 : last * 16]
        pltpu.make_async_copy(sent, sent, send_sem.at[stage]).wait()

    issue(0)
    issue(1)
    for copy in small:
        copy.wait()
    fill_tables(chan, delays_ref, flags_ref, hi, lo)

    @pl.when(tm == 0)
    def _():
        y[:, :, 0:HALO, :] = jnp.zeros((2, signals, HALO, LANES), jnp.float32)

    def transform(stage):
        fc, first, last = stages[stage]
        base = HALO + fc * LANES

        def one_tile(t, carry):
            part = recv[fc, :, pl.ds(pl.multiple_of(t * 16, 16), 16), :].astype(jnp.float32)
            pols = [part[:, p * 8 : p * 8 + 8, :].reshape(nchan * 8, LANES) for p in range(2)]
            x = jnp.concatenate(pols, axis=1).astype(jnp.bfloat16)
            dims = (((0,), (0,)), ((), ()))
            z = lax.dot_general(x, hi[t], dims, preferred_element_type=jnp.float32)
            z += lax.dot_general(x, lo[t], dims, preferred_element_type=jnp.float32)
            for p in range(2):
                of = slice(p * LANES, (p + 1) * LANES)
                y[0, t * 2 + p, base : base + LANES, :] = z[of, :LANES]
                y[1, t * 2 + p, base : base + LANES, :] = z[of, LANES:]
            return carry

        lax.fori_loop(first, last, one_tile, 0)

    def fir(stage, begin, end):
        _, first, last = stages[stage]
        sigs = 2 * (last - first)

        def one(i, carry):
            d, s = i // sigs, 2 * first + lax.rem(i, sigs)
            for row in range(begin, end, 64):
                count = min(64, end - row)
                total = None
                for j in range(TAPS):
                    start = HALO + row - j
                    term = taps_ref[j : j + 1, :] * y[d, s, start : start + count, :]
                    total = term if total is None else total + term
                result[d, s, row : row + count, :] = total.astype(jnp.bfloat16)
            return carry

        lax.fori_loop(0, 2 * sigs, one, 0)

    frames = nchunk * LANES
    halo = pltpu.make_async_remote_copy(
        src_ref=y.at[:, :, frames : frames + HALO, :],
        dst_ref=y.at[:, :, 0:HALO, :],
        send_sem=halo_sem.at[0],
        recv_sem=halo_sem.at[1],
        device_id={"tm": lax.rem(tm + 1, ntm)},
    )

    stores = []
    for stage, (fc, first, last) in enumerate(stages):
        if stage + 2 < len(stages):
            left(stage)
            issue(stage + 2)
        arriving = recv.at[fc, :, first * 16 : last * 16]
        pltpu.make_async_copy(arriving, arriving, recv_sem.at[stage]).wait()
        transform(stage)
        if stage == 0:

            @pl.when(tm < ntm - 1)
            def _():
                halo.start()

        if fc == 0:

            @pl.when(tm > 0)
            def _():
                halo.wait_recv()

        begin = fc * LANES + (HALO if stage == 0 else 0)
        end = (fc + 1) * LANES + (HALO if fc == nchunk - 2 else 0)
        fir(stage, begin, end)
        at = (slice(None), slice(2 * first, 2 * last), slice(begin, end))
        stores.append(pltpu.make_async_copy(result.at[at], out_ref.at[at], out_sem.at[stage]))
        stores[-1].start()

    for stage in range(len(stages) - 2, len(stages)):
        left(stage)

    @pl.when(tm < ntm - 1)
    def _():
        halo.wait_send()

    for copy in stores:
        copy.wait()


def per_device(ntm, nchan, spectra, delays, flags, taps):
    parts, chans, sigs, frames = spectra.shape
    signals = sigs // nchan
    nfine = chans * nchan
    nchunk = frames // LANES
    rows = parts * chans * signals
    nstage = len(stages_of(nchunk, signals // 2))
    any_spec = pl.BlockSpec(memory_space=pl.ANY)

    def body(*refs):
        kernel(ntm, nchan, *refs)

    voltages = pl.pallas_call(
        body,
        out_shape=pltpu.VMEM((2, signals, frames, nfine), jnp.bfloat16),
        in_specs=[any_spec] * 4,
        out_specs=any_spec,
        scratch_shapes=[
            pltpu.SMEM(delays.shape, jnp.int32),
            pltpu.VMEM(flags.shape, jnp.int32),
            pltpu.VMEM(taps.shape, jnp.float32),
            pltpu.VMEM((nchunk, parts, chans, sigs, LANES), jnp.bfloat16),
            pltpu.VMEM((2, rows, LANES), jnp.float32),
            pltpu.VMEM((nchunk, nchan, rows, LANES), jnp.bfloat16),
            pltpu.VMEM((nchunk, nchan, rows, LANES), jnp.bfloat16),
            pltpu.VMEM((2, signals, HALO + frames, nfine), jnp.float32),
            pltpu.VMEM((signals // 2, 2 * nfine, 2 * nfine), jnp.bfloat16),
            pltpu.VMEM((signals // 2, 2 * nfine, 2 * nfine), jnp.bfloat16),
            pltpu.VMEM((2, signals, frames, nfine), jnp.bfloat16),
            pltpu.SemaphoreType.DMA((nchunk,)),
            pltpu.SemaphoreType.DMA((3,)),
            pltpu.SemaphoreType.DMA((nstage,)),
            pltpu.SemaphoreType.DMA((nstage,)),
            pltpu.SemaphoreType.DMA((2,)),
            pltpu.SemaphoreType.DMA((nstage,)),
            pltpu.SemaphoreType.REGULAR((nchan // 4 + 1,)),
            pltpu.SemaphoreType.REGULAR((nchan // 4 + 1,)),
        ],
        compiler_params=pltpu.CompilerParams(
            collective_id=0, has_side_effects=True, vmem_limit_bytes=20 * 2**20
        ),
        cost_estimate=pl.CostEstimate(
            flops=8 * 2**27, bytes_accessed=4 * 2**20, transcendentals=0
        ),
        name="resynthesis",
    )(*(pltpu.with_memory_space_constraint(x, pltpu.HBM) for x in (spectra, delays, flags, taps)))
    return voltages


def solution(mesh):
    ntm, nchan = mesh.shape["tm"], mesh.shape["chan"]

    def body(spectra, delays, flags, taps):
        return per_device(ntm, nchan, spectra, delays, flags, taps)

    in_specs = (P(None, "chan", None, "tm"), P(), P(), P())
    return jax.shard_map(
        body, mesh=mesh, in_specs=in_specs, out_specs=P(None, "chan", "tm", None), check_vma=False
    )
```

```python
import math

import jax
import jax.numpy as jnp
from jax import lax
from jax.experimental import pallas as pl
from jax.experimental.pallas import tpu as pltpu
from jax.sharding import PartitionSpec as P

TAPS = 12
LANES = 128
HALO = 16


def fill_tables(chan, delays_ref, flags_ref, hi_ref, lo_ref):
    tiles, rows, cols = hi_ref.shape
    nfine = rows // 2
    row = lax.broadcasted_iota(jnp.int32, (rows, cols), 0)
    col = lax.broadcasted_iota(jnp.int32, (rows, cols), 1)
    fine = (row >> 3) * 4 + (row & 3)
    sample = col & (nfine - 1)
    quarter = (((row >> 2) & 1) - (col >> 7)) * (nfine // 4)
    frow = lax.broadcasted_iota(jnp.int32, (rows, nfine), 0)
    fcol = lax.broadcasted_iota(jnp.int32, (rows, nfine), 1)
    spread = (fcol == (frow >> 3) * 4 + (frow & 3)).astype(jnp.float32).astype(jnp.bfloat16)
    kept = jnp.dot(
        spread,
        flags_ref[...].astype(jnp.float32).astype(jnp.bfloat16),
        preferred_element_type=jnp.float32,
    )

    def one_tile(t, carry):
        tile = chan * tiles + t
        delay = delays_ref[tile]
        turn = (fine * (sample - delay) + quarter) & (nfine - 1)
        fold = nfine // 4 - jnp.abs(turn - nfine // 2)
        x = fold.astype(jnp.float32) * (2.0 * math.pi / nfine)
        x2 = x * x
        poly = -1.0 / 39916800.0
        for c in (1.0 / 362880.0, -1.0 / 5040.0, 1.0 / 120.0, -1.0 / 6.0, 1.0):
            poly = poly * x2 + c
        lane = lax.broadcasted_iota(jnp.int32, kept.shape, 1)
        keep = jnp.sum(jnp.where(lane == tile, kept, 0.0), axis=1, keepdims=True)
        table = (poly * x) * (keep * (-1.0 / math.sqrt(nfine)))
        hi = table.astype(jnp.bfloat16)
        hi_ref[t] = hi
        lo_ref[t] = (table - hi.astype(jnp.float32)).astype(jnp.bfloat16)
        return carry

    lax.fori_loop(0, tiles, one_tile, 0)


def stages_of(nchunk, tiles):
    whole = [(nchunk - 1, 0, tiles)] + [(fc, 0, tiles) for fc in range(nchunk - 2)]
    half = tiles // 2
    return whole + [(nchunk - 2, 0, half)] + [(nchunk - 2, t, t + 1) for t in range(half, tiles)]


def kernel(
    ntm,
    nchan,
    spectra_ref,
    delays_hbm,
    flags_hbm,
    taps_hbm,
    out_ref,
    delays_ref,
    flags_ref,
    taps_ref,
    raw,
    mix,
    send,
    recv,
    y,
    hi,
    lo,
    raw_sem,
    small_sem,
    send_sem,
    recv_sem,
    halo_sem,
    from_below,
    from_above,
):
    tm = lax.axis_index("tm")
    chan = lax.axis_index("chan")
    nchunk, _, rows, _ = send.shape
    signals = rows // 8
    tiles = signals // 2
    chips = nchan // 2
    chip, core = chan >> 1, chan & 1
    stages = stages_of(nchunk, tiles)
    order = [fc for i, (fc, _, _) in enumerate(stages) if fc not in [s[0] for s in stages[:i]]]

    def around(away):
        return lax.rem(chip + away, chips)

    loads = {
        fc: pltpu.make_async_copy(
            spectra_ref.at[:, :, :, fc * LANES : (fc + 1) * LANES], raw.at[fc], raw_sem.at[fc]
        )
        for fc in order
    }
    loads[order[0]].start()
    barrier = pltpu.get_barrier_semaphore()

    for near in (
        chip * 2 + 1 - core,
        around(1) * 2,
        around(1) * 2 + 1,
        around(chips - 1) * 2,
        around(chips - 1) * 2 + 1,
    ):
        pl.semaphore_signal(barrier, inc=1, device_id={"chan": near})

    @pl.when(tm > 0)
    def _():
        pl.semaphore_signal(barrier, inc=1, device_id={"tm": tm - 1})

    for fc in order[1:]:
        loads[fc].start()

    small = [
        pltpu.make_async_copy(whole, mine, small_sem.at[i])
        for i, (whole, mine) in enumerate(
            ((delays_hbm, delays_ref), (flags_hbm, flags_ref), (taps_hbm, taps_ref))
        )
    ]
    for copy in small:
        copy.start()

    def arrange(fc, pair):
        at = pl.ds(pl.multiple_of(pair * 16, 16), 16)
        part = raw[fc, :, :, at, :].astype(jnp.float32)
        for q in range(2):
            for c in range(2):
                for k in range(4):
                    mix[q, pl.ds(c * 4 + k, signals, stride=8), :] = part[c, k, q * 8 : q * 8 + 8, :]
        for q in range(2):
            send[fc, pair * 2 + q] = mix[q].astype(jnp.bfloat16)

    def push(stage, to):
        fc, first, last = stages[stage]
        at = pl.ds(first * 16, (last - first) * 16)
        pltpu.make_async_remote_copy(
            src_ref=send.at[fc, to, at],
            dst_ref=recv.at[fc, chan, at],
            send_sem=send_sem.at[stage],
            recv_sem=recv_sem.at[stage],
            device_id={"chan": to},
        ).start()

    def keep(stage):
        fc, first, last = stages[stage]
        at = pl.ds(first * 16, (last - first) * 16)
        pltpu.make_async_copy(
            send.at[fc, chan, at], recv.at[fc, chan, at], recv_sem.at[stage]
        ).start()

    def each_chip(work):
        def body(i, carry):
            far = chips // 2 - ((i + 1) >> 1)
            work(around(jnp.where((i & 1) == 0, far, chips - far)))
            return carry

        lax.fori_loop(0, chips - 1, body, 0)

    def as_known(work):
        up, down = around(1) * 2 + core, around(chips - 1) * 2 + core
        last = chips // 2

        def tell_up(d):
            pl.semaphore_signal(from_below.at[d], inc=1, device_id={"chan": up})

        def tell_down(d):
            pl.semaphore_signal(from_above.at[d], inc=1, device_id={"chan": down})

        pl.semaphore_wait(barrier, 5 + jnp.where(tm < ntm - 1, 1, 0))
        tell_up(2)
        tell_down(2)
        work(around(1))
        work(around(chips - 1))

        def body(d, carry):
            pl.semaphore_wait(from_below.at[d], 1)
            tell_up(d + 1)
            pl.semaphore_wait(from_above.at[d], 1)

            @pl.when(d < last - 1)
            def _():
                tell_down(d + 1)

            work(around(d))
            work(around(chips - d))
            return carry

        lax.fori_loop(2, last, body, 0)
        pl.semaphore_wait(from_below.at[last], 1)
        work(around(last))

    def issue(stage):
        fc, first, last = stages[stage]
        fresh = first == 0

        def to_chip(pair):
            if fresh:
                arrange(fc, pair)
            push(stage, pair * 2 + core)
            push(stage, pair * 2 + 1 - core)

        if fresh:
            loads[fc].wait()
        if stage == 0:
            as_known(to_chip)
        else:
            each_chip(to_chip)
        if fresh:
            arrange(fc, chip)
        push(stage, chip * 2 + 1 - core)
        keep(stage)

    def left(stage):
        fc, first, last = stages[stage]
        sent = send.at[fc, 0 : nchan - 1, first * 16 : last * 16]
        pltpu.make_async_copy(sent, sent, send_sem.at[stage]).wait()

    issue(0)
    issue(1)
    for copy in small:
        copy.wait()
    fill_tables(chan, delays_ref, flags_ref, hi, lo)

    @pl.when(tm == 0)
    def _():
        y[:, :, 0:HALO, :] = jnp.zeros((2, signals, HALO, LANES), jnp.float32)

    def transform(stage):
        fc, first, last = stages[stage]
        base = HALO + fc * LANES

        def one_tile(t, carry):
            part = recv[fc, :, pl.ds(pl.multiple_of(t * 16, 16), 16), :].astype(jnp.float32)
            pols = [part[:, p * 8 : p * 8 + 8, :].reshape(nchan * 8, LANES) for p in range(2)]
            x = jnp.concatenate(pols, axis=1).astype(jnp.bfloat16)
            dims = (((0,), (0,)), ((), ()))
            z = lax.dot_general(x, hi[t], dims, preferred_element_type=jnp.float32)
            z += lax.dot_general(x, lo[t], dims, preferred_element_type=jnp.float32)
            for p in range(2):
                of = slice(p * LANES, (p + 1) * LANES)
                y[0, t * 2 + p, base : base + LANES, :] = z[of, :LANES]
                y[1, t * 2 + p, base : base + LANES, :] = z[of, LANES:]
            return carry

        lax.fori_loop(first, last, one_tile, 0)

    def fir(stage, begin, end):
        _, first, last = stages[stage]
        sigs = 2 * (last - first)

        def one(i, carry):
            d, s = i // sigs, 2 * first + lax.rem(i, sigs)
            for row in range(begin, end, 64):
                count = min(64, end - row)
                total = None
                for j in range(TAPS):
                    start = HALO + row - j
                    term = taps_ref[j : j + 1, :] * y[d, s, start : start + count, :]
                    total = term if total is None else total + term
                out_ref[d, s, row : row + count, :] = total.astype(jnp.bfloat16)
            return carry

        lax.fori_loop(0, 2 * sigs, one, 0)

    frames = nchunk * LANES
    halo = pltpu.make_async_remote_copy(
        src_ref=y.at[:, :, frames : frames + HALO, :],
        dst_ref=y.at[:, :, 0:HALO, :],
        send_sem=halo_sem.at[0],
        recv_sem=halo_sem.at[1],
        device_id={"tm": lax.rem(tm + 1, ntm)},
    )

    for stage, (fc, first, last) in enumerate(stages):
        if stage + 2 < len(stages):
            left(stage)
            issue(stage + 2)
        arriving = recv.at[fc, :, first * 16 : last * 16]
        pltpu.make_async_copy(arriving, arriving, recv_sem.at[stage]).wait()
        transform(stage)
        if stage == 0:

            @pl.when(tm < ntm - 1)
            def _():
                halo.start()

        if fc == 0:

            @pl.when(tm > 0)
            def _():
                halo.wait_recv()

        begin = fc * LANES + (HALO if stage == 0 else 0)
        end = (fc + 1) * LANES + (HALO if fc == nchunk - 2 else 0)
        fir(stage, begin, end)

    for stage in range(len(stages) - 2, len(stages)):
        left(stage)

    @pl.when(tm < ntm - 1)
    def _():
        halo.wait_send()


def per_device(ntm, nchan, spectra, delays, flags, taps):
    parts, chans, sigs, frames = spectra.shape
    signals = sigs // nchan
    nfine = chans * nchan
    nchunk = frames // LANES
    rows = parts * chans * signals
    nstage = len(stages_of(nchunk, signals // 2))
    any_spec = pl.BlockSpec(memory_space=pl.ANY)

    def body(*refs):
        kernel(ntm, nchan, *refs)

    voltages = pl.pallas_call(
        body,
        out_shape=pltpu.VMEM((2, signals, frames, nfine), jnp.bfloat16),
        in_specs=[any_spec] * 4,
        out_specs=pl.BlockSpec(memory_space=pltpu.VMEM),
        scratch_shapes=[
            pltpu.SMEM(delays.shape, jnp.int32),
            pltpu.VMEM(flags.shape, jnp.int32),
            pltpu.VMEM(taps.shape, jnp.float32),
            pltpu.VMEM((nchunk, parts, chans, sigs, LANES), jnp.bfloat16),
            pltpu.VMEM((2, rows, LANES), jnp.float32),
            pltpu.VMEM((nchunk, nchan, rows, LANES), jnp.bfloat16),
            pltpu.VMEM((nchunk, nchan, rows, LANES), jnp.bfloat16),
            pltpu.VMEM((2, signals, HALO + frames, nfine), jnp.float32),
            pltpu.VMEM((signals // 2, 2 * nfine, 2 * nfine), jnp.bfloat16),
            pltpu.VMEM((signals // 2, 2 * nfine, 2 * nfine), jnp.bfloat16),
            pltpu.SemaphoreType.DMA((nchunk,)),
            pltpu.SemaphoreType.DMA((3,)),
            pltpu.SemaphoreType.DMA((nstage,)),
            pltpu.SemaphoreType.DMA((nstage,)),
            pltpu.SemaphoreType.DMA((2,)),
            pltpu.SemaphoreType.REGULAR((nchan // 4 + 1,)),
            pltpu.SemaphoreType.REGULAR((nchan // 4 + 1,)),
        ],
        compiler_params=pltpu.CompilerParams(
            collective_id=0, has_side_effects=True, vmem_limit_bytes=20 * 2**20
        ),
        cost_estimate=pl.CostEstimate(
            flops=8 * 2**27, bytes_accessed=4 * 2**20, transcendentals=0
        ),
        name="resynthesis",
    )(*(pltpu.with_memory_space_constraint(x, pltpu.HBM) for x in (spectra, delays, flags, taps)))
    return voltages


def solution(mesh):
    ntm, nchan = mesh.shape["tm"], mesh.shape["chan"]

    def body(spectra, delays, flags, taps):
        return per_device(ntm, nchan, spectra, delays, flags, taps)

    in_specs = (P(None, "chan", None, "tm"), P(), P(), P())
    return jax.shard_map(
        body, mesh=mesh, in_specs=in_specs, out_specs=P(None, "chan", "tm", None), check_vma=False
    )
```

```python
import math

import jax
import jax.numpy as jnp
from jax import lax
from jax.experimental import pallas as pl
from jax.experimental.pallas import tpu as pltpu
from jax.sharding import PartitionSpec as P

TAPS = 12
LANES = 128
HALO = 16


def fill_tables(chan, delays_ref, flags_ref, hi_ref, lo_ref):
    tiles, rows, cols = hi_ref.shape
    nfine = rows // 2
    row = lax.broadcasted_iota(jnp.int32, (rows, cols), 0)
    col = lax.broadcasted_iota(jnp.int32, (rows, cols), 1)
    fine = (row >> 3) * 4 + (row & 3)
    sample = col & (nfine - 1)
    quarter = (((row >> 2) & 1) - (col >> 7)) * (nfine // 4)
    frow = lax.broadcasted_iota(jnp.int32, (rows, nfine), 0)
    fcol = lax.broadcasted_iota(jnp.int32, (rows, nfine), 1)
    spread = (fcol == (frow >> 3) * 4 + (frow & 3)).astype(jnp.float32).astype(jnp.bfloat16)
    kept = jnp.dot(
        spread,
        flags_ref[...].astype(jnp.float32).astype(jnp.bfloat16),
        preferred_element_type=jnp.float32,
    )

    def one_tile(t, carry):
        tile = chan * tiles + t
        delay = delays_ref[tile]
        turn = (fine * (sample - delay) + quarter) & (nfine - 1)
        fold = nfine // 4 - jnp.abs(turn - nfine // 2)
        x = fold.astype(jnp.float32) * (2.0 * math.pi / nfine)
        x2 = x * x
        poly = -1.0 / 39916800.0
        for c in (1.0 / 362880.0, -1.0 / 5040.0, 1.0 / 120.0, -1.0 / 6.0, 1.0):
            poly = poly * x2 + c
        lane = lax.broadcasted_iota(jnp.int32, kept.shape, 1)
        keep = jnp.sum(jnp.where(lane == tile, kept, 0.0), axis=1, keepdims=True)
        table = (poly * x) * (keep * (-1.0 / math.sqrt(nfine)))
        hi = table.astype(jnp.bfloat16)
        hi_ref[t] = hi
        lo_ref[t] = (table - hi.astype(jnp.float32)).astype(jnp.bfloat16)
        return carry

    lax.fori_loop(0, tiles, one_tile, 0)


def to_series(part, hi, lo):
    part = part.astype(jnp.float32)
    count = part.shape[0] * 8
    pols = [part[:, p * 8 : p * 8 + 8, :].reshape(count, LANES) for p in range(2)]
    x = jnp.concatenate(pols, axis=1).astype(jnp.bfloat16)
    dims = (((0,), (0,)), ((), ()))
    z = lax.dot_general(x, hi, dims, preferred_element_type=jnp.float32)
    return z + lax.dot_general(x, lo, dims, preferred_element_type=jnp.float32)


def filtered(taps_ref, series_ref, at, start, count):
    total = None
    for j in range(TAPS):
        term = taps_ref[j : j + 1, :] * series_ref[(*at, pl.ds(start - j, count), slice(None))]
        total = term if total is None else total + term
    return total.astype(jnp.bfloat16)


def stages_of(nchunk, tiles):
    whole = [(nchunk - 1, 0, tiles)] + [(fc, 0, tiles) for fc in range(nchunk - 2)]
    half = tiles // 2
    return whole + [(nchunk - 2, 0, half)] + [(nchunk - 2, t, t + 1) for t in range(half, tiles)]


def kernel(
    ntm,
    nchan,
    spectra_ref,
    delays_hbm,
    flags_hbm,
    taps_hbm,
    out_ref,
    last_ref,
    table_ref,
    edges_ref,
    taps_out_ref,
    delays_ref,
    flags_ref,
    taps_ref,
    raw,
    mix,
    send,
    recv,
    y,
    hi,
    lo,
    raw_sem,
    small_sem,
    send_sem,
    recv_sem,
    halo_sem,
    from_below,
    from_above,
):
    tm = lax.axis_index("tm")
    chan = lax.axis_index("chan")
    nchunk, _, rows, _ = send.shape
    signals = rows // 8
    tiles = signals // 2
    chips = nchan // 2
    chip, core = chan >> 1, chan & 1
    stages = stages_of(nchunk, tiles)
    order = [fc for i, (fc, _, _) in enumerate(stages) if fc not in [s[0] for s in stages[:i]]]

    def around(away):
        return lax.rem(chip + away, chips)

    loads = {
        fc: pltpu.make_async_copy(
            spectra_ref.at[:, :, :, fc * LANES : (fc + 1) * LANES], raw.at[fc], raw_sem.at[fc]
        )
        for fc in order
    }
    loads[order[0]].start()
    barrier = pltpu.get_barrier_semaphore()

    for near in (
        chip * 2 + 1 - core,
        around(1) * 2,
        around(1) * 2 + 1,
        around(chips - 1) * 2,
        around(chips - 1) * 2 + 1,
    ):
        pl.semaphore_signal(barrier, inc=1, device_id={"chan": near})

    @pl.when(tm > 0)
    def _():
        pl.semaphore_signal(barrier, inc=1, device_id={"tm": tm - 1})

    for fc in order[1:]:
        loads[fc].start()

    small = [
        pltpu.make_async_copy(whole, mine, small_sem.at[i])
        for i, (whole, mine) in enumerate(
            ((delays_hbm, delays_ref), (flags_hbm, flags_ref), (taps_hbm, taps_ref))
        )
    ]
    for copy in small:
        copy.start()

    def arrange(fc, pair):
        at = pl.ds(pl.multiple_of(pair * 16, 16), 16)
        part = raw[fc, :, :, at, :].astype(jnp.float32)
        for q in range(2):
            for c in range(2):
                for k in range(4):
                    mix[q, pl.ds(c * 4 + k, signals, stride=8), :] = part[c, k, q * 8 : q * 8 + 8, :]
        for q in range(2):
            send[fc, pair * 2 + q] = mix[q].astype(jnp.bfloat16)

    def push(stage, to):
        fc, first, last = stages[stage]
        at = pl.ds(first * 16, (last - first) * 16)
        pltpu.make_async_remote_copy(
            src_ref=send.at[fc, to, at],
            dst_ref=recv.at[fc, chan, at],
            send_sem=send_sem.at[stage],
            recv_sem=recv_sem.at[stage],
            device_id={"chan": to},
        ).start()

    def keep(stage):
        fc, first, last = stages[stage]
        at = pl.ds(first * 16, (last - first) * 16)
        pltpu.make_async_copy(
            send.at[fc, chan, at], recv.at[fc, chan, at], recv_sem.at[stage]
        ).start()

    def each_chip(work):
        def body(i, carry):
            far = chips // 2 - ((i + 1) >> 1)
            work(around(jnp.where((i & 1) == 0, far, chips - far)))
            return carry

        lax.fori_loop(0, chips - 1, body, 0)

    def as_known(work):
        up, down = around(1) * 2 + core, around(chips - 1) * 2 + core
        last = chips // 2

        def tell_up(d):
            pl.semaphore_signal(from_below.at[d], inc=1, device_id={"chan": up})

        def tell_down(d):
            pl.semaphore_signal(from_above.at[d], inc=1, device_id={"chan": down})

        pl.semaphore_wait(barrier, 5 + jnp.where(tm < ntm - 1, 1, 0))
        tell_up(2)
        tell_down(2)
        work(around(1))
        work(around(chips - 1))

        def body(d, carry):
            pl.semaphore_wait(from_below.at[d], 1)
            tell_up(d + 1)
            pl.semaphore_wait(from_above.at[d], 1)

            @pl.when(d < last - 1)
            def _():
                tell_down(d + 1)

            work(around(d))
            work(around(chips - d))
            return carry

        lax.fori_loop(2, last, body, 0)
        pl.semaphore_wait(from_below.at[last], 1)
        work(around(last))

    def issue(stage):
        fc, first, last = stages[stage]
        fresh = first == 0

        def to_chip(pair):
            if fresh:
                arrange(fc, pair)
            push(stage, pair * 2 + core)
            push(stage, pair * 2 + 1 - core)

        if fresh:
            loads[fc].wait()
        if stage == 0:
            as_known(to_chip)
        else:
            each_chip(to_chip)
        if fresh:
            arrange(fc, chip)
        push(stage, chip * 2 + 1 - core)
        keep(stage)

    def left(stage):
        fc, first, last = stages[stage]
        sent = send.at[fc, 0 : nchan - 1, first * 16 : last * 16]
        pltpu.make_async_copy(sent, sent, send_sem.at[stage]).wait()

    issue(0)
    issue(1)
    for copy in small:
        copy.wait()
    fill_tables(chan, delays_ref, flags_ref, hi, lo)

    @pl.when(tm == 0)
    def _():
        y[:, :, 0:HALO, :] = jnp.zeros((2, signals, HALO, LANES), jnp.float32)

    def transform(stage):
        fc, first, last = stages[stage]
        base = HALO + fc * LANES

        def one_tile(t, carry):
            part = recv[fc, :, pl.ds(pl.multiple_of(t * 16, 16), 16), :]
            z = to_series(part, hi[t], lo[t])
            for p in range(2):
                of = slice(p * LANES, (p + 1) * LANES)
                y[0, t * 2 + p, base : base + LANES, :] = z[of, :LANES]
                y[1, t * 2 + p, base : base + LANES, :] = z[of, LANES:]
            return carry

        lax.fori_loop(first, last, one_tile, 0)

    def fir(stage, begin, end):
        _, first, last = stages[stage]
        sigs = 2 * (last - first)

        def one(i, carry):
            d, s = i // sigs, 2 * first + lax.rem(i, sigs)
            for row in range(begin, end, 64):
                count = min(64, end - row)
                rows_out = filtered(taps_ref, y, (d, s), HALO + row, count)
                out_ref[d, s, row : row + count, :] = rows_out
            return carry

        lax.fori_loop(0, 2 * sigs, one, 0)

    frames = nchunk * LANES
    halo = pltpu.make_async_remote_copy(
        src_ref=y.at[:, :, frames : frames + HALO, :],
        dst_ref=y.at[:, :, 0:HALO, :],
        send_sem=halo_sem.at[0],
        recv_sem=halo_sem.at[1],
        device_id={"tm": lax.rem(tm + 1, ntm)},
    )

    for stage, (fc, first, last) in enumerate(stages):
        if stage + 2 < len(stages):
            left(stage)
            issue(stage + 2)
        if stage == len(stages) - 1:
            table_ref[0], table_ref[1] = hi[first], lo[first]
            taps_out_ref[...] = taps_ref[...]
            sigs = slice(2 * first, 2 * last)
            edges_ref[0] = y[:, sigs, fc * LANES : fc * LANES + HALO, :]
            after = HALO + (fc + 1) * LANES
            edges_ref[1] = y[:, sigs, after : after + HALO, :]
        arriving = recv.at[fc, :, first * 16 : last * 16]
        pltpu.make_async_copy(arriving, arriving, recv_sem.at[stage]).wait()
        if stage == len(stages) - 1:
            last_ref[...] = recv[fc, :, first * 16 : last * 16, :]
            break
        transform(stage)
        if stage == 0:

            @pl.when(tm < ntm - 1)
            def _():
                halo.start()

        if fc == 0:

            @pl.when(tm > 0)
            def _():
                halo.wait_recv()

        begin = fc * LANES + (HALO if stage == 0 else 0)
        end = (fc + 1) * LANES + (HALO if fc == nchunk - 2 else 0)
        fir(stage, begin, end)

    for stage in range(len(stages) - 2, len(stages)):
        left(stage)

    @pl.when(tm < ntm - 1)
    def _():
        halo.wait_send()


def finish(stage, done_ref, last_ref, table_ref, edges_ref, taps_ref, out_ref, y, result, sem):
    fc, first, last = stage
    _, signals, frames, _ = done_ref.shape
    begin, end = fc * LANES, (fc + 1) * LANES + HALO
    spans = [(s, 0, frames) for s in range(signals) if not 2 * first <= s < 2 * last]
    for s in range(2 * first, 2 * last):
        spans += [(s, 0, begin), (s, end, frames)]
    copies = []
    for s, start, stop in spans:
        for d in range(2):
            at = (d, s, slice(start, stop))
            copies.append(
                pltpu.make_async_copy(done_ref.at[at], out_ref.at[at], sem.at[len(copies)])
            )
            copies[-1].start()
    y[:, :, 0:HALO, :] = edges_ref[0]
    y[:, :, HALO + LANES :, :] = edges_ref[1]
    z = to_series(last_ref[...], table_ref[0], table_ref[1])
    for p in range(2):
        of = slice(p * LANES, (p + 1) * LANES)
        y[0, p, HALO : HALO + LANES, :] = z[of, :LANES]
        y[1, p, HALO : HALO + LANES, :] = z[of, LANES:]
    for d in range(2):
        for p in range(2):
            for row in range(0, end - begin, 48):
                result[d, p, row : row + 48, :] = filtered(taps_ref, y, (d, p), HALO + row, 48)
            at = (d, 2 * first + p, slice(begin, end))
            copies.append(
                pltpu.make_async_copy(result.at[d, p], out_ref.at[at], sem.at[len(copies)])
            )
            copies[-1].start()
    for copy in copies:
        copy.wait()


def per_device(ntm, nchan, spectra, delays, flags, taps):
    parts, chans, sigs, frames = spectra.shape
    signals = sigs // nchan
    nfine = chans * nchan
    nchunk = frames // LANES
    rows = parts * chans * signals
    nstage = len(stages_of(nchunk, signals // 2))
    any_spec = pl.BlockSpec(memory_space=pl.ANY)

    def body(*refs):
        kernel(ntm, nchan, *refs)

    stages = stages_of(nchunk, signals // 2)
    vmem_spec = pl.BlockSpec(memory_space=pltpu.VMEM)
    handed_over = pl.pallas_call(
        body,
        out_shape=[
            pltpu.VMEM((2, signals, frames, nfine), jnp.bfloat16),
            pltpu.VMEM((nchan, 16, LANES), jnp.bfloat16),
            pltpu.VMEM((2, 2 * nfine, 2 * nfine), jnp.bfloat16),
            pltpu.VMEM((2, 2, 2, HALO, nfine), jnp.float32),
            pltpu.VMEM(taps.shape, jnp.float32),
        ],
        in_specs=[any_spec] * 4,
        out_specs=[vmem_spec] * 5,
        scratch_shapes=[
            pltpu.SMEM(delays.shape, jnp.int32),
            pltpu.VMEM(flags.shape, jnp.int32),
            pltpu.VMEM(taps.shape, jnp.float32),
            pltpu.VMEM((nchunk, parts, chans, sigs, LANES), jnp.bfloat16),
            pltpu.VMEM((2, rows, LANES), jnp.float32),
            pltpu.VMEM((nchunk, nchan, rows, LANES), jnp.bfloat16),
            pltpu.VMEM((nchunk, nchan, rows, LANES), jnp.bfloat16),
            pltpu.VMEM((2, signals, HALO + frames, nfine), jnp.float32),
            pltpu.VMEM((signals // 2, 2 * nfine, 2 * nfine), jnp.bfloat16),
            pltpu.VMEM((signals // 2, 2 * nfine, 2 * nfine), jnp.bfloat16),
            pltpu.SemaphoreType.DMA((nchunk,)),
            pltpu.SemaphoreType.DMA((3,)),
            pltpu.SemaphoreType.DMA((nstage,)),
            pltpu.SemaphoreType.DMA((nstage,)),
            pltpu.SemaphoreType.DMA((2,)),
            pltpu.SemaphoreType.REGULAR((nchan // 4 + 1,)),
            pltpu.SemaphoreType.REGULAR((nchan // 4 + 1,)),
        ],
        compiler_params=pltpu.CompilerParams(
            collective_id=0, has_side_effects=True, vmem_limit_bytes=20 * 2**20
        ),
        cost_estimate=pl.CostEstimate(
            flops=8 * 2**27, bytes_accessed=4 * 2**20, transcendentals=0
        ),
        name="resynthesis",
    )(*(pltpu.with_memory_space_constraint(x, pltpu.HBM) for x in (spectra, delays, flags, taps)))
    held = [pltpu.with_memory_space_constraint(x, pltpu.VMEM) for x in handed_over]

    def finish_body(*refs):
        finish(stages[-1], *refs)

    return pl.pallas_call(
        finish_body,
        out_shape=jax.ShapeDtypeStruct((2, signals, frames, nfine), jnp.bfloat16),
        in_specs=[vmem_spec] * 5,
        out_specs=any_spec,
        scratch_shapes=[
            pltpu.VMEM((2, 2, HALO + LANES + HALO, nfine), jnp.float32),
            pltpu.VMEM((2, 2, LANES + HALO, nfine), jnp.bfloat16),
            pltpu.SemaphoreType.DMA((2 * signals + 8,)),
        ],
        compiler_params=pltpu.CompilerParams(vmem_limit_bytes=20 * 2**20),
        cost_estimate=pl.CostEstimate(
            flops=2**27, bytes_accessed=2 * 2**20, transcendentals=0
        ),
        name="last_stage",
    )(*held)


def solution(mesh):
    ntm, nchan = mesh.shape["tm"], mesh.shape["chan"]

    def body(spectra, delays, flags, taps):
        return per_device(ntm, nchan, spectra, delays, flags, taps)

    in_specs = (P(None, "chan", None, "tm"), P(), P(), P())
    return jax.shard_map(
        body, mesh=mesh, in_specs=in_specs, out_specs=P(None, "chan", "tm", None), check_vma=False
    )
```

```python
import math

import jax
import jax.numpy as jnp
from jax import lax
from jax.experimental import pallas as pl
from jax.experimental.pallas import tpu as pltpu
from jax.sharding import PartitionSpec as P

TAPS = 12
LANES = 128
HALO = 16


def fill_tables(chan, delays_ref, flags_ref, hi_ref, lo_ref):
    tiles, rows, cols = hi_ref.shape
    nfine = rows // 2
    row = lax.broadcasted_iota(jnp.int32, (rows, cols), 0)
    col = lax.broadcasted_iota(jnp.int32, (rows, cols), 1)
    fine = (row >> 3) * 4 + (row & 3)
    sample = col & (nfine - 1)
    quarter = (((row >> 2) & 1) - (col >> 7)) * (nfine // 4)
    frow = lax.broadcasted_iota(jnp.int32, (rows, nfine), 0)
    fcol = lax.broadcasted_iota(jnp.int32, (rows, nfine), 1)
    spread = (fcol == (frow >> 3) * 4 + (frow & 3)).astype(jnp.float32).astype(jnp.bfloat16)
    kept = jnp.dot(
        spread,
        flags_ref[...].astype(jnp.float32).astype(jnp.bfloat16),
        preferred_element_type=jnp.float32,
    )

    def one_tile(t, carry):
        tile = chan * tiles + t
        delay = delays_ref[tile]
        turn = (fine * (sample - delay) + quarter) & (nfine - 1)
        fold = nfine // 4 - jnp.abs(turn - nfine // 2)
        x = fold.astype(jnp.float32) * (2.0 * math.pi / nfine)
        x2 = x * x
        poly = -1.0 / 39916800.0
        for c in (1.0 / 362880.0, -1.0 / 5040.0, 1.0 / 120.0, -1.0 / 6.0, 1.0):
            poly = poly * x2 + c
        lane = lax.broadcasted_iota(jnp.int32, kept.shape, 1)
        keep = jnp.sum(jnp.where(lane == tile, kept, 0.0), axis=1, keepdims=True)
        table = (poly * x) * (keep * (-1.0 / math.sqrt(nfine)))
        hi = table.astype(jnp.bfloat16)
        hi_ref[t] = hi
        lo_ref[t] = (table - hi.astype(jnp.float32)).astype(jnp.bfloat16)
        return carry

    lax.fori_loop(0, tiles, one_tile, 0)


def to_series(part, hi, lo):
    part = part.astype(jnp.float32)
    count = part.shape[0] * 8
    pols = [part[:, p * 8 : p * 8 + 8, :].reshape(count, LANES) for p in range(2)]
    x = jnp.concatenate(pols, axis=1).astype(jnp.bfloat16)
    dims = (((0,), (0,)), ((), ()))
    z = lax.dot_general(x, hi, dims, preferred_element_type=jnp.float32)
    return z + lax.dot_general(x, lo, dims, preferred_element_type=jnp.float32)


def filtered(taps_ref, series_ref, at, start, count):
    total = None
    for j in range(TAPS):
        term = taps_ref[j : j + 1, :] * series_ref[(*at, pl.ds(start - j, count), slice(None))]
        total = term if total is None else total + term
    return total.astype(jnp.bfloat16)


def stages_of(nchunk, tiles):
    whole = [(nchunk - 1, 0, tiles)] + [(fc, 0, tiles) for fc in range(nchunk - 2)]
    half = tiles // 2
    return whole + [(nchunk - 2, 0, half)] + [(nchunk - 2, t, t + 1) for t in range(half, tiles)]


def kernel(
    ntm,
    nchan,
    spectra_ref,
    delays_hbm,
    flags_hbm,
    taps_hbm,
    out_ref,
    last_ref,
    table_ref,
    edges_ref,
    taps_out_ref,
    delays_ref,
    flags_ref,
    taps_ref,
    raw,
    mix,
    send,
    ring_a,
    ring_b,
    own,
    recv,
    y,
    hi,
    lo,
    raw_sem,
    small_sem,
    send_sem,
    recv_sem,
    halo_sem,
    from_below,
    from_above,
    pass_send_a,
    pass_recv_a,
    pass_send_b,
    pass_recv_b,
):
    tm = lax.axis_index("tm")
    chan = lax.axis_index("chan")
    nchunk, _, rows, _ = recv.shape
    signals = rows // 8
    tiles = signals // 2
    chips = nchan // 2
    chip, core = chan >> 1, chan & 1
    stages = stages_of(nchunk, tiles)
    order = [fc for i, (fc, _, _) in enumerate(stages) if fc not in [s[0] for s in stages[:i]]]

    def around(away):
        return lax.rem(chip + away, chips)

    loads = {
        fc: pltpu.make_async_copy(
            spectra_ref.at[:, :, :, fc * LANES : (fc + 1) * LANES], raw.at[fc], raw_sem.at[fc]
        )
        for fc in order
    }
    loads[order[0]].start()
    barrier = pltpu.get_barrier_semaphore()

    for near in (
        chip * 2 + 1 - core,
        around(1) * 2,
        around(1) * 2 + 1,
        around(chips - 1) * 2,
        around(chips - 1) * 2 + 1,
    ):
        pl.semaphore_signal(barrier, inc=1, device_id={"chan": near})

    @pl.when(tm > 0)
    def _():
        pl.semaphore_signal(barrier, inc=1, device_id={"tm": tm - 1})

    for fc in order[1:]:
        loads[fc].start()

    small = [
        pltpu.make_async_copy(whole, mine, small_sem.at[i])
        for i, (whole, mine) in enumerate(
            ((delays_hbm, delays_ref), (flags_hbm, flags_ref), (taps_hbm, taps_ref))
        )
    ]
    for copy in small:
        copy.start()

    def arrange(fc, pair, put):
        at = pl.ds(pl.multiple_of(pair * 16, 16), 16)
        part = raw[fc, :, :, at, :].astype(jnp.float32)
        for q in range(2):
            for c in range(2):
                for k in range(4):
                    mix[q, pl.ds(c * 4 + k, signals, stride=8), :] = part[c, k, q * 8 : q * 8 + 8, :]
        for q in range(2):
            put(q, mix[q].astype(jnp.bfloat16))

    def remote(src, dst, send_to, recv_to, to):
        return pltpu.make_async_remote_copy(
            src_ref=src, dst_ref=dst, send_sem=send_to, recv_sem=recv_to, device_id={"chan": to}
        )

    half = chips // 2
    ways = []
    for blocks, count, sends, recvs, sign in (
        (ring_a, half, pass_send_a, pass_recv_a, 1),
        (ring_b, half - 1, pass_send_b, pass_recv_b, -1),
    ):
        step = jnp.where(core == 0, sign, -sign)
        ways.append((blocks, count, sends, recvs, step))

    def ahead(step, r):
        return lax.rem(chip + step * r + 2 * chips, chips)

    def held_at(count, h):
        return h * count - h * (h - 1) // 2

    def deliver(i, way, h):
        blocks, count, _, _, step = way
        for q in range(2):
            remote(
                blocks.at[i, held_at(count, h), q],
                recv.at[order[i], ahead(step, -h) * 2 + core],
                send_sem.at[i],
                recv_sem.at[i],
                ahead(step, 1) * 2 + q,
            ).start()

    def passed_on(i, way, h):
        blocks, count, sends, recvs, step = way
        size, here, there = count - h - 1, held_at(count, h) + 1, held_at(count, h + 1)
        return remote(
            blocks.at[i, here : here + size],
            blocks.at[i, there : there + size],
            sends.at[i, h],
            recvs.at[i, h],
            ahead(step, 1) * 2 + core,
        )

    def first_hop(i):
        fc = order[i]
        loads[fc].wait()

        def lay(way, r):
            def put(q, value):
                way[0][i, r - 1, q] = value

            arrange(fc, ahead(way[4], r), put)

        for way in ways:
            lay(way, 1)
            if i == 0 and way is ways[0]:
                pl.semaphore_wait(barrier, 5 + jnp.where(tm < ntm - 1, 1, 0))
                tell_up(2)
                tell_down(2)
            deliver(i, way, 0)

        def one(way, r):
            blocks, count, sends, recvs, step = way
            lay(way, r)
            remote(
                blocks.at[i, r - 1],
                blocks.at[i, count + r - 2],
                sends.at[i, 0],
                recvs.at[i, 0],
                ahead(step, 1) * 2 + core,
            ).start()

        def body(r, carry):
            for way in ways:
                one(way, r)
            return carry

        lax.fori_loop(2, half, body, 0)
        one(ways[0], half)

        def put(q, value):
            own[i, q] = value

        arrange(fc, chip, put)
        remote(
            own.at[i, 1 - core],
            recv.at[fc, chan],
            send_sem.at[i],
            recv_sem.at[i],
            chip * 2 + 1 - core,
        ).start()
        pltpu.make_async_copy(own.at[i, core], recv.at[fc, chan], recv_sem.at[i]).start()

    def next_hop(i, h):
        for way in ways:
            count = way[1]
            if h < count:
                passed_on(i, way, h - 1).wait_recv()
                deliver(i, way, h)
                if h < count - 1:
                    passed_on(i, way, h).start()

    def push(stage, to):
        fc, first, last = stages[stage]
        at = pl.ds(first * 16, (last - first) * 16)
        remote(
            send.at[to, at], recv.at[fc, chan, at], send_sem.at[stage], recv_sem.at[stage], to
        ).start()

    def push_chip(stage, pair):
        push(stage, pair * 2 + core)
        push(stage, pair * 2 + 1 - core)

    def push_own(stage):
        fc, first, last = stages[stage]
        at = pl.ds(first * 16, (last - first) * 16)
        push(stage, chip * 2 + 1 - core)
        pltpu.make_async_copy(send.at[chan, at], recv.at[fc, chan, at], recv_sem.at[stage]).start()

    def issue(stage):
        def body(i, carry):
            far = half - ((i + 1) >> 1)
            push_chip(stage, around(jnp.where((i & 1) == 0, far, chips - far)))
            return carry

        lax.fori_loop(0, chips - 1, body, 0)
        push_own(stage)

    def tell_up(d):
        pl.semaphore_signal(from_below.at[d], inc=1, device_id={"chan": around(1) * 2 + core})

    def tell_down(d):
        pl.semaphore_signal(
            from_above.at[d], inc=1, device_id={"chan": around(chips - 1) * 2 + core}
        )

    def left(stage):
        fc, first, last = stages[stage]
        sent = recv.at[fc, 0 : nchan - 1, first * 16 : last * 16]
        pltpu.make_async_copy(sent, sent, send_sem.at[stage]).wait()

    first_hop(0)
    first_hop(1)
    for copy in small:
        copy.wait()
    fill_tables(chan, delays_ref, flags_ref, hi, lo)
    loads[order[2]].wait()

    def lay_direct(pair, carry):
        def put(q, value):
            send[pair * 2 + q] = value

        arrange(order[2], pair, put)
        return carry

    lax.fori_loop(0, chips, lay_direct, 0)
    for h in range(1, half):
        next_hop(0, h)
        next_hop(1, h)
        push_chip(2, around(h))
        push_chip(2, around(chips - h))
        pl.semaphore_wait(from_below.at[h + 1], 1)
        if h + 2 <= half:
            tell_up(h + 2)
        if h + 1 < half:
            pl.semaphore_wait(from_above.at[h + 1], 1)
        if h + 2 < half:
            tell_down(h + 2)
    push_chip(2, around(half))
    push_own(2)
    for stage in range(3, len(stages)):
        issue(stage)

    @pl.when(tm == 0)
    def _():
        y[:, :, 0:HALO, :] = jnp.zeros((2, signals, HALO, LANES), jnp.float32)

    def transform(stage):
        fc, first, last = stages[stage]
        base = HALO + fc * LANES

        def one_tile(t, carry):
            part = recv[fc, :, pl.ds(pl.multiple_of(t * 16, 16), 16), :]
            z = to_series(part, hi[t], lo[t])
            for p in range(2):
                of = slice(p * LANES, (p + 1) * LANES)
                y[0, t * 2 + p, base : base + LANES, :] = z[of, :LANES]
                y[1, t * 2 + p, base : base + LANES, :] = z[of, LANES:]
            return carry

        lax.fori_loop(first, last, one_tile, 0)

    def fir(stage, begin, end):
        _, first, last = stages[stage]
        sigs = 2 * (last - first)

        def one(i, carry):
            d, s = i // sigs, 2 * first + lax.rem(i, sigs)
            for row in range(begin, end, 64):
                count = min(64, end - row)
                rows_out = filtered(taps_ref, y, (d, s), HALO + row, count)
                out_ref[d, s, row : row + count, :] = rows_out
            return carry

        lax.fori_loop(0, 2 * sigs, one, 0)

    frames = nchunk * LANES
    halo = pltpu.make_async_remote_copy(
        src_ref=y.at[:, :, frames : frames + HALO, :],
        dst_ref=y.at[:, :, 0:HALO, :],
        send_sem=halo_sem.at[0],
        recv_sem=halo_sem.at[1],
        device_id={"tm": lax.rem(tm + 1, ntm)},
    )

    for stage, (fc, first, last) in enumerate(stages):
        if stage == len(stages) - 1:
            table_ref[0], table_ref[1] = hi[first], lo[first]
            taps_out_ref[...] = taps_ref[...]
            sigs = slice(2 * first, 2 * last)
            edges_ref[0] = y[:, sigs, fc * LANES : fc * LANES + HALO, :]
            after = HALO + (fc + 1) * LANES
            edges_ref[1] = y[:, sigs, after : after + HALO, :]
        arriving = recv.at[fc, :, first * 16 : last * 16]
        pltpu.make_async_copy(arriving, arriving, recv_sem.at[stage]).wait()
        if stage == len(stages) - 1:
            last_ref[...] = recv[fc, :, first * 16 : last * 16, :]
            break
        transform(stage)
        if stage == 0:

            @pl.when(tm < ntm - 1)
            def _():
                halo.start()

        if fc == 0:

            @pl.when(tm > 0)
            def _():
                halo.wait_recv()

        begin = fc * LANES + (HALO if stage == 0 else 0)
        end = (fc + 1) * LANES + (HALO if fc == nchunk - 2 else 0)
        fir(stage, begin, end)

    for stage in range(len(stages)):
        left(stage)
    for i in range(2):
        for way in ways:
            for h in range(way[1] - 1):
                passed_on(i, way, h).wait_send()

    @pl.when(tm < ntm - 1)
    def _():
        halo.wait_send()


def finish(stage, done_ref, last_ref, table_ref, edges_ref, taps_ref, out_ref, y, result, sem):
    fc, first, last = stage
    _, signals, frames, _ = done_ref.shape
    begin, end = fc * LANES, (fc + 1) * LANES + HALO
    spans = [(s, 0, frames) for s in range(signals) if not 2 * first <= s < 2 * last]
    for s in range(2 * first, 2 * last):
        spans += [(s, 0, begin), (s, end, frames)]
    copies = []
    for s, start, stop in spans:
        for d in range(2):
            at = (d, s, slice(start, stop))
            copies.append(
                pltpu.make_async_copy(done_ref.at[at], out_ref.at[at], sem.at[len(copies)])
            )
            copies[-1].start()
    y[:, :, 0:HALO, :] = edges_ref[0]
    y[:, :, HALO + LANES :, :] = edges_ref[1]
    z = to_series(last_ref[...], table_ref[0], table_ref[1])
    for p in range(2):
        of = slice(p * LANES, (p + 1) * LANES)
        y[0, p, HALO : HALO + LANES, :] = z[of, :LANES]
        y[1, p, HALO : HALO + LANES, :] = z[of, LANES:]
    for d in range(2):
        for p in range(2):
            for row in range(0, end - begin, 48):
                result[d, p, row : row + 48, :] = filtered(taps_ref, y, (d, p), HALO + row, 48)
            at = (d, 2 * first + p, slice(begin, end))
            copies.append(
                pltpu.make_async_copy(result.at[d, p], out_ref.at[at], sem.at[len(copies)])
            )
            copies[-1].start()
    for copy in copies:
        copy.wait()


def per_device(ntm, nchan, spectra, delays, flags, taps):
    parts, chans, sigs, frames = spectra.shape
    signals = sigs // nchan
    nfine = chans * nchan
    nchunk = frames // LANES
    rows = parts * chans * signals
    half = nchan // 4
    nstage = len(stages_of(nchunk, signals // 2))
    any_spec = pl.BlockSpec(memory_space=pl.ANY)

    def body(*refs):
        kernel(ntm, nchan, *refs)

    stages = stages_of(nchunk, signals // 2)
    vmem_spec = pl.BlockSpec(memory_space=pltpu.VMEM)
    handed_over = pl.pallas_call(
        body,
        out_shape=[
            pltpu.VMEM((2, signals, frames, nfine), jnp.bfloat16),
            pltpu.VMEM((nchan, 16, LANES), jnp.bfloat16),
            pltpu.VMEM((2, 2 * nfine, 2 * nfine), jnp.bfloat16),
            pltpu.VMEM((2, 2, 2, HALO, nfine), jnp.float32),
            pltpu.VMEM(taps.shape, jnp.float32),
        ],
        in_specs=[any_spec] * 4,
        out_specs=[vmem_spec] * 5,
        scratch_shapes=[
            pltpu.SMEM(delays.shape, jnp.int32),
            pltpu.VMEM(flags.shape, jnp.int32),
            pltpu.VMEM(taps.shape, jnp.float32),
            pltpu.VMEM((nchunk, parts, chans, sigs, LANES), jnp.bfloat16),
            pltpu.VMEM((2, rows, LANES), jnp.float32),
            pltpu.VMEM((nchan, rows, LANES), jnp.bfloat16),
            pltpu.VMEM((2, half * (half + 1) // 2, 2, rows, LANES), jnp.bfloat16),
            pltpu.VMEM((2, half * (half - 1) // 2, 2, rows, LANES), jnp.bfloat16),
            pltpu.VMEM((2, 2, rows, LANES), jnp.bfloat16),
            pltpu.VMEM((nchunk, nchan, rows, LANES), jnp.bfloat16),
            pltpu.VMEM((2, signals, HALO + frames, nfine), jnp.float32),
            pltpu.VMEM((signals // 2, 2 * nfine, 2 * nfine), jnp.bfloat16),
            pltpu.VMEM((signals // 2, 2 * nfine, 2 * nfine), jnp.bfloat16),
            pltpu.SemaphoreType.DMA((nchunk,)),
            pltpu.SemaphoreType.DMA((3,)),
            pltpu.SemaphoreType.DMA((nstage,)),
            pltpu.SemaphoreType.DMA((nstage,)),
            pltpu.SemaphoreType.DMA((2,)),
            pltpu.SemaphoreType.REGULAR((half + 1,)),
            pltpu.SemaphoreType.REGULAR((half + 1,)),
            pltpu.SemaphoreType.DMA((2, half)),
            pltpu.SemaphoreType.DMA((2, half)),
            pltpu.SemaphoreType.DMA((2, half)),
            pltpu.SemaphoreType.DMA((2, half)),
        ],
        compiler_params=pltpu.CompilerParams(
            collective_id=0, has_side_effects=True, vmem_limit_bytes=24 * 2**20
        ),
        cost_estimate=pl.CostEstimate(
            flops=8 * 2**27, bytes_accessed=4 * 2**20, transcendentals=0
        ),
        name="resynthesis",
    )(*(pltpu.with_memory_space_constraint(x, pltpu.HBM) for x in (spectra, delays, flags, taps)))
    held = [pltpu.with_memory_space_constraint(x, pltpu.VMEM) for x in handed_over]

    def finish_body(*refs):
        finish(stages[-1], *refs)

    return pl.pallas_call(
        finish_body,
        out_shape=jax.ShapeDtypeStruct((2, signals, frames, nfine), jnp.bfloat16),
        in_specs=[vmem_spec] * 5,
        out_specs=any_spec,
        scratch_shapes=[
            pltpu.VMEM((2, 2, HALO + LANES + HALO, nfine), jnp.float32),
            pltpu.VMEM((2, 2, LANES + HALO, nfine), jnp.bfloat16),
            pltpu.SemaphoreType.DMA((2 * signals + 8,)),
        ],
        compiler_params=pltpu.CompilerParams(vmem_limit_bytes=20 * 2**20),
        cost_estimate=pl.CostEstimate(
            flops=2**27, bytes_accessed=2 * 2**20, transcendentals=0
        ),
        name="last_stage",
    )(*held)


def solution(mesh):
    ntm, nchan = mesh.shape["tm"], mesh.shape["chan"]

    def body(spectra, delays, flags, taps):
        return per_device(ntm, nchan, spectra, delays, flags, taps)

    in_specs = (P(None, "chan", None, "tm"), P(), P(), P())
    return jax.shard_map(
        body, mesh=mesh, in_specs=in_specs, out_specs=P(None, "chan", "tm", None), check_vma=False
    )
```

```python
import math

import jax
import jax.numpy as jnp
from jax import lax
from jax.experimental import pallas as pl
from jax.experimental.pallas import tpu as pltpu
from jax.sharding import PartitionSpec as P

TAPS = 12
LANES = 128
HALO = 16


def fill_tables(chan, delays_ref, flags_ref, hi_ref, lo_ref):
    tiles, rows, cols = hi_ref.shape
    nfine = rows // 2
    row = lax.broadcasted_iota(jnp.int32, (rows, cols), 0)
    col = lax.broadcasted_iota(jnp.int32, (rows, cols), 1)
    fine = (row >> 3) * 4 + (row & 3)
    sample = col & (nfine - 1)
    quarter = (((row >> 2) & 1) - (col >> 7)) * (nfine // 4)
    frow = lax.broadcasted_iota(jnp.int32, (rows, nfine), 0)
    fcol = lax.broadcasted_iota(jnp.int32, (rows, nfine), 1)
    spread = (fcol == (frow >> 3) * 4 + (frow & 3)).astype(jnp.float32).astype(jnp.bfloat16)
    kept = jnp.dot(
        spread,
        flags_ref[...].astype(jnp.float32).astype(jnp.bfloat16),
        preferred_element_type=jnp.float32,
    )

    def one_tile(t, carry):
        tile = chan * tiles + t
        delay = delays_ref[tile]
        turn = (fine * (sample - delay) + quarter) & (nfine - 1)
        fold = nfine // 4 - jnp.abs(turn - nfine // 2)
        x = fold.astype(jnp.float32) * (2.0 * math.pi / nfine)
        x2 = x * x
        poly = -1.0 / 39916800.0
        for c in (1.0 / 362880.0, -1.0 / 5040.0, 1.0 / 120.0, -1.0 / 6.0, 1.0):
            poly = poly * x2 + c
        lane = lax.broadcasted_iota(jnp.int32, kept.shape, 1)
        keep = jnp.sum(jnp.where(lane == tile, kept, 0.0), axis=1, keepdims=True)
        table = (poly * x) * (keep * (-1.0 / math.sqrt(nfine)))
        hi = table.astype(jnp.bfloat16)
        hi_ref[t] = hi
        lo_ref[t] = (table - hi.astype(jnp.float32)).astype(jnp.bfloat16)
        return carry

    lax.fori_loop(0, tiles, one_tile, 0)


def to_series(part, hi, lo):
    part = part.astype(jnp.float32)
    count = part.shape[0] * 8
    pols = [part[:, p * 8 : p * 8 + 8, :].reshape(count, LANES) for p in range(2)]
    x = jnp.concatenate(pols, axis=1).astype(jnp.bfloat16)
    dims = (((0,), (0,)), ((), ()))
    z = lax.dot_general(x, hi, dims, preferred_element_type=jnp.float32)
    return z + lax.dot_general(x, lo, dims, preferred_element_type=jnp.float32)


def filtered(taps_ref, series_ref, at, start, count):
    total = None
    for j in range(TAPS):
        term = taps_ref[j : j + 1, :] * series_ref[(*at, pl.ds(start - j, count), slice(None))]
        total = term if total is None else total + term
    return total.astype(jnp.bfloat16)


def stages_of(nchunk, tiles):
    whole = [(nchunk - 1, 0, tiles)] + [(fc, 0, tiles) for fc in range(nchunk - 2)]
    return whole + [(nchunk - 2, 0, tiles // 2), (nchunk - 2, tiles // 2, tiles)]


def kernel(
    ntm,
    nchan,
    spectra_ref,
    delays_hbm,
    flags_hbm,
    taps_hbm,
    out_ref,
    last_ref,
    table_ref,
    edges_ref,
    taps_out_ref,
    delays_ref,
    flags_ref,
    taps_ref,
    raw,
    mix,
    send,
    recv,
    y,
    hi,
    lo,
    raw_sem,
    small_sem,
    send_sem,
    recv_sem,
    halo_sem,
    from_below,
    from_above,
):
    tm = lax.axis_index("tm")
    chan = lax.axis_index("chan")
    nchunk, _, rows, _ = send.shape
    signals = rows // 8
    tiles = signals // 2
    chips = nchan // 2
    chip, core = chan >> 1, chan & 1
    stages = stages_of(nchunk, tiles)
    order = [fc for i, (fc, _, _) in enumerate(stages) if fc not in [s[0] for s in stages[:i]]]

    def around(away):
        return lax.rem(chip + away, chips)

    loads = {
        fc: pltpu.make_async_copy(
            spectra_ref.at[:, :, :, fc * LANES : (fc + 1) * LANES], raw.at[fc], raw_sem.at[fc]
        )
        for fc in order
    }
    loads[order[0]].start()
    barrier = pltpu.get_barrier_semaphore()

    for near in (
        chip * 2 + 1 - core,
        around(1) * 2,
        around(1) * 2 + 1,
        around(chips - 1) * 2,
        around(chips - 1) * 2 + 1,
    ):
        pl.semaphore_signal(barrier, inc=1, device_id={"chan": near})

    @pl.when(tm > 0)
    def _():
        pl.semaphore_signal(barrier, inc=1, device_id={"tm": tm - 1})

    for fc in order[1:]:
        loads[fc].start()

    small = [
        pltpu.make_async_copy(whole, mine, small_sem.at[i])
        for i, (whole, mine) in enumerate(
            ((delays_hbm, delays_ref), (flags_hbm, flags_ref), (taps_hbm, taps_ref))
        )
    ]
    for copy in small:
        copy.start()

    def arrange(fc, pair):
        at = pl.ds(pl.multiple_of(pair * 16, 16), 16)
        part = raw[fc, :, :, at, :].astype(jnp.float32)
        for q in range(2):
            for c in range(2):
                for k in range(4):
                    mix[q, pl.ds(c * 4 + k, signals, stride=8), :] = part[c, k, q * 8 : q * 8 + 8, :]
        for q in range(2):
            send[fc, pair * 2 + q] = mix[q].astype(jnp.bfloat16)

    def push(stage, to):
        fc, first, last = stages[stage]
        at = pl.ds(first * 16, (last - first) * 16)
        pltpu.make_async_remote_copy(
            src_ref=send.at[fc, to, at],
            dst_ref=recv.at[fc, chan, at],
            send_sem=send_sem.at[stage],
            recv_sem=recv_sem.at[stage],
            device_id={"chan": to},
        ).start()

    def keep(stage):
        fc, first, last = stages[stage]
        at = pl.ds(first * 16, (last - first) * 16)
        pltpu.make_async_copy(
            send.at[fc, chan, at], recv.at[fc, chan, at], recv_sem.at[stage]
        ).start()

    def each_chip(work):
        def body(i, carry):
            far = chips // 2 - ((i + 1) >> 1)
            work(around(jnp.where((i & 1) == 0, far, chips - far)))
            return carry

        lax.fori_loop(0, chips - 1, body, 0)

    def as_known(work):
        up, down = around(1) * 2 + core, around(chips - 1) * 2 + core
        last = chips // 2

        def tell_up(d):
            pl.semaphore_signal(from_below.at[d], inc=1, device_id={"chan": up})

        def tell_down(d):
            pl.semaphore_signal(from_above.at[d], inc=1, device_id={"chan": down})

        pl.semaphore_wait(barrier, 5 + jnp.where(tm < ntm - 1, 1, 0))
        tell_up(2)
        tell_down(2)
        work(around(1))
        work(around(chips - 1))

        def body(d, carry):
            pl.semaphore_wait(from_below.at[d], 1)
            tell_up(d + 1)
            pl.semaphore_wait(from_above.at[d], 1)

            @pl.when(d < last - 1)
            def _():
                tell_down(d + 1)

            work(around(d))
            work(around(chips - d))
            return carry

        lax.fori_loop(2, last, body, 0)
        pl.semaphore_wait(from_below.at[last], 1)
        work(around(last))

    def issue(stage):
        fc, first, last = stages[stage]
        fresh = first == 0

        def to_chip(pair):
            if fresh:
                arrange(fc, pair)
            push(stage, pair * 2 + core)
            push(stage, pair * 2 + 1 - core)

        if fresh:
            loads[fc].wait()
        if stage == 0:
            as_known(to_chip)
        else:
            each_chip(to_chip)
        if fresh:
            arrange(fc, chip)
        push(stage, chip * 2 + 1 - core)
        keep(stage)

    def left(stage):
        fc, first, last = stages[stage]
        sent = send.at[fc, 0 : nchan - 1, first * 16 : last * 16]
        pltpu.make_async_copy(sent, sent, send_sem.at[stage]).wait()

    issue(0)
    issue(1)
    for copy in small:
        copy.wait()
    fill_tables(chan, delays_ref, flags_ref, hi, lo)

    @pl.when(tm == 0)
    def _():
        y[:, :, 0:HALO, :] = jnp.zeros((2, signals, HALO, LANES), jnp.float32)

    def transform(stage):
        fc, first, last = stages[stage]
        base = HALO + fc * LANES

        def one_tile(t, carry):
            part = recv[fc, :, pl.ds(pl.multiple_of(t * 16, 16), 16), :]
            z = to_series(part, hi[t], lo[t])
            for p in range(2):
                of = slice(p * LANES, (p + 1) * LANES)
                y[0, t * 2 + p, base : base + LANES, :] = z[of, :LANES]
                y[1, t * 2 + p, base : base + LANES, :] = z[of, LANES:]
            return carry

        lax.fori_loop(first, last, one_tile, 0)

    def fir(stage, begin, end):
        _, first, last = stages[stage]
        sigs = 2 * (last - first)

        def one(i, carry):
            d, s = i // sigs, 2 * first + lax.rem(i, sigs)
            for row in range(begin, end, 64):
                count = min(64, end - row)
                rows_out = filtered(taps_ref, y, (d, s), HALO + row, count)
                out_ref[d, s, row : row + count, :] = rows_out
            return carry

        lax.fori_loop(0, 2 * sigs, one, 0)

    frames = nchunk * LANES
    halo = pltpu.make_async_remote_copy(
        src_ref=y.at[:, :, frames : frames + HALO, :],
        dst_ref=y.at[:, :, 0:HALO, :],
        send_sem=halo_sem.at[0],
        recv_sem=halo_sem.at[1],
        device_id={"tm": lax.rem(tm + 1, ntm)},
    )

    for stage, (fc, first, last) in enumerate(stages):
        if stage + 2 < len(stages):
            left(stage)
            issue(stage + 2)
        if stage == len(stages) - 1:
            table_ref[0], table_ref[1] = hi[first:last], lo[first:last]
            taps_out_ref[...] = taps_ref[...]
            sigs = slice(2 * first, 2 * last)
            edges_ref[0] = y[:, sigs, fc * LANES : fc * LANES + HALO, :]
            after = HALO + (fc + 1) * LANES
            edges_ref[1] = y[:, sigs, after : after + HALO, :]
        arriving = recv.at[fc, :, first * 16 : last * 16]
        pltpu.make_async_copy(arriving, arriving, recv_sem.at[stage]).wait()
        if stage == len(stages) - 1:
            last_ref[...] = recv[fc, :, first * 16 : last * 16, :]
            break
        transform(stage)
        if stage == 0:

            @pl.when(tm < ntm - 1)
            def _():
                halo.start()

        if fc == 0:

            @pl.when(tm > 0)
            def _():
                halo.wait_recv()

        begin = fc * LANES + (HALO if stage == 0 else 0)
        end = (fc + 1) * LANES + (HALO if fc == nchunk - 2 else 0)
        fir(stage, begin, end)

    for stage in range(len(stages) - 2, len(stages)):
        left(stage)

    @pl.when(tm < ntm - 1)
    def _():
        halo.wait_send()


def finish(stage, done_ref, last_ref, table_ref, edges_ref, taps_ref, out_ref, y, result, sem):
    fc, first, last = stage
    _, signals, frames, _ = done_ref.shape
    begin, end = fc * LANES, (fc + 1) * LANES + HALO
    spans = [(s, 0, frames) for s in range(signals) if not 2 * first <= s < 2 * last]
    for s in range(2 * first, 2 * last):
        spans += [(s, 0, begin), (s, end, frames)]
    copies = []
    for s, start, stop in spans:
        for d in range(2):
            at = (d, s, slice(start, stop))
            copies.append(
                pltpu.make_async_copy(done_ref.at[at], out_ref.at[at], sem.at[len(copies)])
            )
            copies[-1].start()
    y[:, :, 0:HALO, :] = edges_ref[0]
    y[:, :, HALO + LANES :, :] = edges_ref[1]
    for t in range(last - first):
        z = to_series(last_ref[:, t * 16 : t * 16 + 16, :], table_ref[0, t], table_ref[1, t])
        for p in range(2):
            of = slice(p * LANES, (p + 1) * LANES)
            y[0, 2 * t + p, HALO : HALO + LANES, :] = z[of, :LANES]
            y[1, 2 * t + p, HALO : HALO + LANES, :] = z[of, LANES:]
    for s in range(2 * (last - first)):
        for d in range(2):
            for row in range(0, end - begin, 48):
                result[d, s, row : row + 48, :] = filtered(taps_ref, y, (d, s), HALO + row, 48)
            at = (d, 2 * first + s, slice(begin, end))
            copies.append(
                pltpu.make_async_copy(result.at[d, s], out_ref.at[at], sem.at[len(copies)])
            )
            copies[-1].start()
    for copy in copies:
        copy.wait()


def per_device(ntm, nchan, spectra, delays, flags, taps):
    parts, chans, sigs, frames = spectra.shape
    signals = sigs // nchan
    nfine = chans * nchan
    nchunk = frames // LANES
    rows = parts * chans * signals
    nstage = len(stages_of(nchunk, signals // 2))
    any_spec = pl.BlockSpec(memory_space=pl.ANY)

    def body(*refs):
        kernel(ntm, nchan, *refs)

    stages = stages_of(nchunk, signals // 2)
    late = stages[-1][2] - stages[-1][1]
    vmem_spec = pl.BlockSpec(memory_space=pltpu.VMEM)
    handed_over = pl.pallas_call(
        body,
        out_shape=[
            pltpu.VMEM((2, signals, frames, nfine), jnp.bfloat16),
            pltpu.VMEM((nchan, 16 * late, LANES), jnp.bfloat16),
            pltpu.VMEM((2, late, 2 * nfine, 2 * nfine), jnp.bfloat16),
            pltpu.VMEM((2, 2, 2 * late, HALO, nfine), jnp.float32),
            pltpu.VMEM(taps.shape, jnp.float32),
        ],
        in_specs=[any_spec] * 4,
        out_specs=[vmem_spec] * 5,
        scratch_shapes=[
            pltpu.SMEM(delays.shape, jnp.int32),
            pltpu.VMEM(flags.shape, jnp.int32),
            pltpu.VMEM(taps.shape, jnp.float32),
            pltpu.VMEM((nchunk, parts, chans, sigs, LANES), jnp.bfloat16),
            pltpu.VMEM((2, rows, LANES), jnp.float32),
            pltpu.VMEM((nchunk, nchan, rows, LANES), jnp.bfloat16),
            pltpu.VMEM((nchunk, nchan, rows, LANES), jnp.bfloat16),
            pltpu.VMEM((2, signals, HALO + frames, nfine), jnp.float32),
            pltpu.VMEM((signals // 2, 2 * nfine, 2 * nfine), jnp.bfloat16),
            pltpu.VMEM((signals // 2, 2 * nfine, 2 * nfine), jnp.bfloat16),
            pltpu.SemaphoreType.DMA((nchunk,)),
            pltpu.SemaphoreType.DMA((3,)),
            pltpu.SemaphoreType.DMA((nstage,)),
            pltpu.SemaphoreType.DMA((nstage,)),
            pltpu.SemaphoreType.DMA((2,)),
            pltpu.SemaphoreType.REGULAR((nchan // 4 + 1,)),
            pltpu.SemaphoreType.REGULAR((nchan // 4 + 1,)),
        ],
        compiler_params=pltpu.CompilerParams(
            collective_id=0, has_side_effects=True, vmem_limit_bytes=20 * 2**20
        ),
        cost_estimate=pl.CostEstimate(
            flops=8 * 2**27, bytes_accessed=4 * 2**20, transcendentals=0
        ),
        name="resynthesis",
    )(*(pltpu.with_memory_space_constraint(x, pltpu.HBM) for x in (spectra, delays, flags, taps)))
    held = [pltpu.with_memory_space_constraint(x, pltpu.VMEM) for x in handed_over]

    def finish_body(*refs):
        finish(stages[-1], *refs)

    return pl.pallas_call(
        finish_body,
        out_shape=jax.ShapeDtypeStruct((2, signals, frames, nfine), jnp.bfloat16),
        in_specs=[vmem_spec] * 5,
        out_specs=any_spec,
        scratch_shapes=[
            pltpu.VMEM((2, 2 * late, HALO + LANES + HALO, nfine), jnp.float32),
            pltpu.VMEM((2, 2 * late, LANES + HALO, nfine), jnp.bfloat16),
            pltpu.SemaphoreType.DMA((2 * signals + 8 * late,)),
        ],
        compiler_params=pltpu.CompilerParams(vmem_limit_bytes=20 * 2**20),
        cost_estimate=pl.CostEstimate(
            flops=2**27, bytes_accessed=2 * 2**20, transcendentals=0
        ),
        name="last_stage",
    )(*held)


def solution(mesh):
    ntm, nchan = mesh.shape["tm"], mesh.shape["chan"]

    def body(spectra, delays, flags, taps):
        return per_device(ntm, nchan, spectra, delays, flags, taps)

    in_specs = (P(None, "chan", None, "tm"), P(), P(), P())
    return jax.shard_map(
        body, mesh=mesh, in_specs=in_specs, out_specs=P(None, "chan", "tm", None), check_vma=False
    )
```

```python
import math

import jax
import jax.numpy as jnp
from jax import lax
from jax.experimental import pallas as pl
from jax.experimental.pallas import tpu as pltpu
from jax.sharding import PartitionSpec as P

TAPS = 12
LANES = 128
HALO = 16


def fill_tables(chan, delays_ref, flags_ref, hi_ref, lo_ref):
    tiles, rows, cols = hi_ref.shape
    nfine = rows // 2
    row = lax.broadcasted_iota(jnp.int32, (rows, cols), 0)
    col = lax.broadcasted_iota(jnp.int32, (rows, cols), 1)
    fine = (row >> 3) * 4 + (row & 3)
    sample = col & (nfine - 1)
    quarter = (((row >> 2) & 1) - (col >> 7)) * (nfine // 4)
    frow = lax.broadcasted_iota(jnp.int32, (rows, nfine), 0)
    fcol = lax.broadcasted_iota(jnp.int32, (rows, nfine), 1)
    spread = (fcol == (frow >> 3) * 4 + (frow & 3)).astype(jnp.float32).astype(jnp.bfloat16)
    kept = jnp.dot(
        spread,
        flags_ref[...].astype(jnp.float32).astype(jnp.bfloat16),
        preferred_element_type=jnp.float32,
    )

    def one_tile(t, carry):
        tile = chan * tiles + t
        delay = delays_ref[tile]
        turn = (fine * (sample - delay) + quarter) & (nfine - 1)
        fold = nfine // 4 - jnp.abs(turn - nfine // 2)
        x = fold.astype(jnp.float32) * (2.0 * math.pi / nfine)
        x2 = x * x
        poly = -1.0 / 39916800.0
        for c in (1.0 / 362880.0, -1.0 / 5040.0, 1.0 / 120.0, -1.0 / 6.0, 1.0):
            poly = poly * x2 + c
        lane = lax.broadcasted_iota(jnp.int32, kept.shape, 1)
        keep = jnp.sum(jnp.where(lane == tile, kept, 0.0), axis=1, keepdims=True)
        table = (poly * x) * (keep * (-1.0 / math.sqrt(nfine)))
        hi = table.astype(jnp.bfloat16)
        hi_ref[t] = hi
        lo_ref[t] = (table - hi.astype(jnp.float32)).astype(jnp.bfloat16)
        return carry

    lax.fori_loop(0, tiles, one_tile, 0)


def to_series(part, hi, lo):
    part = part.astype(jnp.float32)
    count = part.shape[0] * 8
    pols = [part[:, p * 8 : p * 8 + 8, :].reshape(count, LANES) for p in range(2)]
    x = jnp.concatenate(pols, axis=1).astype(jnp.bfloat16)
    dims = (((0,), (0,)), ((), ()))
    z = lax.dot_general(x, hi, dims, preferred_element_type=jnp.float32)
    return z + lax.dot_general(x, lo, dims, preferred_element_type=jnp.float32)


def filtered(taps_ref, series_ref, at, start, count):
    total = None
    for j in range(TAPS):
        term = taps_ref[j : j + 1, :] * series_ref[(*at, pl.ds(start - j, count), slice(None))]
        total = term if total is None else total + term
    return total.astype(jnp.bfloat16)


def pieces_of(nchunk, tiles):
    whole = [(nchunk - 1, 0, tiles)] + [(fc, 0, tiles) for fc in range(nchunk - 2)]
    return whole + [(nchunk - 2, 0, tiles // 2), (nchunk - 2, tiles // 2, tiles)]


def kernel(
    ntm,
    nchan,
    spectra_ref,
    delays_hbm,
    flags_hbm,
    taps_hbm,
    out_ref,
    last_ref,
    table_ref,
    edges_ref,
    taps_out_ref,
    delays_ref,
    flags_ref,
    taps_ref,
    raw,
    mix,
    send,
    recv,
    y,
    hi,
    lo,
    raw_sem,
    small_sem,
    send_sem,
    recv_sem,
    halo_sem,
    from_below,
    from_above,
):
    tm = lax.axis_index("tm")
    chan = lax.axis_index("chan")
    _, length, _ = send.shape
    frames = raw.shape[3]
    nchunk = frames // LANES
    rows = length // nchunk
    signals = rows // 8
    tiles = signals // 2
    chips = nchan // 2
    chip, core = chan >> 1, chan & 1
    pieces = pieces_of(nchunk, tiles)
    row_of = {fc: i * rows for i, fc in enumerate(dict.fromkeys(fc for fc, _, _ in pieces))}
    late = 16 * (pieces[-1][2] - pieces[-1][1])
    stages = [(0, length - late), (length - late, late)]

    def around(away):
        return lax.rem(chip + away, chips)

    def load(pair):
        at = (slice(None), slice(None), pl.ds(pl.multiple_of(pair * 16, 16), 16), slice(None))
        return pltpu.make_async_copy(spectra_ref.at[at], raw.at[at], raw_sem.at[pair])

    load(around(1)).start()
    load(around(chips - 1)).start()
    barrier = pltpu.get_barrier_semaphore()

    for near in (
        chip * 2 + 1 - core,
        around(1) * 2,
        around(1) * 2 + 1,
        around(chips - 1) * 2,
        around(chips - 1) * 2 + 1,
    ):
        pl.semaphore_signal(barrier, inc=1, device_id={"chan": near})

    @pl.when(tm > 0)
    def _():
        pl.semaphore_signal(barrier, inc=1, device_id={"tm": tm - 1})

    def load_pairs(d, carry):
        load(around(d)).start()
        load(around(chips - d)).start()
        return carry

    lax.fori_loop(2, chips // 2, load_pairs, 0)
    load(around(chips // 2)).start()
    load(chip).start()
    small = [
        pltpu.make_async_copy(whole, mine, small_sem.at[i])
        for i, (whole, mine) in enumerate(
            ((delays_hbm, delays_ref), (flags_hbm, flags_ref), (taps_hbm, taps_ref))
        )
    ]
    for copy in small:
        copy.start()

    def arrange(pair):
        load(pair).wait()
        at = pl.ds(pl.multiple_of(pair * 16, 16), 16)
        for fc, row in row_of.items():
            part = raw[:, :, at, fc * LANES : (fc + 1) * LANES].astype(jnp.float32)
            for q in range(2):
                for c in range(2):
                    for k in range(4):
                        mix[fc, q, pl.ds(c * 4 + k, signals, stride=8), :] = part[
                            c, k, q * 8 : q * 8 + 8, :
                        ]
            for q in range(2):
                send[pair * 2 + q, row : row + rows, :] = mix[fc, q].astype(jnp.bfloat16)

    def push(stage, to):
        at = pl.ds(*stages[stage])
        pltpu.make_async_remote_copy(
            src_ref=send.at[to, at],
            dst_ref=recv.at[chan, at],
            send_sem=send_sem.at[stage],
            recv_sem=recv_sem.at[stage],
            device_id={"chan": to},
        ).start()

    def keep(stage):
        at = pl.ds(*stages[stage])
        pltpu.make_async_copy(send.at[chan, at], recv.at[chan, at], recv_sem.at[stage]).start()

    def each_chip(work):
        def body(i, carry):
            far = chips // 2 - ((i + 1) >> 1)
            work(around(jnp.where((i & 1) == 0, far, chips - far)))
            return carry

        lax.fori_loop(0, chips - 1, body, 0)

    def as_known(work):
        up, down = around(1) * 2 + core, around(chips - 1) * 2 + core
        last = chips // 2

        def tell_up(d):
            pl.semaphore_signal(from_below.at[d], inc=1, device_id={"chan": up})

        def tell_down(d):
            pl.semaphore_signal(from_above.at[d], inc=1, device_id={"chan": down})

        pl.semaphore_wait(barrier, 5 + jnp.where(tm < ntm - 1, 1, 0))
        tell_up(2)
        tell_down(2)
        work(around(1))
        work(around(chips - 1))

        def body(d, carry):
            pl.semaphore_wait(from_below.at[d], 1)
            tell_up(d + 1)
            pl.semaphore_wait(from_above.at[d], 1)

            @pl.when(d < last - 1)
            def _():
                tell_down(d + 1)

            work(around(d))
            work(around(chips - d))
            return carry

        lax.fori_loop(2, last, body, 0)
        pl.semaphore_wait(from_below.at[last], 1)
        work(around(last))

    def issue(stage):
        def to_chip(pair):
            if stage == 0:
                arrange(pair)
            push(stage, pair * 2 + core)
            push(stage, pair * 2 + 1 - core)

        if stage == 0:
            as_known(to_chip)
            arrange(chip)
        else:
            each_chip(to_chip)
        push(stage, chip * 2 + 1 - core)
        keep(stage)

    def left(stage):
        sent = send.at[0 : nchan - 1, pl.ds(*stages[stage])]
        pltpu.make_async_copy(sent, sent, send_sem.at[stage]).wait()

    def arrived(stage):
        arriving = recv.at[:, pl.ds(*stages[stage])]
        pltpu.make_async_copy(arriving, arriving, recv_sem.at[stage]).wait()

    issue(0)
    issue(1)
    for copy in small:
        copy.wait()
    fill_tables(chan, delays_ref, flags_ref, hi, lo)

    @pl.when(tm == 0)
    def _():
        y[:, :, 0:HALO, :] = jnp.zeros((2, signals, HALO, LANES), jnp.float32)

    def transform(fc, first, last):
        base = HALO + fc * LANES

        def one_tile(t, carry):
            at = pl.ds(pl.multiple_of(row_of[fc] + t * 16, 16), 16)
            z = to_series(recv[:, at, :], hi[t], lo[t])
            for p in range(2):
                of = slice(p * LANES, (p + 1) * LANES)
                y[0, t * 2 + p, base : base + LANES, :] = z[of, :LANES]
                y[1, t * 2 + p, base : base + LANES, :] = z[of, LANES:]
            return carry

        lax.fori_loop(first, last, one_tile, 0)

    def fir(first, last, begin, end):
        sigs = 2 * (last - first)

        def one(i, carry):
            d, s = i // sigs, 2 * first + lax.rem(i, sigs)
            for row in range(begin, end, 64):
                count = min(64, end - row)
                rows_out = filtered(taps_ref, y, (d, s), HALO + row, count)
                out_ref[d, s, row : row + count, :] = rows_out
            return carry

        lax.fori_loop(0, 2 * sigs, one, 0)

    halo = pltpu.make_async_remote_copy(
        src_ref=y.at[:, :, frames : frames + HALO, :],
        dst_ref=y.at[:, :, 0:HALO, :],
        send_sem=halo_sem.at[0],
        recv_sem=halo_sem.at[1],
        device_id={"tm": lax.rem(tm + 1, ntm)},
    )

    arrived(0)
    for i, piece in enumerate(pieces[:-1]):
        transform(*piece)
        if i == 0:

            @pl.when(tm < ntm - 1)
            def _():
                halo.start()

    def span(fc, first, last):
        begin = fc * LANES + (HALO if fc == nchunk - 1 else 0)
        fir(first, last, begin, (fc + 1) * LANES + (HALO if fc == nchunk - 2 else 0))

    for piece in pieces[:-1]:
        if piece[0] > 0:
            span(*piece)

    @pl.when(tm > 0)
    def _():
        halo.wait_recv()

    for piece in pieces[:-1]:
        if piece[0] == 0:
            span(*piece)

    fc, first, last = pieces[-1]
    table_ref[0], table_ref[1] = hi[first:last], lo[first:last]
    taps_out_ref[...] = taps_ref[...]
    sigs = slice(2 * first, 2 * last)
    edges_ref[0] = y[:, sigs, fc * LANES : fc * LANES + HALO, :]
    after = HALO + (fc + 1) * LANES
    edges_ref[1] = y[:, sigs, after : after + HALO, :]
    arrived(1)
    last_ref[...] = recv[:, length - late :, :]
    left(0)
    left(1)

    @pl.when(tm < ntm - 1)
    def _():
        halo.wait_send()


def finish(piece, done_ref, last_ref, table_ref, edges_ref, taps_ref, out_ref, y, result, sem):
    fc, first, last = piece
    _, signals, frames, _ = done_ref.shape
    begin, end = fc * LANES, (fc + 1) * LANES + HALO
    spans = [(s, 0, frames) for s in range(signals) if not 2 * first <= s < 2 * last]
    for s in range(2 * first, 2 * last):
        spans += [(s, 0, begin), (s, end, frames)]
    copies = []
    for s, start, stop in spans:
        for d in range(2):
            at = (d, s, slice(start, stop))
            copies.append(
                pltpu.make_async_copy(done_ref.at[at], out_ref.at[at], sem.at[len(copies)])
            )
            copies[-1].start()
    y[:, :, 0:HALO, :] = edges_ref[0]
    y[:, :, HALO + LANES :, :] = edges_ref[1]
    for t in range(last - first):
        z = to_series(last_ref[:, t * 16 : t * 16 + 16, :], table_ref[0, t], table_ref[1, t])
        for p in range(2):
            of = slice(p * LANES, (p + 1) * LANES)
            y[0, 2 * t + p, HALO : HALO + LANES, :] = z[of, :LANES]
            y[1, 2 * t + p, HALO : HALO + LANES, :] = z[of, LANES:]
    for s in range(2 * (last - first)):
        for d in range(2):
            for row in range(0, end - begin, 48):
                result[d, s, row : row + 48, :] = filtered(taps_ref, y, (d, s), HALO + row, 48)
            at = (d, 2 * first + s, slice(begin, end))
            copies.append(
                pltpu.make_async_copy(result.at[d, s], out_ref.at[at], sem.at[len(copies)])
            )
            copies[-1].start()
    for copy in copies:
        copy.wait()


def per_device(ntm, nchan, spectra, delays, flags, taps):
    parts, chans, sigs, frames = spectra.shape
    signals = sigs // nchan
    nfine = chans * nchan
    nchunk = frames // LANES
    rows = parts * chans * signals
    any_spec = pl.BlockSpec(memory_space=pl.ANY)

    def body(*refs):
        kernel(ntm, nchan, *refs)

    pieces = pieces_of(nchunk, signals // 2)
    late = pieces[-1][2] - pieces[-1][1]
    vmem_spec = pl.BlockSpec(memory_space=pltpu.VMEM)
    handed_over = pl.pallas_call(
        body,
        out_shape=[
            pltpu.VMEM((2, signals, frames, nfine), jnp.bfloat16),
            pltpu.VMEM((nchan, 16 * late, LANES), jnp.bfloat16),
            pltpu.VMEM((2, late, 2 * nfine, 2 * nfine), jnp.bfloat16),
            pltpu.VMEM((2, 2, 2 * late, HALO, nfine), jnp.float32),
            pltpu.VMEM(taps.shape, jnp.float32),
        ],
        in_specs=[any_spec] * 4,
        out_specs=[vmem_spec] * 5,
        scratch_shapes=[
            pltpu.SMEM(delays.shape, jnp.int32),
            pltpu.VMEM(flags.shape, jnp.int32),
            pltpu.VMEM(taps.shape, jnp.float32),
            pltpu.VMEM(spectra.shape, jnp.bfloat16),
            pltpu.VMEM((nchunk, 2, rows, LANES), jnp.float32),
            pltpu.VMEM((nchan, nchunk * rows, LANES), jnp.bfloat16),
            pltpu.VMEM((nchan, nchunk * rows, LANES), jnp.bfloat16),
            pltpu.VMEM((2, signals, HALO + frames, nfine), jnp.float32),
            pltpu.VMEM((signals // 2, 2 * nfine, 2 * nfine), jnp.bfloat16),
            pltpu.VMEM((signals // 2, 2 * nfine, 2 * nfine), jnp.bfloat16),
            pltpu.SemaphoreType.DMA((nchan // 2,)),
            pltpu.SemaphoreType.DMA((3,)),
            pltpu.SemaphoreType.DMA((2,)),
            pltpu.SemaphoreType.DMA((2,)),
            pltpu.SemaphoreType.DMA((2,)),
            pltpu.SemaphoreType.REGULAR((nchan // 4 + 1,)),
            pltpu.SemaphoreType.REGULAR((nchan // 4 + 1,)),
        ],
        compiler_params=pltpu.CompilerParams(
            collective_id=0, has_side_effects=True, vmem_limit_bytes=20 * 2**20
        ),
        cost_estimate=pl.CostEstimate(
            flops=8 * 2**27, bytes_accessed=4 * 2**20, transcendentals=0
        ),
        name="resynthesis",
    )(*(pltpu.with_memory_space_constraint(x, pltpu.HBM) for x in (spectra, delays, flags, taps)))
    held = [pltpu.with_memory_space_constraint(x, pltpu.VMEM) for x in handed_over]

    def finish_body(*refs):
        finish(pieces[-1], *refs)

    return pl.pallas_call(
        finish_body,
        out_shape=jax.ShapeDtypeStruct((2, signals, frames, nfine), jnp.bfloat16),
        in_specs=[vmem_spec] * 5,
        out_specs=any_spec,
        scratch_shapes=[
            pltpu.VMEM((2, 2 * late, HALO + LANES + HALO, nfine), jnp.float32),
            pltpu.VMEM((2, 2 * late, LANES + HALO, nfine), jnp.bfloat16),
            pltpu.SemaphoreType.DMA((2 * signals + 8 * late,)),
        ],
        compiler_params=pltpu.CompilerParams(vmem_limit_bytes=20 * 2**20),
        cost_estimate=pl.CostEstimate(
            flops=2**27, bytes_accessed=2 * 2**20, transcendentals=0
        ),
        name="last_stage",
    )(*held)


def solution(mesh):
    ntm, nchan = mesh.shape["tm"], mesh.shape["chan"]

    def body(spectra, delays, flags, taps):
        return per_device(ntm, nchan, spectra, delays, flags, taps)

    in_specs = (P(None, "chan", None, "tm"), P(), P(), P())
    return jax.shard_map(
        body, mesh=mesh, in_specs=in_specs, out_specs=P(None, "chan", "tm", None), check_vma=False
    )
```

```python
import math

import jax
import jax.numpy as jnp
from jax import lax
from jax.experimental import pallas as pl
from jax.experimental.pallas import tpu as pltpu
from jax.sharding import PartitionSpec as P

TAPS = 12
LANES = 128
HALO = 16


def fill_tables(chan, delays_ref, flags_ref, hi_ref, lo_ref):
    tiles, rows, cols = hi_ref.shape
    nfine = rows // 2
    row = lax.broadcasted_iota(jnp.int32, (rows, cols), 0)
    col = lax.broadcasted_iota(jnp.int32, (rows, cols), 1)
    fine = (row >> 3) * 4 + (row & 3)
    sample = col & (nfine - 1)
    quarter = (((row >> 2) & 1) - (col >> 7)) * (nfine // 4)
    frow = lax.broadcasted_iota(jnp.int32, (rows, nfine), 0)
    fcol = lax.broadcasted_iota(jnp.int32, (rows, nfine), 1)
    spread = (fcol == (frow >> 3) * 4 + (frow & 3)).astype(jnp.float32).astype(jnp.bfloat16)
    kept = jnp.dot(
        spread,
        flags_ref[...].astype(jnp.float32).astype(jnp.bfloat16),
        preferred_element_type=jnp.float32,
    )

    def one_tile(t, carry):
        tile = chan * tiles + t
        delay = delays_ref[tile]
        turn = (fine * (sample - delay) + quarter) & (nfine - 1)
        fold = nfine // 4 - jnp.abs(turn - nfine // 2)
        x = fold.astype(jnp.float32) * (2.0 * math.pi / nfine)
        x2 = x * x
        poly = -1.0 / 39916800.0
        for c in (1.0 / 362880.0, -1.0 / 5040.0, 1.0 / 120.0, -1.0 / 6.0, 1.0):
            poly = poly * x2 + c
        lane = lax.broadcasted_iota(jnp.int32, kept.shape, 1)
        keep = jnp.sum(jnp.where(lane == tile, kept, 0.0), axis=1, keepdims=True)
        table = (poly * x) * (keep * (-1.0 / math.sqrt(nfine)))
        hi = table.astype(jnp.bfloat16)
        hi_ref[t] = hi
        lo_ref[t] = (table - hi.astype(jnp.float32)).astype(jnp.bfloat16)
        return carry

    lax.fori_loop(0, tiles, one_tile, 0)


def to_series(part, hi, lo):
    part = part.astype(jnp.float32)
    count = part.shape[0] * 8
    pols = [part[:, p * 8 : p * 8 + 8, :].reshape(count, LANES) for p in range(2)]
    x = jnp.concatenate(pols, axis=1).astype(jnp.bfloat16)
    dims = (((0,), (0,)), ((), ()))
    z = lax.dot_general(x, hi, dims, preferred_element_type=jnp.float32)
    return z + lax.dot_general(x, lo, dims, preferred_element_type=jnp.float32)


def filtered(taps_ref, series_ref, at, start, count):
    total = None
    for j in range(TAPS):
        term = taps_ref[j : j + 1, :] * series_ref[(*at, pl.ds(start - j, count), slice(None))]
        total = term if total is None else total + term
    return total.astype(jnp.bfloat16)


def stages_of(nchunk, tiles):
    half = tiles // 2
    bulk = [(nchunk - 1, half, tiles)] + [(fc, 0, tiles) for fc in range(nchunk - 2)]
    bulk += [(nchunk - 2, 0, half)]
    return [[(nchunk - 1, 0, half)], bulk, [(nchunk - 2, half, tiles)]]


def kernel(
    ntm,
    nchan,
    spectra_ref,
    delays_hbm,
    flags_hbm,
    taps_hbm,
    out_ref,
    last_ref,
    table_ref,
    edges_ref,
    taps_out_ref,
    delays_ref,
    flags_ref,
    taps_ref,
    raw,
    mix,
    send,
    recv,
    y,
    hi,
    lo,
    raw_sem,
    small_sem,
    send_sem,
    recv_sem,
    halo_sem,
    from_below,
    from_above,
):
    tm = lax.axis_index("tm")
    chan = lax.axis_index("chan")
    _, length, _ = send.shape
    frames = raw.shape[3]
    nchunk = frames // LANES
    rows = length // nchunk
    signals = rows // 8
    tiles = signals // 2
    chips = nchan // 2
    chip, core = chan >> 1, chan & 1
    plan = stages_of(nchunk, tiles)
    row_of = {}
    stages, row = [], 0
    for held in plan:
        begin = row
        for fc, first, last in held:
            row_of.setdefault(fc, row)
            row += 16 * (last - first)
        stages.append((begin, row - begin))

    def around(away):
        return lax.rem(chip + away, chips)

    def load(pair):
        at = (slice(None), slice(None), pl.ds(pl.multiple_of(pair * 16, 16), 16), slice(None))
        return pltpu.make_async_copy(spectra_ref.at[at], raw.at[at], raw_sem.at[pair])

    load(around(1)).start()
    load(around(chips - 1)).start()
    barrier = pltpu.get_barrier_semaphore()

    for near in (
        chip * 2 + 1 - core,
        around(1) * 2,
        around(1) * 2 + 1,
        around(chips - 1) * 2,
        around(chips - 1) * 2 + 1,
    ):
        pl.semaphore_signal(barrier, inc=1, device_id={"chan": near})

    @pl.when(tm > 0)
    def _():
        pl.semaphore_signal(barrier, inc=1, device_id={"tm": tm - 1})

    def load_pairs(d, carry):
        load(around(d)).start()
        load(around(chips - d)).start()
        return carry

    lax.fori_loop(2, chips // 2, load_pairs, 0)
    load(around(chips // 2)).start()
    load(chip).start()
    small = [
        pltpu.make_async_copy(whole, mine, small_sem.at[i])
        for i, (whole, mine) in enumerate(
            ((delays_hbm, delays_ref), (flags_hbm, flags_ref), (taps_hbm, taps_ref))
        )
    ]
    for copy in small:
        copy.start()

    def arrange(pair, chunks):
        at = pl.ds(pl.multiple_of(pair * 16, 16), 16)
        for fc in chunks:
            row = row_of[fc]
            part = raw[:, :, at, fc * LANES : (fc + 1) * LANES].astype(jnp.float32)
            for q in range(2):
                for c in range(2):
                    for k in range(4):
                        mix[fc, q, pl.ds(c * 4 + k, signals, stride=8), :] = part[
                            c, k, q * 8 : q * 8 + 8, :
                        ]
            for q in range(2):
                send[pair * 2 + q, row : row + rows, :] = mix[fc, q].astype(jnp.bfloat16)

    def push(stage, to, sem=None):
        at = pl.ds(*stages[stage])
        pltpu.make_async_remote_copy(
            src_ref=send.at[to, at],
            dst_ref=recv.at[chan, at],
            send_sem=send_sem.at[stage if sem is None else sem],
            recv_sem=recv_sem.at[stage],
            device_id={"chan": to},
        ).start()

    def keep(stage):
        at = pl.ds(*stages[stage])
        pltpu.make_async_copy(send.at[chan, at], recv.at[chan, at], recv_sem.at[stage]).start()

    def each_chip(work, begin, end):
        def body(i, carry):
            far = chips // 2 - ((i + 1) >> 1)
            work(around(jnp.where((i & 1) == 0, far, chips - far)))
            return carry

        lax.fori_loop(begin, end, body, 0)

    def as_known(work):
        up, down = around(1) * 2 + core, around(chips - 1) * 2 + core
        last = chips // 2

        def tell_up(d):
            pl.semaphore_signal(from_below.at[d], inc=1, device_id={"chan": up})

        def tell_down(d):
            pl.semaphore_signal(from_above.at[d], inc=1, device_id={"chan": down})

        pl.semaphore_wait(barrier, 5 + jnp.where(tm < ntm - 1, 1, 0))
        tell_up(2)
        tell_down(2)
        work(around(1))
        work(around(chips - 1))

        def body(d, carry):
            pl.semaphore_wait(from_below.at[d], 1)
            tell_up(d + 1)
            pl.semaphore_wait(from_above.at[d], 1)

            @pl.when(d < last - 1)
            def _():
                tell_down(d + 1)

            work(around(d))
            work(around(chips - d))
            return carry

        lax.fori_loop(2, last, body, 0)
        pl.semaphore_wait(from_below.at[last], 1)
        work(around(last))

    early, farther = plan[0][0][0], chips // 2 - 1
    others = [fc for fc in row_of if fc != early]

    def push_chip(stage, pair, sem=None):
        push(stage, pair * 2 + core, sem)
        push(stage, pair * 2 + 1 - core, sem)

    def push_own(stage):
        push(stage, chip * 2 + 1 - core)
        keep(stage)

    def start_chip(pair):
        load(pair).wait()
        arrange(pair, [early])
        push_chip(0, pair)

    def far_chip(pair):
        arrange(pair, others)
        push_chip(1, pair, 3)

    def near_chip(pair):
        arrange(pair, others)
        push_chip(1, pair)

    def left(stage, count, sem=None):
        sent = send.at[0:count, pl.ds(*stages[stage])]
        pltpu.make_async_copy(sent, sent, send_sem.at[stage if sem is None else sem]).wait()

    def arrived(stage):
        arriving = recv.at[:, pl.ds(*stages[stage])]
        pltpu.make_async_copy(arriving, arriving, recv_sem.at[stage]).wait()

    as_known(start_chip)
    load(chip).wait()
    arrange(chip, row_of)
    push_own(0)
    each_chip(far_chip, 0, farther)
    each_chip(near_chip, farther, chips - 1)
    push_own(1)
    for copy in small:
        copy.wait()
    fill_tables(chan, delays_ref, flags_ref, hi, lo)

    @pl.when(tm == 0)
    def _():
        y[:, :, 0:HALO, :] = jnp.zeros((2, signals, HALO, LANES), jnp.float32)

    def transform(fc, first, last):
        base = HALO + fc * LANES

        def one_tile(t, carry):
            at = pl.ds(pl.multiple_of(row_of[fc] + t * 16, 16), 16)
            z = to_series(recv[:, at, :], hi[t], lo[t])
            for p in range(2):
                of = slice(p * LANES, (p + 1) * LANES)
                y[0, t * 2 + p, base : base + LANES, :] = z[of, :LANES]
                y[1, t * 2 + p, base : base + LANES, :] = z[of, LANES:]
            return carry

        lax.fori_loop(first, last, one_tile, 0)

    def fir(first, last, begin, end):
        sigs = 2 * (last - first)

        def one(i, carry):
            d, s = i // sigs, 2 * first + lax.rem(i, sigs)
            for row in range(begin, end, 64):
                count = min(64, end - row)
                rows_out = filtered(taps_ref, y, (d, s), HALO + row, count)
                out_ref[d, s, row : row + count, :] = rows_out
            return carry

        lax.fori_loop(0, 2 * sigs, one, 0)

    halo = pltpu.make_async_remote_copy(
        src_ref=y.at[:, :, frames : frames + HALO, :],
        dst_ref=y.at[:, :, 0:HALO, :],
        send_sem=halo_sem.at[0],
        recv_sem=halo_sem.at[1],
        device_id={"tm": lax.rem(tm + 1, ntm)},
    )

    def span(fc, first, last):
        begin = fc * LANES + (HALO if fc == nchunk - 1 else 0)
        fir(first, last, begin, (fc + 1) * LANES + (HALO if fc == nchunk - 2 else 0))

    arrived(0)
    for piece in plan[0]:
        transform(*piece)
        span(*piece)
    left(1, 2 * farther, 3)
    each_chip(lambda pair: push_chip(2, pair), 0, chips - 1)
    push_own(2)
    arrived(1)
    for i, piece in enumerate(plan[1]):
        transform(*piece)
        if i == 0:

            @pl.when(tm < ntm - 1)
            def _():
                halo.start()

    for piece in plan[1]:
        if piece[0] > 0:
            span(*piece)

    @pl.when(tm > 0)
    def _():
        halo.wait_recv()

    for piece in plan[1]:
        if piece[0] == 0:
            span(*piece)

    ((fc, first, last),) = plan[2]
    table_ref[0], table_ref[1] = hi[first:last], lo[first:last]
    taps_out_ref[...] = taps_ref[...]
    sigs = slice(2 * first, 2 * last)
    edges_ref[0] = y[:, sigs, fc * LANES : fc * LANES + HALO, :]
    after = HALO + (fc + 1) * LANES
    edges_ref[1] = y[:, sigs, after : after + HALO, :]
    left(0, nchan - 1)
    left(1, nchan - 1 - 2 * farther)
    arrived(2)
    last_ref[...] = recv[:, pl.ds(*stages[2]), :]
    left(2, nchan - 1)

    @pl.when(tm < ntm - 1)
    def _():
        halo.wait_send()


def finish(piece, done_ref, last_ref, table_ref, edges_ref, taps_ref, out_ref, y, result, sem):
    fc, first, last = piece
    _, signals, frames, _ = done_ref.shape
    begin, end = fc * LANES, (fc + 1) * LANES + HALO
    spans = [(s, 0, frames) for s in range(signals) if not 2 * first <= s < 2 * last]
    for s in range(2 * first, 2 * last):
        spans += [(s, 0, begin), (s, end, frames)]
    copies = []
    for s, start, stop in spans:
        for d in range(2):
            at = (d, s, slice(start, stop))
            copies.append(
                pltpu.make_async_copy(done_ref.at[at], out_ref.at[at], sem.at[len(copies)])
            )
            copies[-1].start()
    y[:, :, 0:HALO, :] = edges_ref[0]
    y[:, :, HALO + LANES :, :] = edges_ref[1]
    for t in range(last - first):
        z = to_series(last_ref[:, t * 16 : t * 16 + 16, :], table_ref[0, t], table_ref[1, t])
        for p in range(2):
            of = slice(p * LANES, (p + 1) * LANES)
            y[0, 2 * t + p, HALO : HALO + LANES, :] = z[of, :LANES]
            y[1, 2 * t + p, HALO : HALO + LANES, :] = z[of, LANES:]
    for s in range(2 * (last - first)):
        for d in range(2):
            for row in range(0, end - begin, 48):
                result[d, s, row : row + 48, :] = filtered(taps_ref, y, (d, s), HALO + row, 48)
            at = (d, 2 * first + s, slice(begin, end))
            copies.append(
                pltpu.make_async_copy(result.at[d, s], out_ref.at[at], sem.at[len(copies)])
            )
            copies[-1].start()
    for copy in copies:
        copy.wait()


def per_device(ntm, nchan, spectra, delays, flags, taps):
    parts, chans, sigs, frames = spectra.shape
    signals = sigs // nchan
    nfine = chans * nchan
    nchunk = frames // LANES
    rows = parts * chans * signals
    any_spec = pl.BlockSpec(memory_space=pl.ANY)

    def body(*refs):
        kernel(ntm, nchan, *refs)

    final = stages_of(nchunk, signals // 2)[-1][0]
    late = final[2] - final[1]
    vmem_spec = pl.BlockSpec(memory_space=pltpu.VMEM)
    handed_over = pl.pallas_call(
        body,
        out_shape=[
            pltpu.VMEM((2, signals, frames, nfine), jnp.bfloat16),
            pltpu.VMEM((nchan, 16 * late, LANES), jnp.bfloat16),
            pltpu.VMEM((2, late, 2 * nfine, 2 * nfine), jnp.bfloat16),
            pltpu.VMEM((2, 2, 2 * late, HALO, nfine), jnp.float32),
            pltpu.VMEM(taps.shape, jnp.float32),
        ],
        in_specs=[any_spec] * 4,
        out_specs=[vmem_spec] * 5,
        scratch_shapes=[
            pltpu.SMEM(delays.shape, jnp.int32),
            pltpu.VMEM(flags.shape, jnp.int32),
            pltpu.VMEM(taps.shape, jnp.float32),
            pltpu.VMEM(spectra.shape, jnp.bfloat16),
            pltpu.VMEM((nchunk, 2, rows, LANES), jnp.float32),
            pltpu.VMEM((nchan, nchunk * rows, LANES), jnp.bfloat16),
            pltpu.VMEM((nchan, nchunk * rows, LANES), jnp.bfloat16),
            pltpu.VMEM((2, signals, HALO + frames, nfine), jnp.float32),
            pltpu.VMEM((signals // 2, 2 * nfine, 2 * nfine), jnp.bfloat16),
            pltpu.VMEM((signals // 2, 2 * nfine, 2 * nfine), jnp.bfloat16),
            pltpu.SemaphoreType.DMA((nchan // 2,)),
            pltpu.SemaphoreType.DMA((3,)),
            pltpu.SemaphoreType.DMA((4,)),
            pltpu.SemaphoreType.DMA((3,)),
            pltpu.SemaphoreType.DMA((2,)),
            pltpu.SemaphoreType.REGULAR((nchan // 4 + 1,)),
            pltpu.SemaphoreType.REGULAR((nchan // 4 + 1,)),
        ],
        compiler_params=pltpu.CompilerParams(
            collective_id=0, has_side_effects=True, vmem_limit_bytes=20 * 2**20
        ),
        cost_estimate=pl.CostEstimate(
            flops=8 * 2**27, bytes_accessed=4 * 2**20, transcendentals=0
        ),
        name="resynthesis",
    )(*(pltpu.with_memory_space_constraint(x, pltpu.HBM) for x in (spectra, delays, flags, taps)))
    held = [pltpu.with_memory_space_constraint(x, pltpu.VMEM) for x in handed_over]

    def finish_body(*refs):
        finish(final, *refs)

    return pl.pallas_call(
        finish_body,
        out_shape=jax.ShapeDtypeStruct((2, signals, frames, nfine), jnp.bfloat16),
        in_specs=[vmem_spec] * 5,
        out_specs=any_spec,
        scratch_shapes=[
            pltpu.VMEM((2, 2 * late, HALO + LANES + HALO, nfine), jnp.float32),
            pltpu.VMEM((2, 2 * late, LANES + HALO, nfine), jnp.bfloat16),
            pltpu.SemaphoreType.DMA((2 * signals + 8 * late,)),
        ],
        compiler_params=pltpu.CompilerParams(vmem_limit_bytes=20 * 2**20),
        cost_estimate=pl.CostEstimate(
            flops=2**27, bytes_accessed=2 * 2**20, transcendentals=0
        ),
        name="last_stage",
    )(*held)


def solution(mesh):
    ntm, nchan = mesh.shape["tm"], mesh.shape["chan"]

    def body(spectra, delays, flags, taps):
        return per_device(ntm, nchan, spectra, delays, flags, taps)

    in_specs = (P(None, "chan", None, "tm"), P(), P(), P())
    return jax.shard_map(
        body, mesh=mesh, in_specs=in_specs, out_specs=P(None, "chan", "tm", None), check_vma=False
    )
```

```python
import math

import jax
import jax.numpy as jnp
from jax import lax
from jax.experimental import pallas as pl
from jax.experimental.pallas import tpu as pltpu
from jax.sharding import PartitionSpec as P

TAPS = 12
LANES = 128
HALO = 16


def fill_tables(chan, delays_ref, flags_ref, hi_ref, lo_ref):
    tiles, rows, cols = hi_ref.shape
    nfine = rows // 2
    row = lax.broadcasted_iota(jnp.int32, (rows, cols), 0)
    col = lax.broadcasted_iota(jnp.int32, (rows, cols), 1)
    fine = (row >> 3) * 4 + (row & 3)
    sample = col & (nfine - 1)
    quarter = (((row >> 2) & 1) - (col >> 7)) * (nfine // 4)
    frow = lax.broadcasted_iota(jnp.int32, (rows, nfine), 0)
    fcol = lax.broadcasted_iota(jnp.int32, (rows, nfine), 1)
    spread = (fcol == (frow >> 3) * 4 + (frow & 3)).astype(jnp.float32).astype(jnp.bfloat16)
    kept = jnp.dot(
        spread,
        flags_ref[...].astype(jnp.float32).astype(jnp.bfloat16),
        preferred_element_type=jnp.float32,
    )

    def one_tile(t, carry):
        tile = chan * tiles + t
        delay = delays_ref[tile]
        turn = (fine * (sample - delay) + quarter) & (nfine - 1)
        fold = nfine // 4 - jnp.abs(turn - nfine // 2)
        x = fold.astype(jnp.float32) * (2.0 * math.pi / nfine)
        x2 = x * x
        poly = -1.0 / 39916800.0
        for c in (1.0 / 362880.0, -1.0 / 5040.0, 1.0 / 120.0, -1.0 / 6.0, 1.0):
            poly = poly * x2 + c
        lane = lax.broadcasted_iota(jnp.int32, kept.shape, 1)
        keep = jnp.sum(jnp.where(lane == tile, kept, 0.0), axis=1, keepdims=True)
        table = (poly * x) * (keep * (-1.0 / math.sqrt(nfine)))
        hi = table.astype(jnp.bfloat16)
        hi_ref[t] = hi
        lo_ref[t] = (table - hi.astype(jnp.float32)).astype(jnp.bfloat16)
        return carry

    lax.fori_loop(0, tiles, one_tile, 0)


def to_series(part, hi, lo):
    part = part.astype(jnp.float32)
    count = part.shape[0] * 8
    pols = [part[:, p * 8 : p * 8 + 8, :].reshape(count, LANES) for p in range(2)]
    x = jnp.concatenate(pols, axis=1).astype(jnp.bfloat16)
    dims = (((0,), (0,)), ((), ()))
    z = lax.dot_general(x, hi, dims, preferred_element_type=jnp.float32)
    return z + lax.dot_general(x, lo, dims, preferred_element_type=jnp.float32)


def filtered(taps_ref, series_ref, at, start, count):
    total = None
    for j in range(TAPS):
        term = taps_ref[j : j + 1, :] * series_ref[(*at, pl.ds(start - j, count), slice(None))]
        total = term if total is None else total + term
    return total.astype(jnp.bfloat16)


def stages_of(nchunk, tiles):
    half = tiles // 2
    bulk = [(nchunk - 1, half, tiles)] + [(fc, 0, tiles) for fc in range(nchunk - 2)]
    bulk += [(nchunk - 2, 0, half)]
    return [[(nchunk - 1, 0, half)], bulk, [(nchunk - 2, half, tiles)]]


def kernel(
    ntm,
    nchan,
    spectra_ref,
    delays_hbm,
    flags_hbm,
    taps_hbm,
    out_ref,
    last_ref,
    table_ref,
    edges_ref,
    taps_out_ref,
    delays_ref,
    flags_ref,
    taps_ref,
    raw,
    mix,
    send,
    recv,
    y,
    hi,
    lo,
    raw_sem,
    small_sem,
    send_sem,
    recv_sem,
    halo_sem,
    from_below,
    from_above,
):
    tm = lax.axis_index("tm")
    chan = lax.axis_index("chan")
    _, length, _ = send.shape
    frames = raw.shape[3]
    nchunk = frames // LANES
    rows = length // nchunk
    signals = rows // 8
    tiles = signals // 2
    chips = nchan // 2
    chip, core = chan >> 1, chan & 1
    plan = stages_of(nchunk, tiles)
    row_of = {}
    stages, row = [], 0
    for held in plan:
        begin = row
        for fc, first, last in held:
            row_of.setdefault(fc, row)
            row += 16 * (last - first)
        stages.append((begin, row - begin))

    def around(away):
        return lax.rem(chip + away, chips)

    def load(pair):
        at = (slice(None), slice(None), pl.ds(pl.multiple_of(pair * 16, 16), 16), slice(None))
        return pltpu.make_async_copy(spectra_ref.at[at], raw.at[at], raw_sem.at[pair])

    load(around(1)).start()
    load(around(chips - 1)).start()
    barrier = pltpu.get_barrier_semaphore()

    for near in (
        chip * 2 + 1 - core,
        around(1) * 2,
        around(1) * 2 + 1,
        around(chips - 1) * 2,
        around(chips - 1) * 2 + 1,
    ):
        pl.semaphore_signal(barrier, inc=1, device_id={"chan": near})

    @pl.when(tm > 0)
    def _():
        pl.semaphore_signal(barrier, inc=1, device_id={"tm": tm - 1})

    def load_pairs(d, carry):
        load(around(d)).start()
        load(around(chips - d)).start()
        return carry

    lax.fori_loop(2, chips // 2, load_pairs, 0)
    load(around(chips // 2)).start()
    load(chip).start()
    small = [
        pltpu.make_async_copy(whole, mine, small_sem.at[i])
        for i, (whole, mine) in enumerate(
            ((delays_hbm, delays_ref), (flags_hbm, flags_ref), (taps_hbm, taps_ref))
        )
    ]
    for copy in small:
        copy.start()

    def arrange(pair, chunks):
        at = pl.ds(pl.multiple_of(pair * 16, 16), 16)
        for fc in chunks:
            row = row_of[fc]
            part = raw[:, :, at, fc * LANES : (fc + 1) * LANES].astype(jnp.float32)
            for q in range(2):
                for c in range(2):
                    for k in range(4):
                        mix[fc, q, pl.ds(c * 4 + k, signals, stride=8), :] = part[
                            c, k, q * 8 : q * 8 + 8, :
                        ]
            for q in range(2):
                send[pair * 2 + q, row : row + rows, :] = mix[fc, q].astype(jnp.bfloat16)

    def push(stage, to, sem=None):
        at = pl.ds(*stages[stage])
        pltpu.make_async_remote_copy(
            src_ref=send.at[to, at],
            dst_ref=recv.at[chan, at],
            send_sem=send_sem.at[stage if sem is None else sem],
            recv_sem=recv_sem.at[stage],
            device_id={"chan": to},
        ).start()

    def keep(stage):
        at = pl.ds(*stages[stage])
        pltpu.make_async_copy(send.at[chan, at], recv.at[chan, at], recv_sem.at[stage]).start()

    def each_chip(work, begin, end):
        def body(i, carry):
            far = chips // 2 - ((i + 1) >> 1)
            work(around(jnp.where((i & 1) == 0, far, chips - far)))
            return carry

        lax.fori_loop(begin, end, body, 0)

    def as_known(work):
        up, down = around(1) * 2 + core, around(chips - 1) * 2 + core
        last = chips // 2

        def tell_up(d):
            pl.semaphore_signal(from_below.at[d], inc=1, device_id={"chan": up})

        def tell_down(d):
            pl.semaphore_signal(from_above.at[d], inc=1, device_id={"chan": down})

        pl.semaphore_wait(barrier, 5 + jnp.where(tm < ntm - 1, 1, 0))
        tell_up(2)
        tell_down(2)
        work(around(1))
        work(around(chips - 1))

        def body(d, carry):
            pl.semaphore_wait(from_below.at[d], 1)
            tell_up(d + 1)
            pl.semaphore_wait(from_above.at[d], 1)

            @pl.when(d < last - 1)
            def _():
                tell_down(d + 1)

            work(around(d))
            work(around(chips - d))
            return carry

        lax.fori_loop(2, last, body, 0)
        pl.semaphore_wait(from_below.at[last], 1)
        work(around(last))

    early, farther = plan[0][0][0], chips - 5
    others = [fc for fc in row_of if fc != early]

    def push_chip(stage, pair, sem=None):
        push(stage, pair * 2 + core, sem)
        push(stage, pair * 2 + 1 - core, sem)

    def push_own(stage):
        push(stage, chip * 2 + 1 - core)
        keep(stage)

    def start_chip(pair):
        load(pair).wait()
        arrange(pair, [early])
        push_chip(0, pair)

    def far_chip(pair):
        arrange(pair, others)
        push_chip(1, pair, 3)

    def near_chip(pair):
        arrange(pair, others)
        push_chip(1, pair)

    def left(stage, count, sem=None):
        sent = send.at[0:count, pl.ds(*stages[stage])]
        pltpu.make_async_copy(sent, sent, send_sem.at[stage if sem is None else sem]).wait()

    def arrived(stage):
        arriving = recv.at[:, pl.ds(*stages[stage])]
        pltpu.make_async_copy(arriving, arriving, recv_sem.at[stage]).wait()

    as_known(start_chip)
    load(chip).wait()
    arrange(chip, row_of)
    push_own(0)
    each_chip(far_chip, 0, farther)
    each_chip(near_chip, farther, chips - 1)
    push_own(1)
    for copy in small:
        copy.wait()
    fill_tables(chan, delays_ref, flags_ref, hi, lo)

    @pl.when(tm == 0)
    def _():
        y[:, :, 0:HALO, :] = jnp.zeros((2, signals, HALO, LANES), jnp.float32)

    def transform(fc, first, last):
        base = HALO + fc * LANES

        def one_tile(t, carry):
            at = pl.ds(pl.multiple_of(row_of[fc] + t * 16, 16), 16)
            z = to_series(recv[:, at, :], hi[t], lo[t])
            for p in range(2):
                of = slice(p * LANES, (p + 1) * LANES)
                y[0, t * 2 + p, base : base + LANES, :] = z[of, :LANES]
                y[1, t * 2 + p, base : base + LANES, :] = z[of, LANES:]
            return carry

        lax.fori_loop(first, last, one_tile, 0)

    def fir(first, last, begin, end):
        sigs = 2 * (last - first)

        def one(i, carry):
            d, s = i // sigs, 2 * first + lax.rem(i, sigs)
            for row in range(begin, end, 64):
                count = min(64, end - row)
                rows_out = filtered(taps_ref, y, (d, s), HALO + row, count)
                out_ref[d, s, row : row + count, :] = rows_out
            return carry

        lax.fori_loop(0, 2 * sigs, one, 0)

    halo = pltpu.make_async_remote_copy(
        src_ref=y.at[:, :, frames : frames + HALO, :],
        dst_ref=y.at[:, :, 0:HALO, :],
        send_sem=halo_sem.at[0],
        recv_sem=halo_sem.at[1],
        device_id={"tm": lax.rem(tm + 1, ntm)},
    )

    def span(fc, first, last):
        begin = fc * LANES + (HALO if fc == nchunk - 1 else 0)
        fir(first, last, begin, (fc + 1) * LANES + (HALO if fc == nchunk - 2 else 0))

    arrived(0)
    for piece in plan[0]:
        transform(*piece)
        span(*piece)
    left(1, 2 * farther, 3)
    each_chip(lambda pair: push_chip(2, pair), 0, chips - 1)
    push_own(2)
    arrived(1)
    for i, piece in enumerate(plan[1]):
        transform(*piece)
        if i == 0:

            @pl.when(tm < ntm - 1)
            def _():
                halo.start()

    for piece in plan[1]:
        if piece[0] > 0:
            span(*piece)

    @pl.when(tm > 0)
    def _():
        halo.wait_recv()

    for piece in plan[1]:
        if piece[0] == 0:
            span(*piece)

    ((fc, first, last),) = plan[2]
    table_ref[0], table_ref[1] = hi[first:last], lo[first:last]
    taps_out_ref[...] = taps_ref[...]
    sigs = slice(2 * first, 2 * last)
    edges_ref[0] = y[:, sigs, fc * LANES : fc * LANES + HALO, :]
    after = HALO + (fc + 1) * LANES
    edges_ref[1] = y[:, sigs, after : after + HALO, :]
    left(0, nchan - 1)
    left(1, nchan - 1 - 2 * farther)
    arrived(2)
    last_ref[...] = recv[:, pl.ds(*stages[2]), :]
    left(2, nchan - 1)

    @pl.when(tm < ntm - 1)
    def _():
        halo.wait_send()


def finish(piece, done_ref, last_ref, table_ref, edges_ref, taps_ref, out_ref, y, result, sem):
    fc, first, last = piece
    _, signals, frames, _ = done_ref.shape
    begin, end = fc * LANES, (fc + 1) * LANES + HALO
    spans = [(s, 0, frames) for s in range(signals) if not 2 * first <= s < 2 * last]
    for s in range(2 * first, 2 * last):
        spans += [(s, 0, begin), (s, end, frames)]
    copies = []
    for s, start, stop in spans:
        for d in range(2):
            at = (d, s, slice(start, stop))
            copies.append(
                pltpu.make_async_copy(done_ref.at[at], out_ref.at[at], sem.at[len(copies)])
            )
            copies[-1].start()
    y[:, :, 0:HALO, :] = edges_ref[0]
    y[:, :, HALO + LANES :, :] = edges_ref[1]
    for t in range(last - first):
        z = to_series(last_ref[:, t * 16 : t * 16 + 16, :], table_ref[0, t], table_ref[1, t])
        for p in range(2):
            of = slice(p * LANES, (p + 1) * LANES)
            y[0, 2 * t + p, HALO : HALO + LANES, :] = z[of, :LANES]
            y[1, 2 * t + p, HALO : HALO + LANES, :] = z[of, LANES:]
    for s in range(2 * (last - first)):
        for d in range(2):
            for row in range(0, end - begin, 48):
                result[d, s, row : row + 48, :] = filtered(taps_ref, y, (d, s), HALO + row, 48)
            at = (d, 2 * first + s, slice(begin, end))
            copies.append(
                pltpu.make_async_copy(result.at[d, s], out_ref.at[at], sem.at[len(copies)])
            )
            copies[-1].start()
    for copy in copies:
        copy.wait()


def per_device(ntm, nchan, spectra, delays, flags, taps):
    parts, chans, sigs, frames = spectra.shape
    signals = sigs // nchan
    nfine = chans * nchan
    nchunk = frames // LANES
    rows = parts * chans * signals
    any_spec = pl.BlockSpec(memory_space=pl.ANY)

    def body(*refs):
        kernel(ntm, nchan, *refs)

    final = stages_of(nchunk, signals // 2)[-1][0]
    late = final[2] - final[1]
    vmem_spec = pl.BlockSpec(memory_space=pltpu.VMEM)
    handed_over = pl.pallas_call(
        body,
        out_shape=[
            pltpu.VMEM((2, signals, frames, nfine), jnp.bfloat16),
            pltpu.VMEM((nchan, 16 * late, LANES), jnp.bfloat16),
            pltpu.VMEM((2, late, 2 * nfine, 2 * nfine), jnp.bfloat16),
            pltpu.VMEM((2, 2, 2 * late, HALO, nfine), jnp.float32),
            pltpu.VMEM(taps.shape, jnp.float32),
        ],
        in_specs=[any_spec] * 4,
        out_specs=[vmem_spec] * 5,
        scratch_shapes=[
            pltpu.SMEM(delays.shape, jnp.int32),
            pltpu.VMEM(flags.shape, jnp.int32),
            pltpu.VMEM(taps.shape, jnp.float32),
            pltpu.VMEM(spectra.shape, jnp.bfloat16),
            pltpu.VMEM((nchunk, 2, rows, LANES), jnp.float32),
            pltpu.VMEM((nchan, nchunk * rows, LANES), jnp.bfloat16),
            pltpu.VMEM((nchan, nchunk * rows, LANES), jnp.bfloat16),
            pltpu.VMEM((2, signals, HALO + frames, nfine), jnp.float32),
            pltpu.VMEM((signals // 2, 2 * nfine, 2 * nfine), jnp.bfloat16),
            pltpu.VMEM((signals // 2, 2 * nfine, 2 * nfine), jnp.bfloat16),
            pltpu.SemaphoreType.DMA((nchan // 2,)),
            pltpu.SemaphoreType.DMA((3,)),
            pltpu.SemaphoreType.DMA((4,)),
            pltpu.SemaphoreType.DMA((3,)),
            pltpu.SemaphoreType.DMA((2,)),
            pltpu.SemaphoreType.REGULAR((nchan // 4 + 1,)),
            pltpu.SemaphoreType.REGULAR((nchan // 4 + 1,)),
        ],
        compiler_params=pltpu.CompilerParams(
            collective_id=0, has_side_effects=True, vmem_limit_bytes=20 * 2**20
        ),
        cost_estimate=pl.CostEstimate(
            flops=8 * 2**27, bytes_accessed=4 * 2**20, transcendentals=0
        ),
        name="resynthesis",
    )(*(pltpu.with_memory_space_constraint(x, pltpu.HBM) for x in (spectra, delays, flags, taps)))
    held = [pltpu.with_memory_space_constraint(x, pltpu.VMEM) for x in handed_over]

    def finish_body(*refs):
        finish(final, *refs)

    return pl.pallas_call(
        finish_body,
        out_shape=jax.ShapeDtypeStruct((2, signals, frames, nfine), jnp.bfloat16),
        in_specs=[vmem_spec] * 5,
        out_specs=any_spec,
        scratch_shapes=[
            pltpu.VMEM((2, 2 * late, HALO + LANES + HALO, nfine), jnp.float32),
            pltpu.VMEM((2, 2 * late, LANES + HALO, nfine), jnp.bfloat16),
            pltpu.SemaphoreType.DMA((2 * signals + 8 * late,)),
        ],
        compiler_params=pltpu.CompilerParams(vmem_limit_bytes=20 * 2**20),
        cost_estimate=pl.CostEstimate(
            flops=2**27, bytes_accessed=2 * 2**20, transcendentals=0
        ),
        name="last_stage",
    )(*held)


def solution(mesh):
    ntm, nchan = mesh.shape["tm"], mesh.shape["chan"]

    def body(spectra, delays, flags, taps):
        return per_device(ntm, nchan, spectra, delays, flags, taps)

    in_specs = (P(None, "chan", None, "tm"), P(), P(), P())
    return jax.shard_map(
        body, mesh=mesh, in_specs=in_specs, out_specs=P(None, "chan", "tm", None), check_vma=False
    )
```

```python
import math

import jax
import jax.numpy as jnp
from jax import lax
from jax.experimental import pallas as pl
from jax.experimental.pallas import tpu as pltpu
from jax.sharding import PartitionSpec as P

TAPS = 12
LANES = 128
HALO = 16


def fill_tables(chan, delays_ref, flags_ref, hi_ref, lo_ref):
    tiles, rows, cols = hi_ref.shape
    nfine = rows // 2
    row = lax.broadcasted_iota(jnp.int32, (rows, cols), 0)
    col = lax.broadcasted_iota(jnp.int32, (rows, cols), 1)
    fine = (row >> 3) * 4 + (row & 3)
    sample = col & (nfine - 1)
    quarter = (((row >> 2) & 1) - (col >> 7)) * (nfine // 4)
    frow = lax.broadcasted_iota(jnp.int32, (rows, nfine), 0)
    fcol = lax.broadcasted_iota(jnp.int32, (rows, nfine), 1)
    spread = (fcol == (frow >> 3) * 4 + (frow & 3)).astype(jnp.float32).astype(jnp.bfloat16)
    kept = jnp.dot(
        spread,
        flags_ref[...].astype(jnp.float32).astype(jnp.bfloat16),
        preferred_element_type=jnp.float32,
    )

    def one_tile(t, carry):
        tile = chan * tiles + t
        delay = delays_ref[tile]
        turn = (fine * (sample - delay) + quarter) & (nfine - 1)
        fold = nfine // 4 - jnp.abs(turn - nfine // 2)
        x = fold.astype(jnp.float32) * (2.0 * math.pi / nfine)
        x2 = x * x
        poly = -1.0 / 39916800.0
        for c in (1.0 / 362880.0, -1.0 / 5040.0, 1.0 / 120.0, -1.0 / 6.0, 1.0):
            poly = poly * x2 + c
        lane = lax.broadcasted_iota(jnp.int32, kept.shape, 1)
        keep = jnp.sum(jnp.where(lane == tile, kept, 0.0), axis=1, keepdims=True)
        table = (poly * x) * (keep * (-1.0 / math.sqrt(nfine)))
        hi = table.astype(jnp.bfloat16)
        hi_ref[t] = hi
        lo_ref[t] = (table - hi.astype(jnp.float32)).astype(jnp.bfloat16)
        return carry

    lax.fori_loop(0, tiles, one_tile, 0)


def to_series(part, hi, lo):
    part = part.astype(jnp.float32)
    count = part.shape[0] * 8
    pols = [part[:, p * 8 : p * 8 + 8, :].reshape(count, LANES) for p in range(2)]
    x = jnp.concatenate(pols, axis=1).astype(jnp.bfloat16)
    dims = (((0,), (0,)), ((), ()))
    z = lax.dot_general(x, hi, dims, preferred_element_type=jnp.float32)
    return z + lax.dot_general(x, lo, dims, preferred_element_type=jnp.float32)


def filtered(taps_ref, series_ref, at, start, count):
    total = None
    for j in range(TAPS):
        term = taps_ref[j : j + 1, :] * series_ref[(*at, pl.ds(start - j, count), slice(None))]
        total = term if total is None else total + term
    return total.astype(jnp.bfloat16)


def stages_of(nchunk, tiles):
    whole = [(nchunk - 1, 0, tiles)] + [(fc, 0, tiles) for fc in range(nchunk - 2)]
    return whole + [(nchunk - 2, 0, tiles // 2), (nchunk - 2, tiles // 2, tiles)]


def kernel(
    ntm,
    nchan,
    spectra_ref,
    delays_hbm,
    flags_hbm,
    taps_hbm,
    out_ref,
    last_ref,
    table_ref,
    edges_ref,
    taps_out_ref,
    delays_ref,
    flags_ref,
    taps_ref,
    raw,
    mix,
    send,
    recv,
    y,
    hi,
    lo,
    raw_sem,
    small_sem,
    send_sem,
    recv_sem,
    halo_sem,
    from_below,
    from_above,
):
    tm = lax.axis_index("tm")
    chan = lax.axis_index("chan")
    nchunk, _, rows, _ = send.shape
    signals = rows // 8
    tiles = signals // 2
    chips = nchan // 2
    chip, core = chan >> 1, chan & 1
    stages = stages_of(nchunk, tiles)
    order = [fc for i, (fc, _, _) in enumerate(stages) if fc not in [s[0] for s in stages[:i]]]

    def around(away):
        return lax.rem(chip + away, chips)

    loads = {
        fc: pltpu.make_async_copy(
            spectra_ref.at[:, :, :, fc * LANES : (fc + 1) * LANES], raw.at[fc], raw_sem.at[fc]
        )
        for fc in order
    }
    loads[order[0]].start()
    barrier = pltpu.get_barrier_semaphore()

    for near in (
        chip * 2 + 1 - core,
        around(1) * 2,
        around(1) * 2 + 1,
        around(chips - 1) * 2,
        around(chips - 1) * 2 + 1,
    ):
        pl.semaphore_signal(barrier, inc=1, device_id={"chan": near})

    @pl.when(tm > 0)
    def _():
        pl.semaphore_signal(barrier, inc=1, device_id={"tm": tm - 1})

    for fc in order[1:]:
        loads[fc].start()

    small = [
        pltpu.make_async_copy(whole, mine, small_sem.at[i])
        for i, (whole, mine) in enumerate(
            ((delays_hbm, delays_ref), (flags_hbm, flags_ref), (taps_hbm, taps_ref))
        )
    ]
    for copy in small:
        copy.start()

    def arrange(fc, pair):
        at = pl.ds(pl.multiple_of(pair * 16, 16), 16)
        part = raw[fc, :, :, at, :].astype(jnp.float32)
        for q in range(2):
            for c in range(2):
                for k in range(4):
                    mix[q, pl.ds(c * 4 + k, signals, stride=8), :] = part[c, k, q * 8 : q * 8 + 8, :]
        for q in range(2):
            send[fc, pair * 2 + q] = mix[q].astype(jnp.bfloat16)

    def push(stage, to):
        fc, first, last = stages[stage]
        at = pl.ds(first * 16, (last - first) * 16)
        pltpu.make_async_remote_copy(
            src_ref=send.at[fc, to, at],
            dst_ref=recv.at[fc, chan, at],
            send_sem=send_sem.at[stage],
            recv_sem=recv_sem.at[stage],
            device_id={"chan": to},
        ).start()

    def keep(stage):
        fc, first, last = stages[stage]
        at = pl.ds(first * 16, (last - first) * 16)
        pltpu.make_async_copy(
            send.at[fc, chan, at], recv.at[fc, chan, at], recv_sem.at[stage]
        ).start()

    def each_chip(work, far_first):
        def body(i, carry):
            far = chips // 2 - ((i + 1) >> 1) if far_first else (i >> 1) + 1
            work(around(jnp.where((i & 1) == 0, far, chips - far)))
            return carry

        lax.fori_loop(0, chips - 1, body, 0)

    def as_known(work):
        up, down = around(1) * 2 + core, around(chips - 1) * 2 + core
        last = chips // 2

        def tell_up(d):
            pl.semaphore_signal(from_below.at[d], inc=1, device_id={"chan": up})

        def tell_down(d):
            pl.semaphore_signal(from_above.at[d], inc=1, device_id={"chan": down})

        pl.semaphore_wait(barrier, 5 + jnp.where(tm < ntm - 1, 1, 0))
        tell_up(2)
        tell_down(2)
        work(around(1))
        work(around(chips - 1))

        def body(d, carry):
            pl.semaphore_wait(from_below.at[d], 1)
            tell_up(d + 1)
            pl.semaphore_wait(from_above.at[d], 1)

            @pl.when(d < last - 1)
            def _():
                tell_down(d + 1)

            work(around(d))
            work(around(chips - d))
            return carry

        lax.fori_loop(2, last, body, 0)
        pl.semaphore_wait(from_below.at[last], 1)
        work(around(last))

    def issue(stage):
        fc, first, last = stages[stage]
        fresh = first == 0

        def to_chip(pair):
            if fresh:
                arrange(fc, pair)
            push(stage, pair * 2 + core)
            push(stage, pair * 2 + 1 - core)

        if fresh:
            loads[fc].wait()
        if stage == 0:
            as_known(to_chip)
        else:
            each_chip(to_chip, stage == len(stages) - 1)
        if fresh:
            arrange(fc, chip)
        push(stage, chip * 2 + 1 - core)
        keep(stage)

    def left(stage):
        fc, first, last = stages[stage]
        sent = send.at[fc, 0 : nchan - 1, first * 16 : last * 16]
        pltpu.make_async_copy(sent, sent, send_sem.at[stage]).wait()

    issue(0)
    issue(1)
    for copy in small:
        copy.wait()
    fill_tables(chan, delays_ref, flags_ref, hi, lo)

    @pl.when(tm == 0)
    def _():
        y[:, :, 0:HALO, :] = jnp.zeros((2, signals, HALO, LANES), jnp.float32)

    def transform(stage):
        fc, first, last = stages[stage]
        base = HALO + fc * LANES

        def one_tile(t, carry):
            part = recv[fc, :, pl.ds(pl.multiple_of(t * 16, 16), 16), :]
            z = to_series(part, hi[t], lo[t])
            for p in range(2):
                of = slice(p * LANES, (p + 1) * LANES)
                y[0, t * 2 + p, base : base + LANES, :] = z[of, :LANES]
                y[1, t * 2 + p, base : base + LANES, :] = z[of, LANES:]
            return carry

        lax.fori_loop(first, last, one_tile, 0)

    def fir(stage, begin, end):
        _, first, last = stages[stage]
        sigs = 2 * (last - first)

        def one(i, carry):
            d, s = i // sigs, 2 * first + lax.rem(i, sigs)
            for row in range(begin, end, 64):
                count = min(64, end - row)
                rows_out = filtered(taps_ref, y, (d, s), HALO + row, count)
                out_ref[d, s, row : row + count, :] = rows_out
            return carry

        lax.fori_loop(0, 2 * sigs, one, 0)

    frames = nchunk * LANES
    halo = pltpu.make_async_remote_copy(
        src_ref=y.at[:, :, frames : frames + HALO, :],
        dst_ref=y.at[:, :, 0:HALO, :],
        send_sem=halo_sem.at[0],
        recv_sem=halo_sem.at[1],
        device_id={"tm": lax.rem(tm + 1, ntm)},
    )

    for stage, (fc, first, last) in enumerate(stages):
        if stage + 2 < len(stages):
            left(stage)
            issue(stage + 2)
        if stage == len(stages) - 1:
            table_ref[0], table_ref[1] = hi[first:last], lo[first:last]
            taps_out_ref[...] = taps_ref[...]
            sigs = slice(2 * first, 2 * last)
            edges_ref[0] = y[:, sigs, fc * LANES : fc * LANES + HALO, :]
            after = HALO + (fc + 1) * LANES
            edges_ref[1] = y[:, sigs, after : after + HALO, :]
        arriving = recv.at[fc, :, first * 16 : last * 16]
        pltpu.make_async_copy(arriving, arriving, recv_sem.at[stage]).wait()
        if stage == len(stages) - 1:
            last_ref[...] = recv[fc, :, first * 16 : last * 16, :]
            break
        transform(stage)
        if stage == 0:

            @pl.when(tm < ntm - 1)
            def _():
                halo.start()

        if fc == 0:

            @pl.when(tm > 0)
            def _():
                halo.wait_recv()

        begin = fc * LANES + (HALO if stage == 0 else 0)
        end = (fc + 1) * LANES + (HALO if fc == nchunk - 2 else 0)
        fir(stage, begin, end)

    for stage in range(len(stages) - 2, len(stages)):
        left(stage)

    @pl.when(tm < ntm - 1)
    def _():
        halo.wait_send()


def finish(stage, done_ref, last_ref, table_ref, edges_ref, taps_ref, out_ref, y, result, sem):
    fc, first, last = stage
    _, signals, frames, _ = done_ref.shape
    begin, end = fc * LANES, (fc + 1) * LANES + HALO
    spans = [(s, 0, frames) for s in range(signals) if not 2 * first <= s < 2 * last]
    for s in range(2 * first, 2 * last):
        spans += [(s, 0, begin), (s, end, frames)]
    copies = []
    for s, start, stop in spans:
        for d in range(2):
            at = (d, s, slice(start, stop))
            copies.append(
                pltpu.make_async_copy(done_ref.at[at], out_ref.at[at], sem.at[len(copies)])
            )
            copies[-1].start()
    y[:, :, 0:HALO, :] = edges_ref[0]
    y[:, :, HALO + LANES :, :] = edges_ref[1]
    for t in range(last - first):
        z = to_series(last_ref[:, t * 16 : t * 16 + 16, :], table_ref[0, t], table_ref[1, t])
        for p in range(2):
            of = slice(p * LANES, (p + 1) * LANES)
            y[0, 2 * t + p, HALO : HALO + LANES, :] = z[of, :LANES]
            y[1, 2 * t + p, HALO : HALO + LANES, :] = z[of, LANES:]
    for s in range(2 * (last - first)):
        for d in range(2):
            for row in range(0, end - begin, 48):
                result[d, s, row : row + 48, :] = filtered(taps_ref, y, (d, s), HALO + row, 48)
            at = (d, 2 * first + s, slice(begin, end))
            copies.append(
                pltpu.make_async_copy(result.at[d, s], out_ref.at[at], sem.at[len(copies)])
            )
            copies[-1].start()
    for copy in copies:
        copy.wait()


def per_device(ntm, nchan, spectra, delays, flags, taps):
    parts, chans, sigs, frames = spectra.shape
    signals = sigs // nchan
    nfine = chans * nchan
    nchunk = frames // LANES
    rows = parts * chans * signals
    nstage = len(stages_of(nchunk, signals // 2))
    any_spec = pl.BlockSpec(memory_space=pl.ANY)

    def body(*refs):
        kernel(ntm, nchan, *refs)

    stages = stages_of(nchunk, signals // 2)
    late = stages[-1][2] - stages[-1][1]
    vmem_spec = pl.BlockSpec(memory_space=pltpu.VMEM)
    handed_over = pl.pallas_call(
        body,
        out_shape=[
            pltpu.VMEM((2, signals, frames, nfine), jnp.bfloat16),
            pltpu.VMEM((nchan, 16 * late, LANES), jnp.bfloat16),
            pltpu.VMEM((2, late, 2 * nfine, 2 * nfine), jnp.bfloat16),
            pltpu.VMEM((2, 2, 2 * late, HALO, nfine), jnp.float32),
            pltpu.VMEM(taps.shape, jnp.float32),
        ],
        in_specs=[any_spec] * 4,
        out_specs=[vmem_spec] * 5,
        scratch_shapes=[
            pltpu.SMEM(delays.shape, jnp.int32),
            pltpu.VMEM(flags.shape, jnp.int32),
            pltpu.VMEM(taps.shape, jnp.float32),
            pltpu.VMEM((nchunk, parts, chans, sigs, LANES), jnp.bfloat16),
            pltpu.VMEM((2, rows, LANES), jnp.float32),
            pltpu.VMEM((nchunk, nchan, rows, LANES), jnp.bfloat16),
            pltpu.VMEM((nchunk, nchan, rows, LANES), jnp.bfloat16),
            pltpu.VMEM((2, signals, HALO + frames, nfine), jnp.float32),
            pltpu.VMEM((signals // 2, 2 * nfine, 2 * nfine), jnp.bfloat16),
            pltpu.VMEM((signals // 2, 2 * nfine, 2 * nfine), jnp.bfloat16),
            pltpu.SemaphoreType.DMA((nchunk,)),
            pltpu.SemaphoreType.DMA((3,)),
            pltpu.SemaphoreType.DMA((nstage,)),
            pltpu.SemaphoreType.DMA((nstage,)),
            pltpu.SemaphoreType.DMA((2,)),
            pltpu.SemaphoreType.REGULAR((nchan // 4 + 1,)),
            pltpu.SemaphoreType.REGULAR((nchan // 4 + 1,)),
        ],
        compiler_params=pltpu.CompilerParams(
            collective_id=0, has_side_effects=True, vmem_limit_bytes=20 * 2**20
        ),
        cost_estimate=pl.CostEstimate(
            flops=8 * 2**27, bytes_accessed=4 * 2**20, transcendentals=0
        ),
        name="resynthesis",
    )(*(pltpu.with_memory_space_constraint(x, pltpu.HBM) for x in (spectra, delays, flags, taps)))
    held = [pltpu.with_memory_space_constraint(x, pltpu.VMEM) for x in handed_over]

    def finish_body(*refs):
        finish(stages[-1], *refs)

    return pl.pallas_call(
        finish_body,
        out_shape=jax.ShapeDtypeStruct((2, signals, frames, nfine), jnp.bfloat16),
        in_specs=[vmem_spec] * 5,
        out_specs=any_spec,
        scratch_shapes=[
            pltpu.VMEM((2, 2 * late, HALO + LANES + HALO, nfine), jnp.float32),
            pltpu.VMEM((2, 2 * late, LANES + HALO, nfine), jnp.bfloat16),
            pltpu.SemaphoreType.DMA((2 * signals + 8 * late,)),
        ],
        compiler_params=pltpu.CompilerParams(vmem_limit_bytes=20 * 2**20),
        cost_estimate=pl.CostEstimate(
            flops=2**27, bytes_accessed=2 * 2**20, transcendentals=0
        ),
        name="last_stage",
    )(*held)


def solution(mesh):
    ntm, nchan = mesh.shape["tm"], mesh.shape["chan"]

    def body(spectra, delays, flags, taps):
        return per_device(ntm, nchan, spectra, delays, flags, taps)

    in_specs = (P(None, "chan", None, "tm"), P(), P(), P())
    return jax.shard_map(
        body, mesh=mesh, in_specs=in_specs, out_specs=P(None, "chan", "tm", None), check_vma=False
    )
```

```python
import math

import jax
import jax.numpy as jnp
from jax import lax
from jax.experimental import pallas as pl
from jax.experimental.pallas import tpu as pltpu
from jax.sharding import PartitionSpec as P

TAPS = 12
LANES = 128
HALO = 16


def fill_tables(chan, delays_ref, flags_ref, hi_ref, lo_ref):
    tiles, rows, cols = hi_ref.shape
    nfine = rows // 2
    row = lax.broadcasted_iota(jnp.int32, (rows, cols), 0)
    col = lax.broadcasted_iota(jnp.int32, (rows, cols), 1)
    fine = (row >> 3) * 4 + (row & 3)
    sample = col & (nfine - 1)
    quarter = (((row >> 2) & 1) - (col >> 7)) * (nfine // 4)
    frow = lax.broadcasted_iota(jnp.int32, (rows, nfine), 0)
    fcol = lax.broadcasted_iota(jnp.int32, (rows, nfine), 1)
    spread = (fcol == (frow >> 3) * 4 + (frow & 3)).astype(jnp.float32).astype(jnp.bfloat16)
    kept = jnp.dot(
        spread,
        flags_ref[...].astype(jnp.float32).astype(jnp.bfloat16),
        preferred_element_type=jnp.float32,
    )

    def one_tile(t, carry):
        tile = chan * tiles + t
        delay = delays_ref[tile]
        turn = (fine * (sample - delay) + quarter) & (nfine - 1)
        fold = nfine // 4 - jnp.abs(turn - nfine // 2)
        x = fold.astype(jnp.float32) * (2.0 * math.pi / nfine)
        x2 = x * x
        poly = -1.0 / 39916800.0
        for c in (1.0 / 362880.0, -1.0 / 5040.0, 1.0 / 120.0, -1.0 / 6.0, 1.0):
            poly = poly * x2 + c
        lane = lax.broadcasted_iota(jnp.int32, kept.shape, 1)
        keep = jnp.sum(jnp.where(lane == tile, kept, 0.0), axis=1, keepdims=True)
        table = (poly * x) * (keep * (-1.0 / math.sqrt(nfine)))
        hi = table.astype(jnp.bfloat16)
        hi_ref[t] = hi
        lo_ref[t] = (table - hi.astype(jnp.float32)).astype(jnp.bfloat16)
        return carry

    lax.fori_loop(0, tiles, one_tile, 0)


def to_series(part, hi, lo):
    part = part.astype(jnp.float32)
    count = part.shape[0] * 8
    pols = [part[:, p * 8 : p * 8 + 8, :].reshape(count, LANES) for p in range(2)]
    x = jnp.concatenate(pols, axis=1).astype(jnp.bfloat16)
    dims = (((0,), (0,)), ((), ()))
    z = lax.dot_general(x, hi, dims, preferred_element_type=jnp.float32)
    return z + lax.dot_general(x, lo, dims, preferred_element_type=jnp.float32)


def filtered(taps_ref, series_ref, at, start, count):
    total = None
    for j in range(TAPS):
        term = taps_ref[j : j + 1, :] * series_ref[(*at, pl.ds(start - j, count), slice(None))]
        total = term if total is None else total + term
    return total.astype(jnp.bfloat16)


def stages_of(nchunk, tiles):
    whole = [(nchunk - 1, 0, tiles)] + [(fc, 0, tiles) for fc in range(nchunk - 2)]
    return whole + [(nchunk - 2, 0, tiles - 1), (nchunk - 2, tiles - 1, tiles)]


def kernel(
    ntm,
    nchan,
    spectra_ref,
    delays_hbm,
    flags_hbm,
    taps_hbm,
    out_ref,
    last_ref,
    table_ref,
    edges_ref,
    taps_out_ref,
    delays_ref,
    flags_ref,
    taps_ref,
    raw,
    mix,
    send,
    recv,
    y,
    hi,
    lo,
    raw_sem,
    pair_sem,
    small_sem,
    send_sem,
    recv_sem,
    halo_sem,
    from_below,
    from_above,
):
    tm = lax.axis_index("tm")
    chan = lax.axis_index("chan")
    nchunk, _, rows, _ = send.shape
    signals = rows // 8
    tiles = signals // 2
    chips = nchan // 2
    chip, core = chan >> 1, chan & 1
    stages = stages_of(nchunk, tiles)
    order = [fc for i, (fc, _, _) in enumerate(stages) if fc not in [s[0] for s in stages[:i]]]

    def around(away):
        return lax.rem(chip + away, chips)

    def lanes_of(fc):
        return slice(fc * LANES, (fc + 1) * LANES)

    def load_pair(pair):
        fc = order[0]
        at = pl.ds(pl.multiple_of(pair * 16, 16), 16)
        return pltpu.make_async_copy(
            spectra_ref.at[:, :, at, lanes_of(fc)], raw.at[fc, :, :, at], pair_sem.at[pair]
        )

    loads = {
        fc: pltpu.make_async_copy(
            spectra_ref.at[:, :, :, lanes_of(fc)], raw.at[fc], raw_sem.at[fc]
        )
        for fc in order[1:]
    }
    load_pair(around(1)).start()
    load_pair(around(chips - 1)).start()
    barrier = pltpu.get_barrier_semaphore()

    for near in (
        chip * 2 + 1 - core,
        around(1) * 2,
        around(1) * 2 + 1,
        around(chips - 1) * 2,
        around(chips - 1) * 2 + 1,
    ):
        pl.semaphore_signal(barrier, inc=1, device_id={"chan": near})

    @pl.when(tm > 0)
    def _():
        pl.semaphore_signal(barrier, inc=1, device_id={"tm": tm - 1})

    def load_pairs(d, carry):
        load_pair(around(d)).start()
        load_pair(around(chips - d)).start()
        return carry

    lax.fori_loop(2, chips // 2, load_pairs, 0)
    load_pair(around(chips // 2)).start()
    load_pair(chip).start()
    for fc in order[1:]:
        loads[fc].start()

    small = [
        pltpu.make_async_copy(whole, mine, small_sem.at[i])
        for i, (whole, mine) in enumerate(
            ((delays_hbm, delays_ref), (flags_hbm, flags_ref), (taps_hbm, taps_ref))
        )
    ]
    for copy in small:
        copy.start()

    def arrange(fc, pair):
        at = pl.ds(pl.multiple_of(pair * 16, 16), 16)
        part = raw[fc, :, :, at, :].astype(jnp.float32)
        for q in range(2):
            for c in range(2):
                for k in range(4):
                    mix[q, pl.ds(c * 4 + k, signals, stride=8), :] = part[c, k, q * 8 : q * 8 + 8, :]
        for q in range(2):
            send[fc, pair * 2 + q] = mix[q].astype(jnp.bfloat16)

    def push(stage, to):
        fc, first, last = stages[stage]
        at = pl.ds(first * 16, (last - first) * 16)
        pltpu.make_async_remote_copy(
            src_ref=send.at[fc, to, at],
            dst_ref=recv.at[fc, chan, at],
            send_sem=send_sem.at[stage],
            recv_sem=recv_sem.at[stage],
            device_id={"chan": to},
        ).start()

    def keep(stage):
        fc, first, last = stages[stage]
        at = pl.ds(first * 16, (last - first) * 16)
        pltpu.make_async_copy(
            send.at[fc, chan, at], recv.at[fc, chan, at], recv_sem.at[stage]
        ).start()

    def each_chip(work, far_first):
        def body(i, carry):
            far = chips // 2 - ((i + 1) >> 1) if far_first else (i >> 1) + 1
            work(around(jnp.where((i & 1) == 0, far, chips - far)))
            return carry

        lax.fori_loop(0, chips - 1, body, 0)

    def as_known(work):
        up, down = around(1) * 2 + core, around(chips - 1) * 2 + core
        last = chips // 2

        def tell_up(d):
            pl.semaphore_signal(from_below.at[d], inc=1, device_id={"chan": up})

        def tell_down(d):
            pl.semaphore_signal(from_above.at[d], inc=1, device_id={"chan": down})

        pl.semaphore_wait(barrier, 5 + jnp.where(tm < ntm - 1, 1, 0))
        tell_up(2)
        tell_down(2)
        work(around(1))
        work(around(chips - 1))

        def body(d, carry):
            pl.semaphore_wait(from_below.at[d], 1)
            tell_up(d + 1)
            pl.semaphore_wait(from_above.at[d], 1)

            @pl.when(d < last - 1)
            def _():
                tell_down(d + 1)

            work(around(d))
            work(around(chips - d))
            return carry

        lax.fori_loop(2, last, body, 0)
        pl.semaphore_wait(from_below.at[last], 1)
        work(around(last))

    def issue(stage):
        fc, first, last = stages[stage]
        fresh = first == 0

        def to_chip(pair):
            if stage == 0:
                load_pair(pair).wait()
            if fresh:
                arrange(fc, pair)
            push(stage, pair * 2 + core)
            push(stage, pair * 2 + 1 - core)

        if fresh and stage > 0:
            loads[fc].wait()
        if stage == 0:
            as_known(to_chip)
        else:
            each_chip(to_chip, stage == len(stages) - 1)
        if stage == 0:
            load_pair(chip).wait()
        if fresh:
            arrange(fc, chip)
        push(stage, chip * 2 + 1 - core)
        keep(stage)

    def left(stage):
        fc, first, last = stages[stage]
        sent = send.at[fc, 0 : nchan - 1, first * 16 : last * 16]
        pltpu.make_async_copy(sent, sent, send_sem.at[stage]).wait()

    issue(0)
    issue(1)
    for copy in small:
        copy.wait()
    fill_tables(chan, delays_ref, flags_ref, hi, lo)

    @pl.when(tm == 0)
    def _():
        y[:, :, 0:HALO, :] = jnp.zeros((2, signals, HALO, LANES), jnp.float32)

    def transform(stage):
        fc, first, last = stages[stage]
        base = HALO + fc * LANES

        def one_tile(t, carry):
            part = recv[fc, :, pl.ds(pl.multiple_of(t * 16, 16), 16), :]
            z = to_series(part, hi[t], lo[t])
            for p in range(2):
                of = slice(p * LANES, (p + 1) * LANES)
                y[0, t * 2 + p, base : base + LANES, :] = z[of, :LANES]
                y[1, t * 2 + p, base : base + LANES, :] = z[of, LANES:]
            return carry

        lax.fori_loop(first, last, one_tile, 0)

    def fir(stage, begin, end):
        _, first, last = stages[stage]
        sigs = 2 * (last - first)

        def one(i, carry):
            d, s = i // sigs, 2 * first + lax.rem(i, sigs)
            for row in range(begin, end, 64):
                count = min(64, end - row)
                rows_out = filtered(taps_ref, y, (d, s), HALO + row, count)
                out_ref[d, s, row : row + count, :] = rows_out
            return carry

        lax.fori_loop(0, 2 * sigs, one, 0)

    frames = nchunk * LANES
    halo = pltpu.make_async_remote_copy(
        src_ref=y.at[:, :, frames : frames + HALO, :],
        dst_ref=y.at[:, :, 0:HALO, :],
        send_sem=halo_sem.at[0],
        recv_sem=halo_sem.at[1],
        device_id={"tm": lax.rem(tm + 1, ntm)},
    )

    for stage, (fc, first, last) in enumerate(stages):
        if stage + 2 < len(stages):
            left(stage)
            issue(stage + 2)
        if stage == len(stages) - 1:
            table_ref[0], table_ref[1] = hi[first:last], lo[first:last]
            taps_out_ref[...] = taps_ref[...]
            sigs = slice(2 * first, 2 * last)
            edges_ref[0] = y[:, sigs, fc * LANES : fc * LANES + HALO, :]
            after = HALO + (fc + 1) * LANES
            edges_ref[1] = y[:, sigs, after : after + HALO, :]
        arriving = recv.at[fc, :, first * 16 : last * 16]
        pltpu.make_async_copy(arriving, arriving, recv_sem.at[stage]).wait()
        if stage == len(stages) - 1:
            last_ref[...] = recv[fc, :, first * 16 : last * 16, :]
            break
        transform(stage)
        if stage == 0:

            @pl.when(tm < ntm - 1)
            def _():
                halo.start()

        if fc == 0:

            @pl.when(tm > 0)
            def _():
                halo.wait_recv()

        begin = fc * LANES + (HALO if stage == 0 else 0)
        end = (fc + 1) * LANES + (HALO if fc == nchunk - 2 else 0)
        fir(stage, begin, end)

    for stage in range(len(stages) - 2, len(stages)):
        left(stage)

    @pl.when(tm < ntm - 1)
    def _():
        halo.wait_send()


def finish(stage, done_ref, last_ref, table_ref, edges_ref, taps_ref, out_ref, y, result, sem):
    fc, first, last = stage
    _, signals, frames, _ = done_ref.shape
    begin, end = fc * LANES, (fc + 1) * LANES + HALO
    mine = slice(2 * first, 2 * last)
    spans = [(slice(0, 2 * first), 0, frames)] if first else []
    spans += [(slice(2 * last, signals), 0, frames)] if 2 * last < signals else []
    spans += [(mine, 0, begin), (mine, end, frames)]
    copies = []
    for held, start, stop in spans:
        for d in range(2):
            at = (d, held, slice(start, stop))
            copies.append(
                pltpu.make_async_copy(done_ref.at[at], out_ref.at[at], sem.at[len(copies)])
            )
            copies[-1].start()
    y[:, :, 0:HALO, :] = edges_ref[0]
    y[:, :, HALO + LANES :, :] = edges_ref[1]
    for t in range(last - first):
        z = to_series(last_ref[:, t * 16 : t * 16 + 16, :], table_ref[0, t], table_ref[1, t])
        for p in range(2):
            of = slice(p * LANES, (p + 1) * LANES)
            y[0, 2 * t + p, HALO : HALO + LANES, :] = z[of, :LANES]
            y[1, 2 * t + p, HALO : HALO + LANES, :] = z[of, LANES:]
    for s in range(2 * (last - first)):
        for d in range(2):
            for row in range(0, end - begin, 48):
                result[d, s, row : row + 48, :] = filtered(taps_ref, y, (d, s), HALO + row, 48)
            at = (d, 2 * first + s, slice(begin, end))
            copies.append(
                pltpu.make_async_copy(result.at[d, s], out_ref.at[at], sem.at[len(copies)])
            )
            copies[-1].start()
    for copy in copies:
        copy.wait()


def per_device(ntm, nchan, spectra, delays, flags, taps):
    parts, chans, sigs, frames = spectra.shape
    signals = sigs // nchan
    nfine = chans * nchan
    nchunk = frames // LANES
    rows = parts * chans * signals
    nstage = len(stages_of(nchunk, signals // 2))
    any_spec = pl.BlockSpec(memory_space=pl.ANY)

    def body(*refs):
        kernel(ntm, nchan, *refs)

    stages = stages_of(nchunk, signals // 2)
    late = stages[-1][2] - stages[-1][1]
    vmem_spec = pl.BlockSpec(memory_space=pltpu.VMEM)
    handed_over = pl.pallas_call(
        body,
        out_shape=[
            pltpu.VMEM((2, signals, frames, nfine), jnp.bfloat16),
            pltpu.VMEM((nchan, 16 * late, LANES), jnp.bfloat16),
            pltpu.VMEM((2, late, 2 * nfine, 2 * nfine), jnp.bfloat16),
            pltpu.VMEM((2, 2, 2 * late, HALO, nfine), jnp.float32),
            pltpu.VMEM(taps.shape, jnp.float32),
        ],
        in_specs=[any_spec] * 4,
        out_specs=[vmem_spec] * 5,
        scratch_shapes=[
            pltpu.SMEM(delays.shape, jnp.int32),
            pltpu.VMEM(flags.shape, jnp.int32),
            pltpu.VMEM(taps.shape, jnp.float32),
            pltpu.VMEM((nchunk, parts, chans, sigs, LANES), jnp.bfloat16),
            pltpu.VMEM((2, rows, LANES), jnp.float32),
            pltpu.VMEM((nchunk, nchan, rows, LANES), jnp.bfloat16),
            pltpu.VMEM((nchunk, nchan, rows, LANES), jnp.bfloat16),
            pltpu.VMEM((2, signals, HALO + frames, nfine), jnp.float32),
            pltpu.VMEM((signals // 2, 2 * nfine, 2 * nfine), jnp.bfloat16),
            pltpu.VMEM((signals // 2, 2 * nfine, 2 * nfine), jnp.bfloat16),
            pltpu.SemaphoreType.DMA((nchunk,)),
            pltpu.SemaphoreType.DMA((nchan // 2,)),
            pltpu.SemaphoreType.DMA((3,)),
            pltpu.SemaphoreType.DMA((nstage,)),
            pltpu.SemaphoreType.DMA((nstage,)),
            pltpu.SemaphoreType.DMA((2,)),
            pltpu.SemaphoreType.REGULAR((nchan // 4 + 1,)),
            pltpu.SemaphoreType.REGULAR((nchan // 4 + 1,)),
        ],
        compiler_params=pltpu.CompilerParams(
            collective_id=0, has_side_effects=True, vmem_limit_bytes=20 * 2**20
        ),
        cost_estimate=pl.CostEstimate(
            flops=8 * 2**27, bytes_accessed=4 * 2**20, transcendentals=0
        ),
        name="resynthesis",
    )(*(pltpu.with_memory_space_constraint(x, pltpu.HBM) for x in (spectra, delays, flags, taps)))
    held = [pltpu.with_memory_space_constraint(x, pltpu.VMEM) for x in handed_over]

    def finish_body(*refs):
        finish(stages[-1], *refs)

    return pl.pallas_call(
        finish_body,
        out_shape=jax.ShapeDtypeStruct((2, signals, frames, nfine), jnp.bfloat16),
        in_specs=[vmem_spec] * 5,
        out_specs=any_spec,
        scratch_shapes=[
            pltpu.VMEM((2, 2 * late, HALO + LANES + HALO, nfine), jnp.float32),
            pltpu.VMEM((2, 2 * late, LANES + HALO, nfine), jnp.bfloat16),
            pltpu.SemaphoreType.DMA((8 + 4 * late,)),
        ],
        compiler_params=pltpu.CompilerParams(vmem_limit_bytes=20 * 2**20),
        cost_estimate=pl.CostEstimate(
            flops=2**27, bytes_accessed=2 * 2**20, transcendentals=0
        ),
        name="last_stage",
    )(*held)


def solution(mesh):
    ntm, nchan = mesh.shape["tm"], mesh.shape["chan"]

    def body(spectra, delays, flags, taps):
        return per_device(ntm, nchan, spectra, delays, flags, taps)

    in_specs = (P(None, "chan", None, "tm"), P(), P(), P())
    return jax.shard_map(
        body, mesh=mesh, in_specs=in_specs, out_specs=P(None, "chan", "tm", None), check_vma=False
    )
```

```python
import math

import jax
import jax.numpy as jnp
from jax import lax
from jax.experimental import pallas as pl
from jax.experimental.pallas import tpu as pltpu
from jax.sharding import PartitionSpec as P

TAPS = 12
LANES = 128
HALO = 16


def fill_tables(chan, delays_ref, flags_ref, hi_ref, lo_ref):
    tiles, rows, cols = hi_ref.shape
    nfine = rows // 2
    row = lax.broadcasted_iota(jnp.int32, (rows, cols), 0)
    col = lax.broadcasted_iota(jnp.int32, (rows, cols), 1)
    fine = (row >> 3) * 4 + (row & 3)
    sample = col & (nfine - 1)
    quarter = (((row >> 2) & 1) - (col >> 7)) * (nfine // 4)
    frow = lax.broadcasted_iota(jnp.int32, (rows, nfine), 0)
    fcol = lax.broadcasted_iota(jnp.int32, (rows, nfine), 1)
    spread = (fcol == (frow >> 3) * 4 + (frow & 3)).astype(jnp.float32).astype(jnp.bfloat16)
    kept = jnp.dot(
        spread,
        flags_ref[...].astype(jnp.float32).astype(jnp.bfloat16),
        preferred_element_type=jnp.float32,
    )

    def one_tile(t, carry):
        tile = chan * tiles + t
        delay = delays_ref[tile]
        turn = (fine * (sample - delay) + quarter) & (nfine - 1)
        fold = nfine // 4 - jnp.abs(turn - nfine // 2)
        x = fold.astype(jnp.float32) * (2.0 * math.pi / nfine)
        x2 = x * x
        poly = -1.0 / 39916800.0
        for c in (1.0 / 362880.0, -1.0 / 5040.0, 1.0 / 120.0, -1.0 / 6.0, 1.0):
            poly = poly * x2 + c
        lane = lax.broadcasted_iota(jnp.int32, kept.shape, 1)
        keep = jnp.sum(jnp.where(lane == tile, kept, 0.0), axis=1, keepdims=True)
        table = (poly * x) * (keep * (-1.0 / math.sqrt(nfine)))
        hi = table.astype(jnp.bfloat16)
        hi_ref[t] = hi
        lo_ref[t] = (table - hi.astype(jnp.float32)).astype(jnp.bfloat16)
        return carry

    lax.fori_loop(0, tiles, one_tile, 0)


def to_series(part, hi, lo):
    part = part.astype(jnp.float32)
    count = part.shape[0] * 8
    pols = [part[:, p * 8 : p * 8 + 8, :].reshape(count, LANES) for p in range(2)]
    x = jnp.concatenate(pols, axis=1).astype(jnp.bfloat16)
    dims = (((0,), (0,)), ((), ()))
    z = lax.dot_general(x, hi, dims, preferred_element_type=jnp.float32)
    return z + lax.dot_general(x, lo, dims, preferred_element_type=jnp.float32)


def filtered(taps_ref, series_ref, at, start, count):
    total = None
    for j in range(TAPS):
        term = taps_ref[j : j + 1, :] * series_ref[(*at, pl.ds(start - j, count), slice(None))]
        total = term if total is None else total + term
    return total.astype(jnp.bfloat16)


def stages_of(nchunk, tiles):
    whole = [(nchunk - 1, 0, tiles)] + [(fc, 0, tiles) for fc in range(nchunk - 2)]
    return whole + [(nchunk - 2, 0, tiles - 1), (nchunk - 2, tiles - 1, tiles)]


def kernel(
    ntm,
    nchan,
    spectra_ref,
    delays_hbm,
    flags_hbm,
    taps_hbm,
    out_ref,
    last_ref,
    table_ref,
    edges_ref,
    taps_out_ref,
    delays_ref,
    flags_ref,
    taps_ref,
    raw,
    mix,
    send,
    recv,
    y,
    hi,
    lo,
    raw_sem,
    pair_sem,
    small_sem,
    send_sem,
    recv_sem,
    halo_sem,
    from_below,
    from_above,
):
    tm = lax.axis_index("tm")
    chan = lax.axis_index("chan")
    nchunk, _, rows, _ = send.shape
    signals = rows // 8
    tiles = signals // 2
    chips = nchan // 2
    chip, core = chan >> 1, chan & 1
    stages = stages_of(nchunk, tiles)
    order = [fc for i, (fc, _, _) in enumerate(stages) if fc not in [s[0] for s in stages[:i]]]

    def around(away):
        return lax.rem(chip + away, chips)

    def lanes_of(fc):
        return slice(fc * LANES, (fc + 1) * LANES)

    def load_pair(pair):
        fc = order[0]
        at = pl.ds(pl.multiple_of(pair * 16, 16), 16)
        return pltpu.make_async_copy(
            spectra_ref.at[:, :, at, lanes_of(fc)], raw.at[fc, :, :, at], pair_sem.at[pair]
        )

    loads = {
        fc: pltpu.make_async_copy(
            spectra_ref.at[:, :, :, lanes_of(fc)], raw.at[fc], raw_sem.at[fc]
        )
        for fc in order[1:]
    }
    load_pair(around(1)).start()
    load_pair(around(chips - 1)).start()
    barrier = pltpu.get_barrier_semaphore()

    for near in (
        chip * 2 + 1 - core,
        around(1) * 2,
        around(1) * 2 + 1,
        around(chips - 1) * 2,
        around(chips - 1) * 2 + 1,
    ):
        pl.semaphore_signal(barrier, inc=1, device_id={"chan": near})

    @pl.when(tm > 0)
    def _():
        pl.semaphore_signal(barrier, inc=1, device_id={"tm": tm - 1})

    def load_pairs(d, carry):
        load_pair(around(d)).start()
        load_pair(around(chips - d)).start()
        return carry

    lax.fori_loop(2, chips // 2, load_pairs, 0)
    load_pair(around(chips // 2)).start()
    load_pair(chip).start()
    for fc in order[1:]:
        loads[fc].start()

    small = [
        pltpu.make_async_copy(whole, mine, small_sem.at[i])
        for i, (whole, mine) in enumerate(
            ((delays_hbm, delays_ref), (flags_hbm, flags_ref), (taps_hbm, taps_ref))
        )
    ]
    for copy in small:
        copy.start()

    def arrange(fc, pair):
        at = pl.ds(pl.multiple_of(pair * 16, 16), 16)
        part = raw[fc, :, :, at, :].astype(jnp.float32)
        for q in range(2):
            for c in range(2):
                for k in range(4):
                    mix[q, pl.ds(c * 4 + k, signals, stride=8), :] = part[c, k, q * 8 : q * 8 + 8, :]
        for q in range(2):
            send[fc, pair * 2 + q] = mix[q].astype(jnp.bfloat16)

    def push(stage, to):
        fc, first, last = stages[stage]
        at = pl.ds(first * 16, (last - first) * 16)
        pltpu.make_async_remote_copy(
            src_ref=send.at[fc, to, at],
            dst_ref=recv.at[fc, chan, at],
            send_sem=send_sem.at[stage],
            recv_sem=recv_sem.at[stage],
            device_id={"chan": to},
        ).start()

    def keep(stage):
        fc, first, last = stages[stage]
        at = pl.ds(first * 16, (last - first) * 16)
        pltpu.make_async_copy(
            send.at[fc, chan, at], recv.at[fc, chan, at], recv_sem.at[stage]
        ).start()

    def each_chip(work, far_first):
        def body(i, carry):
            far = chips // 2 - ((i + 1) >> 1) if far_first else (i >> 1) + 1
            work(around(jnp.where((i & 1) == 0, far, chips - far)))
            return carry

        lax.fori_loop(0, chips - 1, body, 0)

    def as_known(work):
        up, down = around(1) * 2 + core, around(chips - 1) * 2 + core
        last = chips // 2

        def tell_up(d):
            pl.semaphore_signal(from_below.at[d], inc=1, device_id={"chan": up})

        def tell_down(d):
            pl.semaphore_signal(from_above.at[d], inc=1, device_id={"chan": down})

        pl.semaphore_wait(barrier, 5 + jnp.where(tm < ntm - 1, 1, 0))
        tell_up(2)
        tell_down(2)
        work(around(1))
        work(around(chips - 1))

        def body(d, carry):
            pl.semaphore_wait(from_below.at[d], 1)
            tell_up(d + 1)
            pl.semaphore_wait(from_above.at[d], 1)

            @pl.when(d < last - 1)
            def _():
                tell_down(d + 1)

            work(around(d))
            work(around(chips - d))
            return carry

        lax.fori_loop(2, last, body, 0)
        pl.semaphore_wait(from_below.at[last], 1)
        work(around(last))

    def issue(stage):
        fc, first, last = stages[stage]
        fresh = first == 0

        def to_chip(pair):
            if stage == 0:
                load_pair(pair).wait()
            if fresh:
                arrange(fc, pair)
            push(stage, pair * 2 + core)
            push(stage, pair * 2 + 1 - core)

        if fresh and stage > 0:
            loads[fc].wait()
        if stage == 0:
            as_known(to_chip)
        else:
            each_chip(to_chip, stage >= len(stages) - 2)
        if stage == 0:
            load_pair(chip).wait()
        if fresh:
            arrange(fc, chip)
        push(stage, chip * 2 + 1 - core)
        keep(stage)

    def left(stage):
        fc, first, last = stages[stage]
        sent = send.at[fc, 0 : nchan - 1, first * 16 : last * 16]
        pltpu.make_async_copy(sent, sent, send_sem.at[stage]).wait()

    issue(0)
    issue(1)
    for copy in small:
        copy.wait()
    fill_tables(chan, delays_ref, flags_ref, hi, lo)

    @pl.when(tm == 0)
    def _():
        y[:, :, 0:HALO, :] = jnp.zeros((2, signals, HALO, LANES), jnp.float32)

    def transform(stage):
        fc, first, last = stages[stage]
        base = HALO + fc * LANES

        def one_tile(t, carry):
            part = recv[fc, :, pl.ds(pl.multiple_of(t * 16, 16), 16), :]
            z = to_series(part, hi[t], lo[t])
            for p in range(2):
                of = slice(p * LANES, (p + 1) * LANES)
                y[0, t * 2 + p, base : base + LANES, :] = z[of, :LANES]
                y[1, t * 2 + p, base : base + LANES, :] = z[of, LANES:]
            return carry

        lax.fori_loop(first, last, one_tile, 0)

    def fir(stage, begin, end):
        _, first, last = stages[stage]
        sigs = 2 * (last - first)

        def one(i, carry):
            d, s = i // sigs, 2 * first + lax.rem(i, sigs)
            for row in range(begin, end, 64):
                count = min(64, end - row)
                rows_out = filtered(taps_ref, y, (d, s), HALO + row, count)
                out_ref[d, s, row : row + count, :] = rows_out
            return carry

        lax.fori_loop(0, 2 * sigs, one, 0)

    frames = nchunk * LANES
    halo = pltpu.make_async_remote_copy(
        src_ref=y.at[:, :, frames : frames + HALO, :],
        dst_ref=y.at[:, :, 0:HALO, :],
        send_sem=halo_sem.at[0],
        recv_sem=halo_sem.at[1],
        device_id={"tm": lax.rem(tm + 1, ntm)},
    )

    for stage, (fc, first, last) in enumerate(stages):
        if stage + 2 < len(stages):
            left(stage)
            issue(stage + 2)
        if stage == len(stages) - 1:
            table_ref[0], table_ref[1] = hi[first:last], lo[first:last]
            taps_out_ref[...] = taps_ref[...]
            sigs = slice(2 * first, 2 * last)
            edges_ref[0] = y[:, sigs, fc * LANES : fc * LANES + HALO, :]
            after = HALO + (fc + 1) * LANES
            edges_ref[1] = y[:, sigs, after : after + HALO, :]
        arriving = recv.at[fc, :, first * 16 : last * 16]
        pltpu.make_async_copy(arriving, arriving, recv_sem.at[stage]).wait()
        if stage == len(stages) - 1:
            last_ref[...] = recv[fc, :, first * 16 : last * 16, :]
            break
        transform(stage)
        if stage == 0:

            @pl.when(tm < ntm - 1)
            def _():
                halo.start()

        if fc == 0:

            @pl.when(tm > 0)
            def _():
                halo.wait_recv()

        begin = fc * LANES + (HALO if stage == 0 else 0)
        end = (fc + 1) * LANES + (HALO if fc == nchunk - 2 else 0)
        fir(stage, begin, end)

    for stage in range(len(stages) - 2, len(stages)):
        left(stage)

    @pl.when(tm < ntm - 1)
    def _():
        halo.wait_send()


def finish(stage, done_ref, last_ref, table_ref, edges_ref, taps_ref, out_ref, y, result, sem):
    fc, first, last = stage
    _, signals, frames, _ = done_ref.shape
    begin, end = fc * LANES, (fc + 1) * LANES + HALO
    mine = slice(2 * first, 2 * last)
    spans = [(slice(0, 2 * first), 0, frames)] if first else []
    spans += [(slice(2 * last, signals), 0, frames)] if 2 * last < signals else []
    spans += [(mine, 0, begin), (mine, end, frames)]
    copies = []
    for held, start, stop in spans:
        for d in range(2):
            at = (d, held, slice(start, stop))
            copies.append(
                pltpu.make_async_copy(done_ref.at[at], out_ref.at[at], sem.at[len(copies)])
            )
            copies[-1].start()
    y[:, :, 0:HALO, :] = edges_ref[0]
    y[:, :, HALO + LANES :, :] = edges_ref[1]
    for t in range(last - first):
        z = to_series(last_ref[:, t * 16 : t * 16 + 16, :], table_ref[0, t], table_ref[1, t])
        for p in range(2):
            of = slice(p * LANES, (p + 1) * LANES)
            y[0, 2 * t + p, HALO : HALO + LANES, :] = z[of, :LANES]
            y[1, 2 * t + p, HALO : HALO + LANES, :] = z[of, LANES:]
    for s in range(2 * (last - first)):
        for d in range(2):
            for row in range(0, end - begin, 48):
                result[d, s, row : row + 48, :] = filtered(taps_ref, y, (d, s), HALO + row, 48)
            at = (d, 2 * first + s, slice(begin, end))
            copies.append(
                pltpu.make_async_copy(result.at[d, s], out_ref.at[at], sem.at[len(copies)])
            )
            copies[-1].start()
    for copy in copies:
        copy.wait()


def per_device(ntm, nchan, spectra, delays, flags, taps):
    parts, chans, sigs, frames = spectra.shape
    signals = sigs // nchan
    nfine = chans * nchan
    nchunk = frames // LANES
    rows = parts * chans * signals
    nstage = len(stages_of(nchunk, signals // 2))
    any_spec = pl.BlockSpec(memory_space=pl.ANY)

    def body(*refs):
        kernel(ntm, nchan, *refs)

    stages = stages_of(nchunk, signals // 2)
    late = stages[-1][2] - stages[-1][1]
    vmem_spec = pl.BlockSpec(memory_space=pltpu.VMEM)
    handed_over = pl.pallas_call(
        body,
        out_shape=[
            pltpu.VMEM((2, signals, frames, nfine), jnp.bfloat16),
            pltpu.VMEM((nchan, 16 * late, LANES), jnp.bfloat16),
            pltpu.VMEM((2, late, 2 * nfine, 2 * nfine), jnp.bfloat16),
            pltpu.VMEM((2, 2, 2 * late, HALO, nfine), jnp.float32),
            pltpu.VMEM(taps.shape, jnp.float32),
        ],
        in_specs=[any_spec] * 4,
        out_specs=[vmem_spec] * 5,
        scratch_shapes=[
            pltpu.SMEM(delays.shape, jnp.int32),
            pltpu.VMEM(flags.shape, jnp.int32),
            pltpu.VMEM(taps.shape, jnp.float32),
            pltpu.VMEM((nchunk, parts, chans, sigs, LANES), jnp.bfloat16),
            pltpu.VMEM((2, rows, LANES), jnp.float32),
            pltpu.VMEM((nchunk, nchan, rows, LANES), jnp.bfloat16),
            pltpu.VMEM((nchunk, nchan, rows, LANES), jnp.bfloat16),
            pltpu.VMEM((2, signals, HALO + frames, nfine), jnp.float32),
            pltpu.VMEM((signals // 2, 2 * nfine, 2 * nfine), jnp.bfloat16),
            pltpu.VMEM((signals // 2, 2 * nfine, 2 * nfine), jnp.bfloat16),
            pltpu.SemaphoreType.DMA((nchunk,)),
            pltpu.SemaphoreType.DMA((nchan // 2,)),
            pltpu.SemaphoreType.DMA((3,)),
            pltpu.SemaphoreType.DMA((nstage,)),
            pltpu.SemaphoreType.DMA((nstage,)),
            pltpu.SemaphoreType.DMA((2,)),
            pltpu.SemaphoreType.REGULAR((nchan // 4 + 1,)),
            pltpu.SemaphoreType.REGULAR((nchan // 4 + 1,)),
        ],
        compiler_params=pltpu.CompilerParams(
            collective_id=0, has_side_effects=True, vmem_limit_bytes=20 * 2**20
        ),
        cost_estimate=pl.CostEstimate(
            flops=8 * 2**27, bytes_accessed=4 * 2**20, transcendentals=0
        ),
        name="resynthesis",
    )(*(pltpu.with_memory_space_constraint(x, pltpu.HBM) for x in (spectra, delays, flags, taps)))
    held = [pltpu.with_memory_space_constraint(x, pltpu.VMEM) for x in handed_over]

    def finish_body(*refs):
        finish(stages[-1], *refs)

    return pl.pallas_call(
        finish_body,
        out_shape=jax.ShapeDtypeStruct((2, signals, frames, nfine), jnp.bfloat16),
        in_specs=[vmem_spec] * 5,
        out_specs=any_spec,
        scratch_shapes=[
            pltpu.VMEM((2, 2 * late, HALO + LANES + HALO, nfine), jnp.float32),
            pltpu.VMEM((2, 2 * late, LANES + HALO, nfine), jnp.bfloat16),
            pltpu.SemaphoreType.DMA((8 + 4 * late,)),
        ],
        compiler_params=pltpu.CompilerParams(vmem_limit_bytes=20 * 2**20),
        cost_estimate=pl.CostEstimate(
            flops=2**27, bytes_accessed=2 * 2**20, transcendentals=0
        ),
        name="last_stage",
    )(*held)


def solution(mesh):
    ntm, nchan = mesh.shape["tm"], mesh.shape["chan"]

    def body(spectra, delays, flags, taps):
        return per_device(ntm, nchan, spectra, delays, flags, taps)

    in_specs = (P(None, "chan", None, "tm"), P(), P(), P())
    return jax.shard_map(
        body, mesh=mesh, in_specs=in_specs, out_specs=P(None, "chan", "tm", None), check_vma=False
    )
```

```python
import math

import jax
import jax.numpy as jnp
from jax import lax
from jax.experimental import pallas as pl
from jax.experimental.pallas import tpu as pltpu
from jax.sharding import PartitionSpec as P

TAPS = 12
LANES = 128
HALO = 16


def fill_tables(chan, delays_ref, flags_ref, hi_ref, lo_ref):
    tiles, rows, cols = hi_ref.shape
    nfine = rows // 2
    row = lax.broadcasted_iota(jnp.int32, (rows, cols), 0)
    col = lax.broadcasted_iota(jnp.int32, (rows, cols), 1)
    fine = (row >> 3) * 4 + (row & 3)
    sample = col & (nfine - 1)
    quarter = (((row >> 2) & 1) - (col >> 7)) * (nfine // 4)
    frow = lax.broadcasted_iota(jnp.int32, (rows, nfine), 0)
    fcol = lax.broadcasted_iota(jnp.int32, (rows, nfine), 1)
    spread = (fcol == (frow >> 3) * 4 + (frow & 3)).astype(jnp.float32).astype(jnp.bfloat16)
    kept = jnp.dot(
        spread,
        flags_ref[...].astype(jnp.float32).astype(jnp.bfloat16),
        preferred_element_type=jnp.float32,
    )

    def one_tile(t, carry):
        tile = chan * tiles + t
        delay = delays_ref[tile]
        turn = (fine * (sample - delay) + quarter) & (nfine - 1)
        fold = nfine // 4 - jnp.abs(turn - nfine // 2)
        x = fold.astype(jnp.float32) * (2.0 * math.pi / nfine)
        x2 = x * x
        poly = -1.0 / 39916800.0
        for c in (1.0 / 362880.0, -1.0 / 5040.0, 1.0 / 120.0, -1.0 / 6.0, 1.0):
            poly = poly * x2 + c
        lane = lax.broadcasted_iota(jnp.int32, kept.shape, 1)
        keep = jnp.sum(jnp.where(lane == tile, kept, 0.0), axis=1, keepdims=True)
        table = (poly * x) * (keep * (-1.0 / math.sqrt(nfine)))
        hi = table.astype(jnp.bfloat16)
        hi_ref[t] = hi
        lo_ref[t] = (table - hi.astype(jnp.float32)).astype(jnp.bfloat16)
        return carry

    lax.fori_loop(0, tiles, one_tile, 0)


def to_series(part, hi, lo):
    part = part.astype(jnp.float32)
    count = part.shape[0] * 8
    pols = [part[:, p * 8 : p * 8 + 8, :].reshape(count, LANES) for p in range(2)]
    x = jnp.concatenate(pols, axis=1).astype(jnp.bfloat16)
    dims = (((0,), (0,)), ((), ()))
    z = lax.dot_general(x, hi, dims, preferred_element_type=jnp.float32)
    return z + lax.dot_general(x, lo, dims, preferred_element_type=jnp.float32)


def filtered(taps_ref, series_ref, at, start, count):
    total = None
    for j in range(TAPS):
        term = taps_ref[j : j + 1, :] * series_ref[(*at, pl.ds(start - j, count), slice(None))]
        total = term if total is None else total + term
    return total.astype(jnp.bfloat16)


def stages_of(nchunk, tiles):
    whole = [(nchunk - 1, 0, tiles)] + [(fc, 0, tiles) for fc in range(nchunk - 2)]
    return whole + [(nchunk - 2, 0, tiles // 2), (nchunk - 2, tiles // 2, tiles)]


def kernel(
    ntm,
    nchan,
    spectra_ref,
    delays_hbm,
    flags_hbm,
    taps_hbm,
    out_ref,
    last_ref,
    table_ref,
    edges_ref,
    taps_out_ref,
    delays_ref,
    flags_ref,
    taps_ref,
    raw,
    mix,
    send,
    recv,
    y,
    hi,
    lo,
    raw_sem,
    small_sem,
    send_sem,
    recv_sem,
    halo_sem,
    from_below,
    from_above,
):
    tm = lax.axis_index("tm")
    chan = lax.axis_index("chan")
    nchunk, _, rows, _ = send.shape
    signals = rows // 8
    tiles = signals // 2
    chips = nchan // 2
    chip, core = chan >> 1, chan & 1
    stages = stages_of(nchunk, tiles)
    order = [fc for i, (fc, _, _) in enumerate(stages) if fc not in [s[0] for s in stages[:i]]]

    def around(away):
        return lax.rem(chip + away, chips)

    loads = {
        fc: pltpu.make_async_copy(
            spectra_ref.at[:, :, :, fc * LANES : (fc + 1) * LANES], raw.at[fc], raw_sem.at[fc]
        )
        for fc in order
    }
    loads[order[0]].start()
    barrier = pltpu.get_barrier_semaphore()

    for near in (
        chip * 2 + 1 - core,
        around(1) * 2,
        around(1) * 2 + 1,
        around(chips - 1) * 2,
        around(chips - 1) * 2 + 1,
    ):
        pl.semaphore_signal(barrier, inc=1, device_id={"chan": near})

    @pl.when(tm > 0)
    def _():
        pl.semaphore_signal(barrier, inc=1, device_id={"tm": tm - 1})

    for fc in order[1:]:
        loads[fc].start()

    small = [
        pltpu.make_async_copy(whole, mine, small_sem.at[i])
        for i, (whole, mine) in enumerate(
            ((delays_hbm, delays_ref), (flags_hbm, flags_ref), (taps_hbm, taps_ref))
        )
    ]
    for copy in small:
        copy.start()

    def arrange(fc, pair):
        at = pl.ds(pl.multiple_of(pair * 16, 16), 16)
        part = raw[fc, :, :, at, :].astype(jnp.float32)
        for q in range(2):
            for c in range(2):
                for k in range(4):
                    mix[q, pl.ds(c * 4 + k, signals, stride=8), :] = part[c, k, q * 8 : q * 8 + 8, :]
        for q in range(2):
            send[fc, pair * 2 + q] = mix[q].astype(jnp.bfloat16)

    def push(stage, to):
        fc, first, last = stages[stage]
        at = pl.ds(first * 16, (last - first) * 16)
        pltpu.make_async_remote_copy(
            src_ref=send.at[fc, to, at],
            dst_ref=recv.at[fc, chan, at],
            send_sem=send_sem.at[stage],
            recv_sem=recv_sem.at[stage],
            device_id={"chan": to},
        ).start()

    def keep(stage):
        fc, first, last = stages[stage]
        at = pl.ds(first * 16, (last - first) * 16)
        pltpu.make_async_copy(
            send.at[fc, chan, at], recv.at[fc, chan, at], recv_sem.at[stage]
        ).start()

    def each_chip(work):
        def body(i, carry):
            away = (i >> 1) + 1
            work(around(jnp.where((i & 1) == 0, away, chips - away)))
            return carry

        lax.fori_loop(0, chips - 1, body, 0)

    def as_known(work):
        up, down = around(1) * 2 + core, around(chips - 1) * 2 + core
        last = chips // 2

        def tell_up(d):
            pl.semaphore_signal(from_below.at[d], inc=1, device_id={"chan": up})

        def tell_down(d):
            pl.semaphore_signal(from_above.at[d], inc=1, device_id={"chan": down})

        pl.semaphore_wait(barrier, 5 + jnp.where(tm < ntm - 1, 1, 0))
        tell_up(2)
        tell_down(2)
        work(around(1))
        work(around(chips - 1))

        def body(d, carry):
            pl.semaphore_wait(from_below.at[d], 1)
            tell_up(d + 1)
            pl.semaphore_wait(from_above.at[d], 1)

            @pl.when(d < last - 1)
            def _():
                tell_down(d + 1)

            work(around(d))
            work(around(chips - d))
            return carry

        lax.fori_loop(2, last, body, 0)
        pl.semaphore_wait(from_below.at[last], 1)
        work(around(last))

    def issue(stage):
        fc, first, last = stages[stage]
        fresh = first == 0

        def to_chip(pair):
            if fresh:
                arrange(fc, pair)
            push(stage, pair * 2 + core)
            push(stage, pair * 2 + 1 - core)

        if fresh:
            loads[fc].wait()
        if stage == 0:
            as_known(to_chip)
        else:
            each_chip(to_chip)
        if fresh:
            arrange(fc, chip)
        push(stage, chip * 2 + 1 - core)
        keep(stage)

    def left(stage):
        fc, first, last = stages[stage]
        sent = send.at[fc, 0 : nchan - 1, first * 16 : last * 16]
        pltpu.make_async_copy(sent, sent, send_sem.at[stage]).wait()

    issue(0)
    issue(1)
    for copy in small:
        copy.wait()
    fill_tables(chan, delays_ref, flags_ref, hi, lo)

    @pl.when(tm == 0)
    def _():
        y[:, :, 0:HALO, :] = jnp.zeros((2, signals, HALO, LANES), jnp.float32)

    def transform(stage):
        fc, first, last = stages[stage]
        base = HALO + fc * LANES

        def one_tile(t, carry):
            part = recv[fc, :, pl.ds(pl.multiple_of(t * 16, 16), 16), :]
            z = to_series(part, hi[t], lo[t])
            for p in range(2):
                of = slice(p * LANES, (p + 1) * LANES)
                y[0, t * 2 + p, base : base + LANES, :] = z[of, :LANES]
                y[1, t * 2 + p, base : base + LANES, :] = z[of, LANES:]
            return carry

        lax.fori_loop(first, last, one_tile, 0)

    def fir(stage, begin, end):
        _, first, last = stages[stage]
        sigs = 2 * (last - first)

        def one(i, carry):
            d, s = i // sigs, 2 * first + lax.rem(i, sigs)
            for row in range(begin, end, 64):
                count = min(64, end - row)
                rows_out = filtered(taps_ref, y, (d, s), HALO + row, count)
                out_ref[d, s, row : row + count, :] = rows_out
            return carry

        lax.fori_loop(0, 2 * sigs, one, 0)

    frames = nchunk * LANES
    halo = pltpu.make_async_remote_copy(
        src_ref=y.at[:, :, frames : frames + HALO, :],
        dst_ref=y.at[:, :, 0:HALO, :],
        send_sem=halo_sem.at[0],
        recv_sem=halo_sem.at[1],
        device_id={"tm": lax.rem(tm + 1, ntm)},
    )

    for stage, (fc, first, last) in enumerate(stages):
        if stage + 2 < len(stages):
            left(stage)
            issue(stage + 2)
        if stage == len(stages) - 1:
            table_ref[0], table_ref[1] = hi[first:last], lo[first:last]
            taps_out_ref[...] = taps_ref[...]
            sigs = slice(2 * first, 2 * last)
            edges_ref[0] = y[:, sigs, fc * LANES : fc * LANES + HALO, :]
            after = HALO + (fc + 1) * LANES
            edges_ref[1] = y[:, sigs, after : after + HALO, :]
        arriving = recv.at[fc, :, first * 16 : last * 16]
        pltpu.make_async_copy(arriving, arriving, recv_sem.at[stage]).wait()
        if stage == len(stages) - 1:
            last_ref[...] = recv[fc, :, first * 16 : last * 16, :]
            break
        transform(stage)
        if stage == 0:

            @pl.when(tm < ntm - 1)
            def _():
                halo.start()

        if fc == 0:

            @pl.when(tm > 0)
            def _():
                halo.wait_recv()

        begin = fc * LANES + (HALO if stage == 0 else 0)
        end = (fc + 1) * LANES + (HALO if fc == nchunk - 2 else 0)
        fir(stage, begin, end)

    for stage in range(len(stages) - 2, len(stages)):
        left(stage)

    @pl.when(tm < ntm - 1)
    def _():
        halo.wait_send()


def finish(stage, done_ref, last_ref, table_ref, edges_ref, taps_ref, out_ref, y, result, sem):
    fc, first, last = stage
    _, signals, frames, _ = done_ref.shape
    begin, end = fc * LANES, (fc + 1) * LANES + HALO
    mine = slice(2 * first, 2 * last)
    spans = [(slice(0, 2 * first), 0, frames)] if first else []
    spans += [(slice(2 * last, signals), 0, frames)] if 2 * last < signals else []
    spans += [(mine, 0, begin), (mine, end, frames)]
    copies = []
    for held, start, stop in spans:
        for d in range(2):
            at = (d, held, slice(start, stop))
            copies.append(
                pltpu.make_async_copy(done_ref.at[at], out_ref.at[at], sem.at[len(copies)])
            )
            copies[-1].start()
    y[:, :, 0:HALO, :] = edges_ref[0]
    y[:, :, HALO + LANES :, :] = edges_ref[1]
    for t in range(last - first):
        z = to_series(last_ref[:, t * 16 : t * 16 + 16, :], table_ref[0, t], table_ref[1, t])
        for p in range(2):
            of = slice(p * LANES, (p + 1) * LANES)
            y[0, 2 * t + p, HALO : HALO + LANES, :] = z[of, :LANES]
            y[1, 2 * t + p, HALO : HALO + LANES, :] = z[of, LANES:]
    for s in range(2 * (last - first)):
        for d in range(2):
            for row in range(0, end - begin, 48):
                result[d, s, row : row + 48, :] = filtered(taps_ref, y, (d, s), HALO + row, 48)
            at = (d, 2 * first + s, slice(begin, end))
            copies.append(
                pltpu.make_async_copy(result.at[d, s], out_ref.at[at], sem.at[len(copies)])
            )
            copies[-1].start()
    for copy in copies:
        copy.wait()


def per_device(ntm, nchan, spectra, delays, flags, taps):
    parts, chans, sigs, frames = spectra.shape
    signals = sigs // nchan
    nfine = chans * nchan
    nchunk = frames // LANES
    rows = parts * chans * signals
    nstage = len(stages_of(nchunk, signals // 2))
    any_spec = pl.BlockSpec(memory_space=pl.ANY)

    def body(*refs):
        kernel(ntm, nchan, *refs)

    stages = stages_of(nchunk, signals // 2)
    late = stages[-1][2] - stages[-1][1]
    vmem_spec = pl.BlockSpec(memory_space=pltpu.VMEM)
    handed_over = pl.pallas_call(
        body,
        out_shape=[
            pltpu.VMEM((2, signals, frames, nfine), jnp.bfloat16),
            pltpu.VMEM((nchan, 16 * late, LANES), jnp.bfloat16),
            pltpu.VMEM((2, late, 2 * nfine, 2 * nfine), jnp.bfloat16),
            pltpu.VMEM((2, 2, 2 * late, HALO, nfine), jnp.float32),
            pltpu.VMEM(taps.shape, jnp.float32),
        ],
        in_specs=[any_spec] * 4,
        out_specs=[vmem_spec] * 5,
        scratch_shapes=[
            pltpu.SMEM(delays.shape, jnp.int32),
            pltpu.VMEM(flags.shape, jnp.int32),
            pltpu.VMEM(taps.shape, jnp.float32),
            pltpu.VMEM((nchunk, parts, chans, sigs, LANES), jnp.bfloat16),
            pltpu.VMEM((2, rows, LANES), jnp.float32),
            pltpu.VMEM((nchunk, nchan, rows, LANES), jnp.bfloat16),
            pltpu.VMEM((nchunk, nchan, rows, LANES), jnp.bfloat16),
            pltpu.VMEM((2, signals, HALO + frames, nfine), jnp.float32),
            pltpu.VMEM((signals // 2, 2 * nfine, 2 * nfine), jnp.bfloat16),
            pltpu.VMEM((signals // 2, 2 * nfine, 2 * nfine), jnp.bfloat16),
            pltpu.SemaphoreType.DMA((nchunk,)),
            pltpu.SemaphoreType.DMA((3,)),
            pltpu.SemaphoreType.DMA((nstage,)),
            pltpu.SemaphoreType.DMA((nstage,)),
            pltpu.SemaphoreType.DMA((2,)),
            pltpu.SemaphoreType.REGULAR((nchan // 4 + 1,)),
            pltpu.SemaphoreType.REGULAR((nchan // 4 + 1,)),
        ],
        compiler_params=pltpu.CompilerParams(
            collective_id=0, has_side_effects=True, vmem_limit_bytes=20 * 2**20
        ),
        cost_estimate=pl.CostEstimate(
            flops=8 * 2**27, bytes_accessed=4 * 2**20, transcendentals=0
        ),
        name="resynthesis",
    )(*(pltpu.with_memory_space_constraint(x, pltpu.HBM) for x in (spectra, delays, flags, taps)))
    held = [pltpu.with_memory_space_constraint(x, pltpu.VMEM) for x in handed_over]

    def finish_body(*refs):
        finish(stages[-1], *refs)

    return pl.pallas_call(
        finish_body,
        out_shape=jax.ShapeDtypeStruct((2, signals, frames, nfine), jnp.bfloat16),
        in_specs=[vmem_spec] * 5,
        out_specs=any_spec,
        scratch_shapes=[
            pltpu.VMEM((2, 2 * late, HALO + LANES + HALO, nfine), jnp.float32),
            pltpu.VMEM((2, 2 * late, LANES + HALO, nfine), jnp.bfloat16),
            pltpu.SemaphoreType.DMA((8 + 4 * late,)),
        ],
        compiler_params=pltpu.CompilerParams(vmem_limit_bytes=20 * 2**20),
        cost_estimate=pl.CostEstimate(
            flops=2**27, bytes_accessed=2 * 2**20, transcendentals=0
        ),
        name="last_stage",
    )(*held)


def solution(mesh):
    ntm, nchan = mesh.shape["tm"], mesh.shape["chan"]

    def body(spectra, delays, flags, taps):
        return per_device(ntm, nchan, spectra, delays, flags, taps)

    in_specs = (P(None, "chan", None, "tm"), P(), P(), P())
    return jax.shard_map(
        body, mesh=mesh, in_specs=in_specs, out_specs=P(None, "chan", "tm", None), check_vma=False
    )
```

```python
import math

import jax
import jax.numpy as jnp
from jax import lax
from jax.experimental import pallas as pl
from jax.experimental.pallas import tpu as pltpu
from jax.sharding import PartitionSpec as P

TAPS = 12
LANES = 128
HALO = 16


def fill_tables(chan, delays_ref, flags_ref, hi_ref, lo_ref):
    tiles, rows, cols = hi_ref.shape
    nfine = rows // 2
    row = lax.broadcasted_iota(jnp.int32, (rows, cols), 0)
    col = lax.broadcasted_iota(jnp.int32, (rows, cols), 1)
    fine = (row >> 3) * 4 + (row & 3)
    sample = col & (nfine - 1)
    quarter = (((row >> 2) & 1) - (col >> 7)) * (nfine // 4)
    frow = lax.broadcasted_iota(jnp.int32, (rows, nfine), 0)
    fcol = lax.broadcasted_iota(jnp.int32, (rows, nfine), 1)
    spread = (fcol == (frow >> 3) * 4 + (frow & 3)).astype(jnp.float32).astype(jnp.bfloat16)
    kept = jnp.dot(
        spread,
        flags_ref[...].astype(jnp.float32).astype(jnp.bfloat16),
        preferred_element_type=jnp.float32,
    )

    def one_tile(t, carry):
        tile = chan * tiles + t
        delay = delays_ref[tile]
        turn = (fine * (sample - delay) + quarter) & (nfine - 1)
        fold = nfine // 4 - jnp.abs(turn - nfine // 2)
        x = fold.astype(jnp.float32) * (2.0 * math.pi / nfine)
        x2 = x * x
        poly = -1.0 / 39916800.0
        for c in (1.0 / 362880.0, -1.0 / 5040.0, 1.0 / 120.0, -1.0 / 6.0, 1.0):
            poly = poly * x2 + c
        lane = lax.broadcasted_iota(jnp.int32, kept.shape, 1)
        keep = jnp.sum(jnp.where(lane == tile, kept, 0.0), axis=1, keepdims=True)
        table = (poly * x) * (keep * (-1.0 / math.sqrt(nfine)))
        hi = table.astype(jnp.bfloat16)
        hi_ref[t] = hi
        lo_ref[t] = (table - hi.astype(jnp.float32)).astype(jnp.bfloat16)
        return carry

    lax.fori_loop(0, tiles, one_tile, 0)


def to_series(part, hi, lo):
    part = part.astype(jnp.float32)
    count = part.shape[0] * 8
    pols = [part[:, p * 8 : p * 8 + 8, :].reshape(count, LANES) for p in range(2)]
    x = jnp.concatenate(pols, axis=1).astype(jnp.bfloat16)
    dims = (((0,), (0,)), ((), ()))
    z = lax.dot_general(x, hi, dims, preferred_element_type=jnp.float32)
    return z + lax.dot_general(x, lo, dims, preferred_element_type=jnp.float32)


def filtered(taps_ref, series_ref, at, start, count):
    total = None
    for j in range(TAPS):
        term = taps_ref[j : j + 1, :] * series_ref[(*at, pl.ds(start - j, count), slice(None))]
        total = term if total is None else total + term
    return total.astype(jnp.bfloat16)


def stages_of(nchunk, tiles):
    whole = [(nchunk - 1, 0, tiles)] + [(fc, 0, tiles) for fc in range(nchunk - 2)]
    return whole + [(nchunk - 2, 0, tiles // 2), (nchunk - 2, tiles // 2, tiles)]


def kernel(
    ntm,
    nchan,
    spectra_ref,
    delays_hbm,
    flags_hbm,
    taps_hbm,
    out_ref,
    last_ref,
    table_ref,
    edges_ref,
    taps_out_ref,
    delays_ref,
    flags_ref,
    taps_ref,
    raw,
    mix,
    send,
    recv,
    y,
    hi,
    lo,
    raw_sem,
    pair_sem,
    small_sem,
    send_sem,
    recv_sem,
    halo_sem,
    from_below,
    from_above,
):
    tm = lax.axis_index("tm")
    chan = lax.axis_index("chan")
    nchunk, _, rows, _ = send.shape
    signals = rows // 8
    tiles = signals // 2
    chips = nchan // 2
    chip, core = chan >> 1, chan & 1
    stages = stages_of(nchunk, tiles)
    order = [fc for i, (fc, _, _) in enumerate(stages) if fc not in [s[0] for s in stages[:i]]]

    def around(away):
        return lax.rem(chip + away, chips)

    def lanes_of(fc):
        return slice(fc * LANES, (fc + 1) * LANES)

    def load_pair(pair):
        fc = order[0]
        at = pl.ds(pl.multiple_of(pair * 16, 16), 16)
        return pltpu.make_async_copy(
            spectra_ref.at[:, :, at, lanes_of(fc)], raw.at[fc, :, :, at], pair_sem.at[pair]
        )

    loads = {
        fc: pltpu.make_async_copy(
            spectra_ref.at[:, :, :, lanes_of(fc)], raw.at[fc], raw_sem.at[fc]
        )
        for fc in order[1:]
    }
    load_pair(around(1)).start()
    load_pair(around(chips - 1)).start()
    barrier = pltpu.get_barrier_semaphore()

    for near in (
        chip * 2 + 1 - core,
        around(1) * 2,
        around(1) * 2 + 1,
        around(chips - 1) * 2,
        around(chips - 1) * 2 + 1,
    ):
        pl.semaphore_signal(barrier, inc=1, device_id={"chan": near})

    @pl.when(tm > 0)
    def _():
        pl.semaphore_signal(barrier, inc=1, device_id={"tm": tm - 1})

    def load_pairs(d, carry):
        load_pair(around(d)).start()
        load_pair(around(chips - d)).start()
        return carry

    lax.fori_loop(2, chips // 2, load_pairs, 0)
    load_pair(around(chips // 2)).start()
    load_pair(chip).start()
    for fc in order[1:]:
        loads[fc].start()

    small = [
        pltpu.make_async_copy(whole, mine, small_sem.at[i])
        for i, (whole, mine) in enumerate(
            ((delays_hbm, delays_ref), (flags_hbm, flags_ref), (taps_hbm, taps_ref))
        )
    ]
    for copy in small:
        copy.start()

    def arrange(fc, pair):
        at = pl.ds(pl.multiple_of(pair * 16, 16), 16)
        part = raw[fc, :, :, at, :].astype(jnp.float32)
        for q in range(2):
            for c in range(2):
                for k in range(4):
                    mix[q, pl.ds(c * 4 + k, signals, stride=8), :] = part[c, k, q * 8 : q * 8 + 8, :]
        for q in range(2):
            send[fc, pair * 2 + q] = mix[q].astype(jnp.bfloat16)

    def push(stage, to):
        fc, first, last = stages[stage]
        at = pl.ds(first * 16, (last - first) * 16)
        pltpu.make_async_remote_copy(
            src_ref=send.at[fc, to, at],
            dst_ref=recv.at[fc, chan, at],
            send_sem=send_sem.at[stage],
            recv_sem=recv_sem.at[stage],
            device_id={"chan": to},
        ).start()

    def keep(stage):
        fc, first, last = stages[stage]
        at = pl.ds(first * 16, (last - first) * 16)
        pltpu.make_async_copy(
            send.at[fc, chan, at], recv.at[fc, chan, at], recv_sem.at[stage]
        ).start()

    def each_chip(work, far_first):
        def body(i, carry):
            far = chips // 2 - ((i + 1) >> 1) if far_first else (i >> 1) + 1
            work(around(jnp.where((i & 1) == 0, far, chips - far)))
            return carry

        lax.fori_loop(0, chips - 1, body, 0)

    def as_known(work):
        up, down = around(1) * 2 + core, around(chips - 1) * 2 + core
        last = chips // 2

        def tell_up(d):
            pl.semaphore_signal(from_below.at[d], inc=1, device_id={"chan": up})

        def tell_down(d):
            pl.semaphore_signal(from_above.at[d], inc=1, device_id={"chan": down})

        pl.semaphore_wait(barrier, 5 + jnp.where(tm < ntm - 1, 1, 0))
        tell_up(2)
        tell_down(2)
        work(around(1))
        work(around(chips - 1))

        def body(d, carry):
            pl.semaphore_wait(from_below.at[d], 1)
            tell_up(d + 1)
            pl.semaphore_wait(from_above.at[d], 1)

            @pl.when(d < last - 1)
            def _():
                tell_down(d + 1)

            work(around(d))
            work(around(chips - d))
            return carry

        lax.fori_loop(2, last, body, 0)
        pl.semaphore_wait(from_below.at[last], 1)
        work(around(last))

    def issue(stage):
        fc, first, last = stages[stage]
        fresh = first == 0

        def to_chip(pair):
            if stage == 0:
                load_pair(pair).wait()
            if fresh:
                arrange(fc, pair)
            push(stage, pair * 2 + core)
            push(stage, pair * 2 + 1 - core)

        if fresh and stage > 0:
            loads[fc].wait()
        if stage == 0:
            as_known(to_chip)
        else:
            each_chip(to_chip, stage == len(stages) - 1)
        if stage == 0:
            load_pair(chip).wait()
        if fresh:
            arrange(fc, chip)
        push(stage, chip * 2 + 1 - core)
        keep(stage)

    def left(stage):
        fc, first, last = stages[stage]
        sent = send.at[fc, 0 : nchan - 1, first * 16 : last * 16]
        pltpu.make_async_copy(sent, sent, send_sem.at[stage]).wait()

    issue(0)
    issue(1)
    for copy in small:
        copy.wait()
    fill_tables(chan, delays_ref, flags_ref, hi, lo)

    @pl.when(tm == 0)
    def _():
        y[:, :, 0:HALO, :] = jnp.zeros((2, signals, HALO, LANES), jnp.float32)

    def transform(stage):
        fc, first, last = stages[stage]
        base = HALO + fc * LANES

        def one_tile(t, carry):
            part = recv[fc, :, pl.ds(pl.multiple_of(t * 16, 16), 16), :]
            z = to_series(part, hi[t], lo[t])
            for p in range(2):
                of = slice(p * LANES, (p + 1) * LANES)
                y[0, t * 2 + p, base : base + LANES, :] = z[of, :LANES]
                y[1, t * 2 + p, base : base + LANES, :] = z[of, LANES:]
            return carry

        lax.fori_loop(first, last, one_tile, 0)

    def fir(stage, begin, end):
        _, first, last = stages[stage]
        sigs = 2 * (last - first)

        def one(i, carry):
            d, s = i // sigs, 2 * first + lax.rem(i, sigs)
            for row in range(begin, end, 64):
                count = min(64, end - row)
                rows_out = filtered(taps_ref, y, (d, s), HALO + row, count)
                out_ref[d, s, row : row + count, :] = rows_out
            return carry

        lax.fori_loop(0, 2 * sigs, one, 0)

    frames = nchunk * LANES
    halo = pltpu.make_async_remote_copy(
        src_ref=y.at[:, :, frames : frames + HALO, :],
        dst_ref=y.at[:, :, 0:HALO, :],
        send_sem=halo_sem.at[0],
        recv_sem=halo_sem.at[1],
        device_id={"tm": lax.rem(tm + 1, ntm)},
    )

    for stage, (fc, first, last) in enumerate(stages):
        if stage + 2 < len(stages):
            left(stage)
            issue(stage + 2)
        if stage == len(stages) - 1:
            table_ref[0], table_ref[1] = hi[first:last], lo[first:last]
            taps_out_ref[...] = taps_ref[...]
            sigs = slice(2 * first, 2 * last)
            edges_ref[0] = y[:, sigs, fc * LANES : fc * LANES + HALO, :]
            after = HALO + (fc + 1) * LANES
            edges_ref[1] = y[:, sigs, after : after + HALO, :]
        arriving = recv.at[fc, :, first * 16 : last * 16]
        pltpu.make_async_copy(arriving, arriving, recv_sem.at[stage]).wait()
        if stage == len(stages) - 1:
            last_ref[...] = recv[fc, :, first * 16 : last * 16, :]
            break
        transform(stage)
        if stage == 0:

            @pl.when(tm < ntm - 1)
            def _():
                halo.start()

        if fc == 0:

            @pl.when(tm > 0)
            def _():
                halo.wait_recv()

        begin = fc * LANES + (HALO if stage == 0 else 0)
        end = (fc + 1) * LANES + (HALO if fc == nchunk - 2 else 0)
        fir(stage, begin, end)

    for stage in range(len(stages) - 2, len(stages)):
        left(stage)

    @pl.when(tm < ntm - 1)
    def _():
        halo.wait_send()


def finish(stage, done_ref, last_ref, table_ref, edges_ref, taps_ref, out_ref, y, result, sem):
    fc, first, last = stage
    _, signals, frames, _ = done_ref.shape
    begin, end = fc * LANES, (fc + 1) * LANES + HALO
    mine = slice(2 * first, 2 * last)
    spans = [(slice(0, 2 * first), 0, frames)] if first else []
    spans += [(slice(2 * last, signals), 0, frames)] if 2 * last < signals else []
    spans += [(mine, 0, begin), (mine, end, frames)]
    copies = []
    for held, start, stop in spans:
        for d in range(2):
            at = (d, held, slice(start, stop))
            copies.append(
                pltpu.make_async_copy(done_ref.at[at], out_ref.at[at], sem.at[len(copies)])
            )
            copies[-1].start()
    y[:, :, 0:HALO, :] = edges_ref[0]
    y[:, :, HALO + LANES :, :] = edges_ref[1]
    for t in range(last - first):
        z = to_series(last_ref[:, t * 16 : t * 16 + 16, :], table_ref[0, t], table_ref[1, t])
        for p in range(2):
            of = slice(p * LANES, (p + 1) * LANES)
            y[0, 2 * t + p, HALO : HALO + LANES, :] = z[of, :LANES]
            y[1, 2 * t + p, HALO : HALO + LANES, :] = z[of, LANES:]
    for s in range(2 * (last - first)):
        for d in range(2):
            for row in range(0, end - begin, 48):
                result[d, s, row : row + 48, :] = filtered(taps_ref, y, (d, s), HALO + row, 48)
            at = (d, 2 * first + s, slice(begin, end))
            copies.append(
                pltpu.make_async_copy(result.at[d, s], out_ref.at[at], sem.at[len(copies)])
            )
            copies[-1].start()
    for copy in copies:
        copy.wait()


def per_device(ntm, nchan, spectra, delays, flags, taps):
    parts, chans, sigs, frames = spectra.shape
    signals = sigs // nchan
    nfine = chans * nchan
    nchunk = frames // LANES
    rows = parts * chans * signals
    nstage = len(stages_of(nchunk, signals // 2))
    any_spec = pl.BlockSpec(memory_space=pl.ANY)

    def body(*refs):
        kernel(ntm, nchan, *refs)

    stages = stages_of(nchunk, signals // 2)
    late = stages[-1][2] - stages[-1][1]
    vmem_spec = pl.BlockSpec(memory_space=pltpu.VMEM)
    handed_over = pl.pallas_call(
        body,
        out_shape=[
            pltpu.VMEM((2, signals, frames, nfine), jnp.bfloat16),
            pltpu.VMEM((nchan, 16 * late, LANES), jnp.bfloat16),
            pltpu.VMEM((2, late, 2 * nfine, 2 * nfine), jnp.bfloat16),
            pltpu.VMEM((2, 2, 2 * late, HALO, nfine), jnp.float32),
            pltpu.VMEM(taps.shape, jnp.float32),
        ],
        in_specs=[any_spec] * 4,
        out_specs=[vmem_spec] * 5,
        scratch_shapes=[
            pltpu.SMEM(delays.shape, jnp.int32),
            pltpu.VMEM(flags.shape, jnp.int32),
            pltpu.VMEM(taps.shape, jnp.float32),
            pltpu.VMEM((nchunk, parts, chans, sigs, LANES), jnp.bfloat16),
            pltpu.VMEM((2, rows, LANES), jnp.float32),
            pltpu.VMEM((nchunk, nchan, rows, LANES), jnp.bfloat16),
            pltpu.VMEM((nchunk, nchan, rows, LANES), jnp.bfloat16),
            pltpu.VMEM((2, signals, HALO + frames, nfine), jnp.float32),
            pltpu.VMEM((signals // 2, 2 * nfine, 2 * nfine), jnp.bfloat16),
            pltpu.VMEM((signals // 2, 2 * nfine, 2 * nfine), jnp.bfloat16),
            pltpu.SemaphoreType.DMA((nchunk,)),
            pltpu.SemaphoreType.DMA((nchan // 2,)),
            pltpu.SemaphoreType.DMA((3,)),
            pltpu.SemaphoreType.DMA((nstage,)),
            pltpu.SemaphoreType.DMA((nstage,)),
            pltpu.SemaphoreType.DMA((2,)),
            pltpu.SemaphoreType.REGULAR((nchan // 4 + 1,)),
            pltpu.SemaphoreType.REGULAR((nchan // 4 + 1,)),
        ],
        compiler_params=pltpu.CompilerParams(
            collective_id=0, has_side_effects=True, vmem_limit_bytes=20 * 2**20
        ),
        cost_estimate=pl.CostEstimate(
            flops=8 * 2**27, bytes_accessed=4 * 2**20, transcendentals=0
        ),
        name="resynthesis",
    )(*(pltpu.with_memory_space_constraint(x, pltpu.HBM) for x in (spectra, delays, flags, taps)))
    held = [pltpu.with_memory_space_constraint(x, pltpu.VMEM) for x in handed_over]

    def finish_body(*refs):
        finish(stages[-1], *refs)

    return pl.pallas_call(
        finish_body,
        out_shape=jax.ShapeDtypeStruct((2, signals, frames, nfine), jnp.bfloat16),
        in_specs=[vmem_spec] * 5,
        out_specs=any_spec,
        scratch_shapes=[
            pltpu.VMEM((2, 2 * late, HALO + LANES + HALO, nfine), jnp.float32),
            pltpu.VMEM((2, 2 * late, LANES + HALO, nfine), jnp.bfloat16),
            pltpu.SemaphoreType.DMA((8 + 4 * late,)),
        ],
        compiler_params=pltpu.CompilerParams(vmem_limit_bytes=20 * 2**20),
        cost_estimate=pl.CostEstimate(
            flops=2**27, bytes_accessed=2 * 2**20, transcendentals=0
        ),
        name="last_stage",
    )(*held)


def solution(mesh):
    ntm, nchan = mesh.shape["tm"], mesh.shape["chan"]

    def body(spectra, delays, flags, taps):
        return per_device(ntm, nchan, spectra, delays, flags, taps)

    in_specs = (P(None, "chan", None, "tm"), P(), P(), P())
    return jax.shard_map(
        body, mesh=mesh, in_specs=in_specs, out_specs=P(None, "chan", "tm", None), check_vma=False
    )
```

```python
import math

import jax
import jax.numpy as jnp
from jax import lax
from jax.experimental import pallas as pl
from jax.experimental.pallas import tpu as pltpu
from jax.sharding import PartitionSpec as P

TAPS = 12
LANES = 128
HALO = 16


def fill_tables(chan, delays_ref, flags_ref, hi_ref, lo_ref):
    tiles, rows, cols = hi_ref.shape
    nfine = rows // 2
    row = lax.broadcasted_iota(jnp.int32, (rows, cols), 0)
    col = lax.broadcasted_iota(jnp.int32, (rows, cols), 1)
    fine = (row >> 3) * 4 + (row & 3)
    sample = col & (nfine - 1)
    quarter = (((row >> 2) & 1) - (col >> 7)) * (nfine // 4)
    frow = lax.broadcasted_iota(jnp.int32, (rows, nfine), 0)
    fcol = lax.broadcasted_iota(jnp.int32, (rows, nfine), 1)
    spread = (fcol == (frow >> 3) * 4 + (frow & 3)).astype(jnp.float32).astype(jnp.bfloat16)
    kept = jnp.dot(
        spread,
        flags_ref[...].astype(jnp.float32).astype(jnp.bfloat16),
        preferred_element_type=jnp.float32,
    )

    def one_tile(t, carry):
        tile = chan * tiles + t
        delay = delays_ref[tile]
        turn = (fine * (sample - delay) + quarter) & (nfine - 1)
        fold = nfine // 4 - jnp.abs(turn - nfine // 2)
        x = fold.astype(jnp.float32) * (2.0 * math.pi / nfine)
        x2 = x * x
        poly = -1.0 / 39916800.0
        for c in (1.0 / 362880.0, -1.0 / 5040.0, 1.0 / 120.0, -1.0 / 6.0, 1.0):
            poly = poly * x2 + c
        lane = lax.broadcasted_iota(jnp.int32, kept.shape, 1)
        keep = jnp.sum(jnp.where(lane == tile, kept, 0.0), axis=1, keepdims=True)
        table = (poly * x) * (keep * (-1.0 / math.sqrt(nfine)))
        hi = table.astype(jnp.bfloat16)
        hi_ref[t] = hi
        lo_ref[t] = (table - hi.astype(jnp.float32)).astype(jnp.bfloat16)
        return carry

    lax.fori_loop(0, tiles, one_tile, 0)


def to_series(part, hi, lo):
    part = part.astype(jnp.float32)
    count = part.shape[0] * 8
    pols = [part[:, p * 8 : p * 8 + 8, :].reshape(count, LANES) for p in range(2)]
    x = jnp.concatenate(pols, axis=1).astype(jnp.bfloat16)
    dims = (((0,), (0,)), ((), ()))
    z = lax.dot_general(x, hi, dims, preferred_element_type=jnp.float32)
    return z + lax.dot_general(x, lo, dims, preferred_element_type=jnp.float32)


def filtered(taps_ref, series_ref, at, start, count):
    total = None
    for j in range(TAPS):
        term = taps_ref[j : j + 1, :] * series_ref[(*at, pl.ds(start - j, count), slice(None))]
        total = term if total is None else total + term
    return total.astype(jnp.bfloat16)


def stages_of(nchunk, tiles):
    half, last = tiles // 2, nchunk - 1
    start = [(last, 0, tiles), (0, 0, half)]
    bulk = [(0, half, tiles)] + [(fc, 0, tiles) for fc in range(1, last - 1)]
    return [start, bulk + [(last - 1, 0, half)], [(last - 1, half, tiles)]]


def kernel(
    ntm,
    nchan,
    spectra_ref,
    delays_hbm,
    flags_hbm,
    taps_hbm,
    out_ref,
    last_ref,
    table_ref,
    edges_ref,
    taps_out_ref,
    delays_ref,
    flags_ref,
    taps_ref,
    raw,
    mix,
    send,
    recv,
    y,
    hi,
    lo,
    raw_sem,
    small_sem,
    send_sem,
    recv_sem,
    halo_sem,
    from_below,
    from_above,
):
    tm = lax.axis_index("tm")
    chan = lax.axis_index("chan")
    _, length, _ = send.shape
    frames = raw.shape[3]
    nchunk = frames // LANES
    rows = length // nchunk
    signals = rows // 8
    tiles = signals // 2
    chips = nchan // 2
    chip, core = chan >> 1, chan & 1
    plan = stages_of(nchunk, tiles)
    row_of = {}
    stages, row = [], 0
    for held in plan:
        begin = row
        for fc, first, last in held:
            row_of.setdefault(fc, row)
            row += 16 * (last - first)
        stages.append((begin, row - begin))

    def around(away):
        return lax.rem(chip + away, chips)

    def load(pair):
        at = (slice(None), slice(None), pl.ds(pl.multiple_of(pair * 16, 16), 16), slice(None))
        return pltpu.make_async_copy(spectra_ref.at[at], raw.at[at], raw_sem.at[pair])

    load(around(1)).start()
    load(around(chips - 1)).start()
    barrier = pltpu.get_barrier_semaphore()

    for near in (
        chip * 2 + 1 - core,
        around(1) * 2,
        around(1) * 2 + 1,
        around(chips - 1) * 2,
        around(chips - 1) * 2 + 1,
    ):
        pl.semaphore_signal(barrier, inc=1, device_id={"chan": near})

    @pl.when(tm > 0)
    def _():
        pl.semaphore_signal(barrier, inc=1, device_id={"tm": tm - 1})

    def load_pairs(d, carry):
        load(around(d)).start()
        load(around(chips - d)).start()
        return carry

    lax.fori_loop(2, chips // 2, load_pairs, 0)
    load(around(chips // 2)).start()
    load(chip).start()
    small = [
        pltpu.make_async_copy(whole, mine, small_sem.at[i])
        for i, (whole, mine) in enumerate(
            ((delays_hbm, delays_ref), (flags_hbm, flags_ref), (taps_hbm, taps_ref))
        )
    ]
    for copy in small:
        copy.start()

    def arrange(pair, chunks):
        at = pl.ds(pl.multiple_of(pair * 16, 16), 16)
        for fc in chunks:
            row = row_of[fc]
            part = raw[:, :, at, fc * LANES : (fc + 1) * LANES].astype(jnp.float32)
            for q in range(2):
                for c in range(2):
                    for k in range(4):
                        mix[fc, q, pl.ds(c * 4 + k, signals, stride=8), :] = part[
                            c, k, q * 8 : q * 8 + 8, :
                        ]
            for q in range(2):
                send[pair * 2 + q, row : row + rows, :] = mix[fc, q].astype(jnp.bfloat16)

    def push(stage, to):
        at = pl.ds(*stages[stage])
        pltpu.make_async_remote_copy(
            src_ref=send.at[to, at],
            dst_ref=recv.at[chan, at],
            send_sem=send_sem.at[stage],
            recv_sem=recv_sem.at[stage],
            device_id={"chan": to},
        ).start()

    def keep(stage):
        at = pl.ds(*stages[stage])
        pltpu.make_async_copy(send.at[chan, at], recv.at[chan, at], recv_sem.at[stage]).start()

    def each_chip(work, far_first):
        def body(i, carry):
            far = chips // 2 - ((i + 1) >> 1) if far_first else (i >> 1) + 1
            work(around(jnp.where((i & 1) == 0, far, chips - far)))
            return carry

        lax.fori_loop(0, chips - 1, body, 0)

    def as_known(work):
        up, down = around(1) * 2 + core, around(chips - 1) * 2 + core
        last = chips // 2

        def tell_up(d):
            pl.semaphore_signal(from_below.at[d], inc=1, device_id={"chan": up})

        def tell_down(d):
            pl.semaphore_signal(from_above.at[d], inc=1, device_id={"chan": down})

        pl.semaphore_wait(barrier, 5 + jnp.where(tm < ntm - 1, 1, 0))
        tell_up(2)
        tell_down(2)
        work(around(1))
        work(around(chips - 1))

        def body(d, carry):
            pl.semaphore_wait(from_below.at[d], 1)
            tell_up(d + 1)
            pl.semaphore_wait(from_above.at[d], 1)

            @pl.when(d < last - 1)
            def _():
                tell_down(d + 1)

            work(around(d))
            work(around(chips - d))
            return carry

        lax.fori_loop(2, last, body, 0)
        pl.semaphore_wait(from_below.at[last], 1)
        work(around(last))

    early = list(dict.fromkeys(fc for fc, _, _ in plan[0]))
    others = [fc for fc in row_of if fc not in early]

    def push_chip(stage, pair):
        push(stage, pair * 2 + core)
        push(stage, pair * 2 + 1 - core)

    def push_own(stage):
        push(stage, chip * 2 + 1 - core)
        keep(stage)

    def start_chip(pair):
        load(pair).wait()
        arrange(pair, early)
        push_chip(0, pair)

    def bulk_chip(pair):
        arrange(pair, others)
        push_chip(1, pair)

    def left(stage):
        sent = send.at[0 : nchan - 1, pl.ds(*stages[stage])]
        pltpu.make_async_copy(sent, sent, send_sem.at[stage]).wait()

    def arrived(stage):
        arriving = recv.at[:, pl.ds(*stages[stage])]
        pltpu.make_async_copy(arriving, arriving, recv_sem.at[stage]).wait()

    as_known(start_chip)
    load(chip).wait()
    arrange(chip, row_of)
    push_own(0)
    each_chip(bulk_chip, False)
    push_own(1)
    for copy in small:
        copy.wait()
    fill_tables(chan, delays_ref, flags_ref, hi, lo)

    @pl.when(tm == 0)
    def _():
        y[:, :, 0:HALO, :] = jnp.zeros((2, signals, HALO, LANES), jnp.float32)

    def transform(fc, first, last):
        base = HALO + fc * LANES

        def one_tile(t, carry):
            at = pl.ds(pl.multiple_of(row_of[fc] + t * 16, 16), 16)
            z = to_series(recv[:, at, :], hi[t], lo[t])
            for p in range(2):
                of = slice(p * LANES, (p + 1) * LANES)
                y[0, t * 2 + p, base : base + LANES, :] = z[of, :LANES]
                y[1, t * 2 + p, base : base + LANES, :] = z[of, LANES:]
            return carry

        lax.fori_loop(first, last, one_tile, 0)

    def fir(first, last, begin, end):
        sigs = 2 * (last - first)

        def one(i, carry):
            d, s = i // sigs, 2 * first + lax.rem(i, sigs)
            for row in range(begin, end, 64):
                count = min(64, end - row)
                rows_out = filtered(taps_ref, y, (d, s), HALO + row, count)
                out_ref[d, s, row : row + count, :] = rows_out
            return carry

        lax.fori_loop(0, 2 * sigs, one, 0)

    halo = pltpu.make_async_remote_copy(
        src_ref=y.at[:, :, frames : frames + HALO, :],
        dst_ref=y.at[:, :, 0:HALO, :],
        send_sem=halo_sem.at[0],
        recv_sem=halo_sem.at[1],
        device_id={"tm": lax.rem(tm + 1, ntm)},
    )

    def span(fc, first, last):
        begin = fc * LANES + (HALO if fc == nchunk - 1 else 0)
        fir(first, last, begin, (fc + 1) * LANES + (HALO if fc == nchunk - 2 else 0))

    left(0)
    each_chip(lambda pair: push_chip(2, pair), True)
    push_own(2)
    arrived(0)
    for i, piece in enumerate(plan[0]):
        transform(*piece)
        if i == 0:

            @pl.when(tm < ntm - 1)
            def _():
                halo.start()

            span(*piece)

    @pl.when(tm > 0)
    def _():
        halo.wait_recv()

    for piece in plan[0][1:]:
        span(*piece)
    arrived(1)
    for piece in plan[1]:
        transform(*piece)
    for piece in plan[1]:
        span(*piece)

    ((fc, first, last),) = plan[2]
    table_ref[0], table_ref[1] = hi[first:last], lo[first:last]
    taps_out_ref[...] = taps_ref[...]
    sigs = slice(2 * first, 2 * last)
    edges_ref[0] = y[:, sigs, fc * LANES : fc * LANES + HALO, :]
    after = HALO + (fc + 1) * LANES
    edges_ref[1] = y[:, sigs, after : after + HALO, :]
    left(1)
    arrived(2)
    last_ref[...] = recv[:, pl.ds(*stages[2]), :]
    left(2)

    @pl.when(tm < ntm - 1)
    def _():
        halo.wait_send()


def finish(piece, done_ref, last_ref, table_ref, edges_ref, taps_ref, out_ref, y, result, sem):
    fc, first, last = piece
    _, signals, frames, _ = done_ref.shape
    begin, end = fc * LANES, (fc + 1) * LANES + HALO
    mine = slice(2 * first, 2 * last)
    spans = [(slice(0, 2 * first), 0, frames)] if first else []
    spans += [(slice(2 * last, signals), 0, frames)] if 2 * last < signals else []
    spans += [(mine, 0, begin), (mine, end, frames)]
    copies = []
    for held, start, stop in spans:
        for d in range(2):
            at = (d, held, slice(start, stop))
            copies.append(
                pltpu.make_async_copy(done_ref.at[at], out_ref.at[at], sem.at[len(copies)])
            )
            copies[-1].start()
    y[:, :, 0:HALO, :] = edges_ref[0]
    y[:, :, HALO + LANES :, :] = edges_ref[1]
    for t in range(last - first):
        z = to_series(last_ref[:, t * 16 : t * 16 + 16, :], table_ref[0, t], table_ref[1, t])
        for p in range(2):
            of = slice(p * LANES, (p + 1) * LANES)
            y[0, 2 * t + p, HALO : HALO + LANES, :] = z[of, :LANES]
            y[1, 2 * t + p, HALO : HALO + LANES, :] = z[of, LANES:]
    for s in range(2 * (last - first)):
        for d in range(2):
            for row in range(0, end - begin, 48):
                result[d, s, row : row + 48, :] = filtered(taps_ref, y, (d, s), HALO + row, 48)
            at = (d, 2 * first + s, slice(begin, end))
            copies.append(
                pltpu.make_async_copy(result.at[d, s], out_ref.at[at], sem.at[len(copies)])
            )
            copies[-1].start()
    for copy in copies:
        copy.wait()


def per_device(ntm, nchan, spectra, delays, flags, taps):
    parts, chans, sigs, frames = spectra.shape
    signals = sigs // nchan
    nfine = chans * nchan
    nchunk = frames // LANES
    rows = parts * chans * signals
    any_spec = pl.BlockSpec(memory_space=pl.ANY)

    def body(*refs):
        kernel(ntm, nchan, *refs)

    final = stages_of(nchunk, signals // 2)[-1][0]
    late = final[2] - final[1]
    vmem_spec = pl.BlockSpec(memory_space=pltpu.VMEM)
    handed_over = pl.pallas_call(
        body,
        out_shape=[
            pltpu.VMEM((2, signals, frames, nfine), jnp.bfloat16),
            pltpu.VMEM((nchan, 16 * late, LANES), jnp.bfloat16),
            pltpu.VMEM((2, late, 2 * nfine, 2 * nfine), jnp.bfloat16),
            pltpu.VMEM((2, 2, 2 * late, HALO, nfine), jnp.float32),
            pltpu.VMEM(taps.shape, jnp.float32),
        ],
        in_specs=[any_spec] * 4,
        out_specs=[vmem_spec] * 5,
        scratch_shapes=[
            pltpu.SMEM(delays.shape, jnp.int32),
            pltpu.VMEM(flags.shape, jnp.int32),
            pltpu.VMEM(taps.shape, jnp.float32),
            pltpu.VMEM(spectra.shape, jnp.bfloat16),
            pltpu.VMEM((nchunk, 2, rows, LANES), jnp.float32),
            pltpu.VMEM((nchan, nchunk * rows, LANES), jnp.bfloat16),
            pltpu.VMEM((nchan, nchunk * rows, LANES), jnp.bfloat16),
            pltpu.VMEM((2, signals, HALO + frames, nfine), jnp.float32),
            pltpu.VMEM((signals // 2, 2 * nfine, 2 * nfine), jnp.bfloat16),
            pltpu.VMEM((signals // 2, 2 * nfine, 2 * nfine), jnp.bfloat16),
            pltpu.SemaphoreType.DMA((nchan // 2,)),
            pltpu.SemaphoreType.DMA((3,)),
            pltpu.SemaphoreType.DMA((3,)),
            pltpu.SemaphoreType.DMA((3,)),
            pltpu.SemaphoreType.DMA((2,)),
            pltpu.SemaphoreType.REGULAR((nchan // 4 + 1,)),
            pltpu.SemaphoreType.REGULAR((nchan // 4 + 1,)),
        ],
        compiler_params=pltpu.CompilerParams(
            collective_id=0, has_side_effects=True, vmem_limit_bytes=20 * 2**20
        ),
        cost_estimate=pl.CostEstimate(
            flops=8 * 2**27, bytes_accessed=4 * 2**20, transcendentals=0
        ),
        name="resynthesis",
    )(*(pltpu.with_memory_space_constraint(x, pltpu.HBM) for x in (spectra, delays, flags, taps)))
    held = [pltpu.with_memory_space_constraint(x, pltpu.VMEM) for x in handed_over]

    def finish_body(*refs):
        finish(final, *refs)

    return pl.pallas_call(
        finish_body,
        out_shape=jax.ShapeDtypeStruct((2, signals, frames, nfine), jnp.bfloat16),
        in_specs=[vmem_spec] * 5,
        out_specs=any_spec,
        scratch_shapes=[
            pltpu.VMEM((2, 2 * late, HALO + LANES + HALO, nfine), jnp.float32),
            pltpu.VMEM((2, 2 * late, LANES + HALO, nfine), jnp.bfloat16),
            pltpu.SemaphoreType.DMA((8 + 4 * late,)),
        ],
        compiler_params=pltpu.CompilerParams(vmem_limit_bytes=20 * 2**20),
        cost_estimate=pl.CostEstimate(
            flops=2**27, bytes_accessed=2 * 2**20, transcendentals=0
        ),
        name="last_stage",
    )(*held)


def solution(mesh):
    ntm, nchan = mesh.shape["tm"], mesh.shape["chan"]

    def body(spectra, delays, flags, taps):
        return per_device(ntm, nchan, spectra, delays, flags, taps)

    in_specs = (P(None, "chan", None, "tm"), P(), P(), P())
    return jax.shard_map(
        body, mesh=mesh, in_specs=in_specs, out_specs=P(None, "chan", "tm", None), check_vma=False
    )
```

```python
import math

import jax
import jax.numpy as jnp
from jax import lax
from jax.experimental import pallas as pl
from jax.experimental.pallas import tpu as pltpu
from jax.sharding import PartitionSpec as P

TAPS = 12
LANES = 128
HALO = 16


def fill_tables(chan, delays_ref, flags_ref, hi_ref, lo_ref):
    tiles, rows, cols = hi_ref.shape
    nfine = rows // 2
    row = lax.broadcasted_iota(jnp.int32, (rows, cols), 0)
    col = lax.broadcasted_iota(jnp.int32, (rows, cols), 1)
    fine = (row >> 3) * 4 + (row & 3)
    sample = col & (nfine - 1)
    quarter = (((row >> 2) & 1) - (col >> 7)) * (nfine // 4)
    frow = lax.broadcasted_iota(jnp.int32, (rows, nfine), 0)
    fcol = lax.broadcasted_iota(jnp.int32, (rows, nfine), 1)
    spread = (fcol == (frow >> 3) * 4 + (frow & 3)).astype(jnp.float32).astype(jnp.bfloat16)
    kept = jnp.dot(
        spread,
        flags_ref[...].astype(jnp.float32).astype(jnp.bfloat16),
        preferred_element_type=jnp.float32,
    )

    def one_tile(t, carry):
        tile = chan * tiles + t
        delay = delays_ref[tile]
        turn = (fine * (sample - delay) + quarter) & (nfine - 1)
        fold = nfine // 4 - jnp.abs(turn - nfine // 2)
        x = fold.astype(jnp.float32) * (2.0 * math.pi / nfine)
        x2 = x * x
        poly = -1.0 / 39916800.0
        for c in (1.0 / 362880.0, -1.0 / 5040.0, 1.0 / 120.0, -1.0 / 6.0, 1.0):
            poly = poly * x2 + c
        lane = lax.broadcasted_iota(jnp.int32, kept.shape, 1)
        keep = jnp.sum(jnp.where(lane == tile, kept, 0.0), axis=1, keepdims=True)
        table = (poly * x) * (keep * (-1.0 / math.sqrt(nfine)))
        hi = table.astype(jnp.bfloat16)
        hi_ref[t] = hi
        lo_ref[t] = (table - hi.astype(jnp.float32)).astype(jnp.bfloat16)
        return carry

    lax.fori_loop(0, tiles, one_tile, 0)


def to_series(part, hi, lo):
    part = part.astype(jnp.float32)
    count = part.shape[0] * 8
    pols = [part[:, p * 8 : p * 8 + 8, :].reshape(count, LANES) for p in range(2)]
    x = jnp.concatenate(pols, axis=1).astype(jnp.bfloat16)
    dims = (((0,), (0,)), ((), ()))
    z = lax.dot_general(x, hi, dims, preferred_element_type=jnp.float32)
    return z + lax.dot_general(x, lo, dims, preferred_element_type=jnp.float32)


def filtered(taps_ref, series_ref, at, start, count):
    total = None
    for j in range(TAPS):
        term = taps_ref[j : j + 1, :] * series_ref[(*at, pl.ds(start - j, count), slice(None))]
        total = term if total is None else total + term
    return total.astype(jnp.bfloat16)


def stages_of(nchunk, tiles):
    whole = [(nchunk - 1, 0, tiles)] + [(fc, 0, tiles) for fc in range(nchunk - 2)]
    return whole + [(nchunk - 2, 0, tiles // 2), (nchunk - 2, tiles // 2, tiles)]


def kernel(
    ntm,
    nchan,
    spectra_ref,
    delays_hbm,
    flags_hbm,
    taps_hbm,
    out_ref,
    last_ref,
    table_ref,
    edges_ref,
    taps_out_ref,
    delays_ref,
    flags_ref,
    taps_ref,
    raw,
    mix,
    send,
    recv,
    y,
    hi,
    lo,
    raw_sem,
    pair_sem,
    small_sem,
    send_sem,
    recv_sem,
    halo_sem,
    from_below,
    from_above,
):
    tm = lax.axis_index("tm")
    chan = lax.axis_index("chan")
    nchunk, _, rows, _ = send.shape
    signals = rows // 8
    tiles = signals // 2
    chips = nchan // 2
    chip, core = chan >> 1, chan & 1
    stages = stages_of(nchunk, tiles)
    order = [fc for i, (fc, _, _) in enumerate(stages) if fc not in [s[0] for s in stages[:i]]]

    def around(away):
        return lax.rem(chip + away, chips)

    def lanes_of(fc):
        return slice(fc * LANES, (fc + 1) * LANES)

    def load_pair(pair):
        fc = order[0]
        at = pl.ds(pl.multiple_of(pair * 16, 16), 16)
        return pltpu.make_async_copy(
            spectra_ref.at[:, :, at, lanes_of(fc)], raw.at[fc, :, :, at], pair_sem.at[pair]
        )

    loads = {
        fc: pltpu.make_async_copy(
            spectra_ref.at[:, :, :, lanes_of(fc)], raw.at[fc], raw_sem.at[fc]
        )
        for fc in order[1:]
    }
    load_pair(around(1)).start()
    load_pair(around(chips - 1)).start()
    barrier = pltpu.get_barrier_semaphore()

    for near in (
        chip * 2 + 1 - core,
        around(1) * 2,
        around(1) * 2 + 1,
        around(chips - 1) * 2,
        around(chips - 1) * 2 + 1,
    ):
        pl.semaphore_signal(barrier, inc=1, device_id={"chan": near})

    @pl.when(tm > 0)
    def _():
        pl.semaphore_signal(barrier, inc=1, device_id={"tm": tm - 1})

    def load_pairs(d, carry):
        load_pair(around(d)).start()
        load_pair(around(chips - d)).start()
        return carry

    lax.fori_loop(2, chips // 2, load_pairs, 0)
    load_pair(around(chips // 2)).start()
    load_pair(chip).start()
    for fc in order[1:]:
        loads[fc].start()

    small = [
        pltpu.make_async_copy(whole, mine, small_sem.at[i])
        for i, (whole, mine) in enumerate(
            ((delays_hbm, delays_ref), (flags_hbm, flags_ref), (taps_hbm, taps_ref))
        )
    ]
    for copy in small:
        copy.start()

    def arrange(fc, pair):
        at = pl.ds(pl.multiple_of(pair * 16, 16), 16)
        part = raw[fc, :, :, at, :].astype(jnp.float32)
        for q in range(2):
            for c in range(2):
                for k in range(4):
                    mix[q, pl.ds(c * 4 + k, signals, stride=8), :] = part[c, k, q * 8 : q * 8 + 8, :]
        for q in range(2):
            send[fc, pair * 2 + q] = mix[q].astype(jnp.bfloat16)

    def push(stage, to):
        fc, first, last = stages[stage]
        at = pl.ds(first * 16, (last - first) * 16)
        pltpu.make_async_remote_copy(
            src_ref=send.at[fc, to, at],
            dst_ref=recv.at[fc, chan, at],
            send_sem=send_sem.at[stage],
            recv_sem=recv_sem.at[stage],
            device_id={"chan": to},
        ).start()

    def keep(stage):
        fc, first, last = stages[stage]
        at = pl.ds(first * 16, (last - first) * 16)
        pltpu.make_async_copy(
            send.at[fc, chan, at], recv.at[fc, chan, at], recv_sem.at[stage]
        ).start()

    def each_chip(work, far_first):
        def body(i, carry):
            far = chips // 2 - ((i + 1) >> 1) if far_first else (i >> 1) + 1
            work(around(jnp.where((i & 1) == 0, far, chips - far)))
            return carry

        lax.fori_loop(0, chips - 1, body, 0)

    def as_known(work):
        up, down = around(1) * 2 + core, around(chips - 1) * 2 + core
        last = chips // 2

        def tell_up(d):
            pl.semaphore_signal(from_below.at[d], inc=1, device_id={"chan": up})

        def tell_down(d):
            pl.semaphore_signal(from_above.at[d], inc=1, device_id={"chan": down})

        pl.semaphore_wait(barrier, 5 + jnp.where(tm < ntm - 1, 1, 0))
        tell_up(2)
        tell_down(2)
        work(around(1))
        work(around(chips - 1))

        def body(d, carry):
            pl.semaphore_wait(from_below.at[d], 1)
            tell_up(d + 1)
            pl.semaphore_wait(from_above.at[d], 1)

            @pl.when(d < last - 1)
            def _():
                tell_down(d + 1)

            work(around(d))
            work(around(chips - d))
            return carry

        lax.fori_loop(2, last, body, 0)
        pl.semaphore_wait(from_below.at[last], 1)
        work(around(last))

    def issue(stage):
        fc, first, last = stages[stage]
        fresh = first == 0

        def to_chip(pair):
            if stage == 0:
                load_pair(pair).wait()
            if fresh:
                arrange(fc, pair)
            push(stage, pair * 2 + core)
            push(stage, pair * 2 + 1 - core)

        if fresh and stage > 0:
            loads[fc].wait()
        if stage == 0:
            as_known(to_chip)
        else:
            each_chip(to_chip, stage == len(stages) - 1)
        if stage == 0:
            load_pair(chip).wait()
        if fresh:
            arrange(fc, chip)
        push(stage, chip * 2 + 1 - core)
        keep(stage)

    def left(stage):
        fc, first, last = stages[stage]
        sent = send.at[fc, 0 : nchan - 1, first * 16 : last * 16]
        pltpu.make_async_copy(sent, sent, send_sem.at[stage]).wait()

    issue(0)
    issue(1)
    for copy in small:
        copy.wait()
    fill_tables(chan, delays_ref, flags_ref, hi, lo)

    @pl.when(tm == 0)
    def _():
        y[:, :, 0:HALO, :] = jnp.zeros((2, signals, HALO, LANES), jnp.float32)

    def transform(stage):
        fc, first, last = stages[stage]
        base = HALO + fc * LANES

        def one_tile(t, carry):
            part = recv[fc, :, pl.ds(pl.multiple_of(t * 16, 16), 16), :]
            z = to_series(part, hi[t], lo[t])
            for p in range(2):
                of = slice(p * LANES, (p + 1) * LANES)
                y[0, t * 2 + p, base : base + LANES, :] = z[of, :LANES]
                y[1, t * 2 + p, base : base + LANES, :] = z[of, LANES:]
            return carry

        lax.fori_loop(first, last, one_tile, 0)

    def fir(stage, begin, end):
        _, first, last = stages[stage]
        sigs = 2 * (last - first)

        def one(i, carry):
            d, s = i // sigs, 2 * first + lax.rem(i, sigs)
            for row in range(begin, end, 64):
                count = min(64, end - row)
                rows_out = filtered(taps_ref, y, (d, s), HALO + row, count)
                out_ref[d, s, row : row + count, :] = rows_out
            return carry

        lax.fori_loop(0, 2 * sigs, one, 0)

    frames = nchunk * LANES
    halo = pltpu.make_async_remote_copy(
        src_ref=y.at[:, :, frames : frames + HALO, :],
        dst_ref=y.at[:, :, 0:HALO, :],
        send_sem=halo_sem.at[0],
        recv_sem=halo_sem.at[1],
        device_id={"tm": lax.rem(tm + 1, ntm)},
    )

    for stage, (fc, first, last) in enumerate(stages):
        if stage == 0:
            left(0)
            issue(2)
        if stage == len(stages) - 1:
            table_ref[0], table_ref[1] = hi[first:last], lo[first:last]
            taps_out_ref[...] = taps_ref[...]
            sigs = slice(2 * first, 2 * last)
            edges_ref[0] = y[:, sigs, fc * LANES : fc * LANES + HALO, :]
            after = HALO + (fc + 1) * LANES
            edges_ref[1] = y[:, sigs, after : after + HALO, :]
        arriving = recv.at[fc, :, first * 16 : last * 16]
        pltpu.make_async_copy(arriving, arriving, recv_sem.at[stage]).wait()
        if stage == len(stages) - 1:
            last_ref[...] = recv[fc, :, first * 16 : last * 16, :]
            break
        transform(stage)
        if stage == 0:

            @pl.when(tm < ntm - 1)
            def _():
                halo.start()

        if fc == 0:

            @pl.when(tm > 0)
            def _():
                halo.wait_recv()

        begin = fc * LANES + (HALO if stage == 0 else 0)
        end = (fc + 1) * LANES + (HALO if fc == nchunk - 2 else 0)
        fir(stage, begin, end)
        if stage == 1:
            left(1)
            issue(3)

    for stage in range(len(stages) - 2, len(stages)):
        left(stage)

    @pl.when(tm < ntm - 1)
    def _():
        halo.wait_send()


def finish(stage, done_ref, last_ref, table_ref, edges_ref, taps_ref, out_ref, y, result, sem):
    fc, first, last = stage
    _, signals, frames, _ = done_ref.shape
    begin, end = fc * LANES, (fc + 1) * LANES + HALO
    mine = slice(2 * first, 2 * last)
    spans = [(slice(0, 2 * first), 0, frames)] if first else []
    spans += [(slice(2 * last, signals), 0, frames)] if 2 * last < signals else []
    spans += [(mine, 0, begin), (mine, end, frames)]
    copies = []
    for held, start, stop in spans:
        for d in range(2):
            at = (d, held, slice(start, stop))
            copies.append(
                pltpu.make_async_copy(done_ref.at[at], out_ref.at[at], sem.at[len(copies)])
            )
            copies[-1].start()
    y[:, :, 0:HALO, :] = edges_ref[0]
    y[:, :, HALO + LANES :, :] = edges_ref[1]
    for t in range(last - first):
        z = to_series(last_ref[:, t * 16 : t * 16 + 16, :], table_ref[0, t], table_ref[1, t])
        for p in range(2):
            of = slice(p * LANES, (p + 1) * LANES)
            y[0, 2 * t + p, HALO : HALO + LANES, :] = z[of, :LANES]
            y[1, 2 * t + p, HALO : HALO + LANES, :] = z[of, LANES:]
    for s in range(2 * (last - first)):
        for d in range(2):
            for row in range(0, end - begin, 48):
                result[d, s, row : row + 48, :] = filtered(taps_ref, y, (d, s), HALO + row, 48)
            at = (d, 2 * first + s, slice(begin, end))
            copies.append(
                pltpu.make_async_copy(result.at[d, s], out_ref.at[at], sem.at[len(copies)])
            )
            copies[-1].start()
    for copy in copies:
        copy.wait()


def per_device(ntm, nchan, spectra, delays, flags, taps):
    parts, chans, sigs, frames = spectra.shape
    signals = sigs // nchan
    nfine = chans * nchan
    nchunk = frames // LANES
    rows = parts * chans * signals
    nstage = len(stages_of(nchunk, signals // 2))
    any_spec = pl.BlockSpec(memory_space=pl.ANY)

    def body(*refs):
        kernel(ntm, nchan, *refs)

    stages = stages_of(nchunk, signals // 2)
    late = stages[-1][2] - stages[-1][1]
    vmem_spec = pl.BlockSpec(memory_space=pltpu.VMEM)
    handed_over = pl.pallas_call(
        body,
        out_shape=[
            pltpu.VMEM((2, signals, frames, nfine), jnp.bfloat16),
            pltpu.VMEM((nchan, 16 * late, LANES), jnp.bfloat16),
            pltpu.VMEM((2, late, 2 * nfine, 2 * nfine), jnp.bfloat16),
            pltpu.VMEM((2, 2, 2 * late, HALO, nfine), jnp.float32),
            pltpu.VMEM(taps.shape, jnp.float32),
        ],
        in_specs=[any_spec] * 4,
        out_specs=[vmem_spec] * 5,
        scratch_shapes=[
            pltpu.SMEM(delays.shape, jnp.int32),
            pltpu.VMEM(flags.shape, jnp.int32),
            pltpu.VMEM(taps.shape, jnp.float32),
            pltpu.VMEM((nchunk, parts, chans, sigs, LANES), jnp.bfloat16),
            pltpu.VMEM((2, rows, LANES), jnp.float32),
            pltpu.VMEM((nchunk, nchan, rows, LANES), jnp.bfloat16),
            pltpu.VMEM((nchunk, nchan, rows, LANES), jnp.bfloat16),
            pltpu.VMEM((2, signals, HALO + frames, nfine), jnp.float32),
            pltpu.VMEM((signals // 2, 2 * nfine, 2 * nfine), jnp.bfloat16),
            pltpu.VMEM((signals // 2, 2 * nfine, 2 * nfine), jnp.bfloat16),
            pltpu.SemaphoreType.DMA((nchunk,)),
            pltpu.SemaphoreType.DMA((nchan // 2,)),
            pltpu.SemaphoreType.DMA((3,)),
            pltpu.SemaphoreType.DMA((nstage,)),
            pltpu.SemaphoreType.DMA((nstage,)),
            pltpu.SemaphoreType.DMA((2,)),
            pltpu.SemaphoreType.REGULAR((nchan // 4 + 1,)),
            pltpu.SemaphoreType.REGULAR((nchan // 4 + 1,)),
        ],
        compiler_params=pltpu.CompilerParams(
            collective_id=0, has_side_effects=True, vmem_limit_bytes=20 * 2**20
        ),
        cost_estimate=pl.CostEstimate(
            flops=8 * 2**27, bytes_accessed=4 * 2**20, transcendentals=0
        ),
        name="resynthesis",
    )(*(pltpu.with_memory_space_constraint(x, pltpu.HBM) for x in (spectra, delays, flags, taps)))
    held = [pltpu.with_memory_space_constraint(x, pltpu.VMEM) for x in handed_over]

    def finish_body(*refs):
        finish(stages[-1], *refs)

    return pl.pallas_call(
        finish_body,
        out_shape=jax.ShapeDtypeStruct((2, signals, frames, nfine), jnp.bfloat16),
        in_specs=[vmem_spec] * 5,
        out_specs=any_spec,
        scratch_shapes=[
            pltpu.VMEM((2, 2 * late, HALO + LANES + HALO, nfine), jnp.float32),
            pltpu.VMEM((2, 2 * late, LANES + HALO, nfine), jnp.bfloat16),
            pltpu.SemaphoreType.DMA((8 + 4 * late,)),
        ],
        compiler_params=pltpu.CompilerParams(vmem_limit_bytes=20 * 2**20),
        cost_estimate=pl.CostEstimate(
            flops=2**27, bytes_accessed=2 * 2**20, transcendentals=0
        ),
        name="last_stage",
    )(*held)


def solution(mesh):
    ntm, nchan = mesh.shape["tm"], mesh.shape["chan"]

    def body(spectra, delays, flags, taps):
        return per_device(ntm, nchan, spectra, delays, flags, taps)

    in_specs = (P(None, "chan", None, "tm"), P(), P(), P())
    return jax.shard_map(
        body, mesh=mesh, in_specs=in_specs, out_specs=P(None, "chan", "tm", None), check_vma=False
    )
```

```python
import math

import jax
import jax.numpy as jnp
from jax import lax
from jax.experimental import pallas as pl
from jax.experimental.pallas import tpu as pltpu
from jax.sharding import PartitionSpec as P

TAPS = 12
LANES = 128
HALO = 16


def fill_tables(chan, delays_ref, flags_ref, hi_ref, lo_ref):
    tiles, rows, cols = hi_ref.shape
    nfine = rows // 2
    row = lax.broadcasted_iota(jnp.int32, (rows, cols), 0)
    col = lax.broadcasted_iota(jnp.int32, (rows, cols), 1)
    fine = (row >> 3) * 4 + (row & 3)
    sample = col & (nfine - 1)
    quarter = (((row >> 2) & 1) - (col >> 7)) * (nfine // 4)
    frow = lax.broadcasted_iota(jnp.int32, (rows, nfine), 0)
    fcol = lax.broadcasted_iota(jnp.int32, (rows, nfine), 1)
    spread = (fcol == (frow >> 3) * 4 + (frow & 3)).astype(jnp.float32).astype(jnp.bfloat16)
    kept = jnp.dot(
        spread,
        flags_ref[...].astype(jnp.float32).astype(jnp.bfloat16),
        preferred_element_type=jnp.float32,
    )

    def one_tile(t, carry):
        tile = chan * tiles + t
        delay = delays_ref[tile]
        turn = (fine * (sample - delay) + quarter) & (nfine - 1)
        fold = nfine // 4 - jnp.abs(turn - nfine // 2)
        x = fold.astype(jnp.float32) * (2.0 * math.pi / nfine)
        x2 = x * x
        poly = -1.0 / 39916800.0
        for c in (1.0 / 362880.0, -1.0 / 5040.0, 1.0 / 120.0, -1.0 / 6.0, 1.0):
            poly = poly * x2 + c
        lane = lax.broadcasted_iota(jnp.int32, kept.shape, 1)
        keep = jnp.sum(jnp.where(lane == tile, kept, 0.0), axis=1, keepdims=True)
        table = (poly * x) * (keep * (-1.0 / math.sqrt(nfine)))
        hi = table.astype(jnp.bfloat16)
        hi_ref[t] = hi
        lo_ref[t] = (table - hi.astype(jnp.float32)).astype(jnp.bfloat16)
        return carry

    lax.fori_loop(0, tiles, one_tile, 0)


def to_series(part, hi, lo):
    part = part.astype(jnp.float32)
    count = part.shape[0] * 8
    pols = [part[:, p * 8 : p * 8 + 8, :].reshape(count, LANES) for p in range(2)]
    x = jnp.concatenate(pols, axis=1).astype(jnp.bfloat16)
    dims = (((0,), (0,)), ((), ()))
    z = lax.dot_general(x, hi, dims, preferred_element_type=jnp.float32)
    return z + lax.dot_general(x, lo, dims, preferred_element_type=jnp.float32)


def filtered(taps_ref, series_ref, at, start, count):
    total = None
    for j in range(TAPS):
        term = taps_ref[j : j + 1, :] * series_ref[(*at, pl.ds(start - j, count), slice(None))]
        total = term if total is None else total + term
    return total.astype(jnp.bfloat16)


def stages_of(nchunk, tiles):
    whole = [(nchunk - 1, 0, tiles)] + [(fc, 0, tiles) for fc in range(nchunk - 2)]
    return whole + [(nchunk - 2, 0, tiles // 2), (nchunk - 2, tiles // 2, tiles)]


def kernel(
    ntm,
    nchan,
    spectra_ref,
    delays_hbm,
    flags_hbm,
    taps_hbm,
    out_ref,
    last_ref,
    table_ref,
    edges_ref,
    taps_out_ref,
    delays_ref,
    flags_ref,
    taps_ref,
    raw,
    mix,
    send,
    recv,
    y,
    hi,
    lo,
    raw_sem,
    small_sem,
    send_sem,
    recv_sem,
    halo_sem,
    from_below,
    from_above,
):
    tm = lax.axis_index("tm")
    chan = lax.axis_index("chan")
    nchunk, _, rows, _ = send.shape
    signals = rows // 8
    tiles = signals // 2
    chips = nchan // 2
    chip, core = chan >> 1, chan & 1
    stages = stages_of(nchunk, tiles)
    order = [fc for i, (fc, _, _) in enumerate(stages) if fc not in [s[0] for s in stages[:i]]]

    def around(away):
        return lax.rem(chip + away, chips)

    loads = {
        fc: pltpu.make_async_copy(
            spectra_ref.at[:, :, :, fc * LANES : (fc + 1) * LANES], raw.at[fc], raw_sem.at[fc]
        )
        for fc in order
    }
    loads[order[0]].start()
    barrier = pltpu.get_barrier_semaphore()

    for near in (
        chip * 2 + 1 - core,
        around(1) * 2,
        around(1) * 2 + 1,
        around(chips - 1) * 2,
        around(chips - 1) * 2 + 1,
    ):
        pl.semaphore_signal(barrier, inc=1, device_id={"chan": near})

    @pl.when(tm > 0)
    def _():
        pl.semaphore_signal(barrier, inc=1, device_id={"tm": tm - 1})

    for fc in order[1:]:
        loads[fc].start()

    small = [
        pltpu.make_async_copy(whole, mine, small_sem.at[i])
        for i, (whole, mine) in enumerate(
            ((delays_hbm, delays_ref), (flags_hbm, flags_ref), (taps_hbm, taps_ref))
        )
    ]
    for copy in small:
        copy.start()

    def arrange(fc, pair):
        at = pl.ds(pl.multiple_of(pair * 16, 16), 16)
        part = raw[fc, :, :, at, :].astype(jnp.float32)
        for q in range(2):
            for c in range(2):
                for k in range(4):
                    mix[q, pl.ds(c * 4 + k, signals, stride=8), :] = part[c, k, q * 8 : q * 8 + 8, :]
        for q in range(2):
            send[fc, pair * 2 + q] = mix[q].astype(jnp.bfloat16)

    def push(stage, to):
        fc, first, last = stages[stage]
        at = pl.ds(first * 16, (last - first) * 16)
        pltpu.make_async_remote_copy(
            src_ref=send.at[fc, to, at],
            dst_ref=recv.at[fc, chan, at],
            send_sem=send_sem.at[stage],
            recv_sem=recv_sem.at[stage],
            device_id={"chan": to},
        ).start()

    def keep(stage):
        fc, first, last = stages[stage]
        at = pl.ds(first * 16, (last - first) * 16)
        pltpu.make_async_copy(
            send.at[fc, chan, at], recv.at[fc, chan, at], recv_sem.at[stage]
        ).start()

    def each_chip(work, far_first):
        def body(i, carry):
            far = chips // 2 - ((i + 1) >> 1) if far_first else (i >> 1) + 1
            work(around(jnp.where((i & 1) == core, far, chips - far)))
            return carry

        lax.fori_loop(0, chips - 1, body, 0)

    def as_known(work):
        up, down = around(1) * 2 + core, around(chips - 1) * 2 + core
        last = chips // 2

        def tell_up(d):
            pl.semaphore_signal(from_below.at[d], inc=1, device_id={"chan": up})

        def tell_down(d):
            pl.semaphore_signal(from_above.at[d], inc=1, device_id={"chan": down})

        pl.semaphore_wait(barrier, 5 + jnp.where(tm < ntm - 1, 1, 0))
        tell_up(2)
        tell_down(2)
        work(around(jnp.where(core == 0, 1, chips - 1)))
        work(around(jnp.where(core == 0, chips - 1, 1)))

        def body(d, carry):
            pl.semaphore_wait(from_below.at[d], 1)
            tell_up(d + 1)
            pl.semaphore_wait(from_above.at[d], 1)

            @pl.when(d < last - 1)
            def _():
                tell_down(d + 1)

            work(around(jnp.where(core == 0, d, chips - d)))
            work(around(jnp.where(core == 0, chips - d, d)))
            return carry

        lax.fori_loop(2, last, body, 0)
        pl.semaphore_wait(from_below.at[last], 1)
        work(around(last))

    def issue(stage):
        fc, first, last = stages[stage]
        fresh = first == 0

        def to_chip(pair):
            if fresh:
                arrange(fc, pair)
            push(stage, pair * 2 + core)
            push(stage, pair * 2 + 1 - core)

        if fresh:
            loads[fc].wait()
        if stage == 0:
            as_known(to_chip)
        else:
            each_chip(to_chip, stage == len(stages) - 1)
        if fresh:
            arrange(fc, chip)
        push(stage, chip * 2 + 1 - core)
        keep(stage)

    def left(stage):
        fc, first, last = stages[stage]
        sent = send.at[fc, 0 : nchan - 1, first * 16 : last * 16]
        pltpu.make_async_copy(sent, sent, send_sem.at[stage]).wait()

    issue(0)
    issue(1)
    for copy in small:
        copy.wait()
    fill_tables(chan, delays_ref, flags_ref, hi, lo)

    @pl.when(tm == 0)
    def _():
        y[:, :, 0:HALO, :] = jnp.zeros((2, signals, HALO, LANES), jnp.float32)

    def transform(stage):
        fc, first, last = stages[stage]
        base = HALO + fc * LANES

        def one_tile(t, carry):
            part = recv[fc, :, pl.ds(pl.multiple_of(t * 16, 16), 16), :]
            z = to_series(part, hi[t], lo[t])
            for p in range(2):
                of = slice(p * LANES, (p + 1) * LANES)
                y[0, t * 2 + p, base : base + LANES, :] = z[of, :LANES]
                y[1, t * 2 + p, base : base + LANES, :] = z[of, LANES:]
            return carry

        lax.fori_loop(first, last, one_tile, 0)

    def fir(stage, begin, end):
        _, first, last = stages[stage]
        sigs = 2 * (last - first)

        def one(i, carry):
            d, s = i // sigs, 2 * first + lax.rem(i, sigs)
            for row in range(begin, end, 64):
                count = min(64, end - row)
                rows_out = filtered(taps_ref, y, (d, s), HALO + row, count)
                out_ref[d, s, row : row + count, :] = rows_out
            return carry

        lax.fori_loop(0, 2 * sigs, one, 0)

    frames = nchunk * LANES
    halo = pltpu.make_async_remote_copy(
        src_ref=y.at[:, :, frames : frames + HALO, :],
        dst_ref=y.at[:, :, 0:HALO, :],
        send_sem=halo_sem.at[0],
        recv_sem=halo_sem.at[1],
        device_id={"tm": lax.rem(tm + 1, ntm)},
    )

    for stage, (fc, first, last) in enumerate(stages):
        if stage + 2 < len(stages):
            left(stage)
            issue(stage + 2)
        if stage == len(stages) - 1:
            table_ref[0], table_ref[1] = hi[first:last], lo[first:last]
            taps_out_ref[...] = taps_ref[...]
            sigs = slice(2 * first, 2 * last)
            edges_ref[0] = y[:, sigs, fc * LANES : fc * LANES + HALO, :]
            after = HALO + (fc + 1) * LANES
            edges_ref[1] = y[:, sigs, after : after + HALO, :]
        arriving = recv.at[fc, :, first * 16 : last * 16]
        pltpu.make_async_copy(arriving, arriving, recv_sem.at[stage]).wait()
        if stage == len(stages) - 1:
            last_ref[...] = recv[fc, :, first * 16 : last * 16, :]
            break
        transform(stage)
        if stage == 0:

            @pl.when(tm < ntm - 1)
            def _():
                halo.start()

        if fc == 0:

            @pl.when(tm > 0)
            def _():
                halo.wait_recv()

        begin = fc * LANES + (HALO if stage == 0 else 0)
        end = (fc + 1) * LANES + (HALO if fc == nchunk - 2 else 0)
        fir(stage, begin, end)

    for stage in range(len(stages) - 2, len(stages)):
        left(stage)

    @pl.when(tm < ntm - 1)
    def _():
        halo.wait_send()


def finish(stage, done_ref, last_ref, table_ref, edges_ref, taps_ref, out_ref, y, result, sem):
    fc, first, last = stage
    _, signals, frames, _ = done_ref.shape
    begin, end = fc * LANES, (fc + 1) * LANES + HALO
    spans = [(s, 0, frames) for s in range(signals) if not 2 * first <= s < 2 * last]
    for s in range(2 * first, 2 * last):
        spans += [(s, 0, begin), (s, end, frames)]
    copies = []
    for s, start, stop in spans:
        for d in range(2):
            at = (d, s, slice(start, stop))
            copies.append(
                pltpu.make_async_copy(done_ref.at[at], out_ref.at[at], sem.at[len(copies)])
            )
            copies[-1].start()
    y[:, :, 0:HALO, :] = edges_ref[0]
    y[:, :, HALO + LANES :, :] = edges_ref[1]
    for t in range(last - first):
        z = to_series(last_ref[:, t * 16 : t * 16 + 16, :], table_ref[0, t], table_ref[1, t])
        for p in range(2):
            of = slice(p * LANES, (p + 1) * LANES)
            y[0, 2 * t + p, HALO : HALO + LANES, :] = z[of, :LANES]
            y[1, 2 * t + p, HALO : HALO + LANES, :] = z[of, LANES:]
    for s in range(2 * (last - first)):
        for d in range(2):
            for row in range(0, end - begin, 48):
                result[d, s, row : row + 48, :] = filtered(taps_ref, y, (d, s), HALO + row, 48)
            at = (d, 2 * first + s, slice(begin, end))
            copies.append(
                pltpu.make_async_copy(result.at[d, s], out_ref.at[at], sem.at[len(copies)])
            )
            copies[-1].start()
    for copy in copies:
        copy.wait()


def per_device(ntm, nchan, spectra, delays, flags, taps):
    parts, chans, sigs, frames = spectra.shape
    signals = sigs // nchan
    nfine = chans * nchan
    nchunk = frames // LANES
    rows = parts * chans * signals
    nstage = len(stages_of(nchunk, signals // 2))
    any_spec = pl.BlockSpec(memory_space=pl.ANY)

    def body(*refs):
        kernel(ntm, nchan, *refs)

    stages = stages_of(nchunk, signals // 2)
    late = stages[-1][2] - stages[-1][1]
    vmem_spec = pl.BlockSpec(memory_space=pltpu.VMEM)
    handed_over = pl.pallas_call(
        body,
        out_shape=[
            pltpu.VMEM((2, signals, frames, nfine), jnp.bfloat16),
            pltpu.VMEM((nchan, 16 * late, LANES), jnp.bfloat16),
            pltpu.VMEM((2, late, 2 * nfine, 2 * nfine), jnp.bfloat16),
            pltpu.VMEM((2, 2, 2 * late, HALO, nfine), jnp.float32),
            pltpu.VMEM(taps.shape, jnp.float32),
        ],
        in_specs=[any_spec] * 4,
        out_specs=[vmem_spec] * 5,
        scratch_shapes=[
            pltpu.SMEM(delays.shape, jnp.int32),
            pltpu.VMEM(flags.shape, jnp.int32),
            pltpu.VMEM(taps.shape, jnp.float32),
            pltpu.VMEM((nchunk, parts, chans, sigs, LANES), jnp.bfloat16),
            pltpu.VMEM((2, rows, LANES), jnp.float32),
            pltpu.VMEM((nchunk, nchan, rows, LANES), jnp.bfloat16),
            pltpu.VMEM((nchunk, nchan, rows, LANES), jnp.bfloat16),
            pltpu.VMEM((2, signals, HALO + frames, nfine), jnp.float32),
            pltpu.VMEM((signals // 2, 2 * nfine, 2 * nfine), jnp.bfloat16),
            pltpu.VMEM((signals // 2, 2 * nfine, 2 * nfine), jnp.bfloat16),
            pltpu.SemaphoreType.DMA((nchunk,)),
            pltpu.SemaphoreType.DMA((3,)),
            pltpu.SemaphoreType.DMA((nstage,)),
            pltpu.SemaphoreType.DMA((nstage,)),
            pltpu.SemaphoreType.DMA((2,)),
            pltpu.SemaphoreType.REGULAR((nchan // 4 + 1,)),
            pltpu.SemaphoreType.REGULAR((nchan // 4 + 1,)),
        ],
        compiler_params=pltpu.CompilerParams(
            collective_id=0, has_side_effects=True, vmem_limit_bytes=20 * 2**20
        ),
        cost_estimate=pl.CostEstimate(
            flops=8 * 2**27, bytes_accessed=4 * 2**20, transcendentals=0
        ),
        name="resynthesis",
    )(*(pltpu.with_memory_space_constraint(x, pltpu.HBM) for x in (spectra, delays, flags, taps)))
    held = [pltpu.with_memory_space_constraint(x, pltpu.VMEM) for x in handed_over]

    def finish_body(*refs):
        finish(stages[-1], *refs)

    return pl.pallas_call(
        finish_body,
        out_shape=jax.ShapeDtypeStruct((2, signals, frames, nfine), jnp.bfloat16),
        in_specs=[vmem_spec] * 5,
        out_specs=any_spec,
        scratch_shapes=[
            pltpu.VMEM((2, 2 * late, HALO + LANES + HALO, nfine), jnp.float32),
            pltpu.VMEM((2, 2 * late, LANES + HALO, nfine), jnp.bfloat16),
            pltpu.SemaphoreType.DMA((2 * signals + 8 * late,)),
        ],
        compiler_params=pltpu.CompilerParams(vmem_limit_bytes=20 * 2**20),
        cost_estimate=pl.CostEstimate(
            flops=2**27, bytes_accessed=2 * 2**20, transcendentals=0
        ),
        name="last_stage",
    )(*held)


def solution(mesh):
    ntm, nchan = mesh.shape["tm"], mesh.shape["chan"]

    def body(spectra, delays, flags, taps):
        return per_device(ntm, nchan, spectra, delays, flags, taps)

    in_specs = (P(None, "chan", None, "tm"), P(), P(), P())
    return jax.shard_map(
        body, mesh=mesh, in_specs=in_specs, out_specs=P(None, "chan", "tm", None), check_vma=False
    )
```
